32 devices in a mesh: row: 4 (over z), col: 2 (over x), rep: 4 (over y, core).
Axes of the slice: x: 2, y: 2, z: 4, core: 2. Of those that a mesh axis runs over, the one named last changes fastest.
Arguments:
- tensor_tiles: bfloat16 [64, 4, 128, 128], P(('row', 'col', 'rep')), may hold values from -12 to 12
- tile_pairs: int32 [64], P(('row', 'col', 'rep')), may hold values from 0 to 1, as said below
- tile_counts: int32 [32], P(('row', 'col', 'rep')), may hold values from 1 to 2, as said below
- occupied: bfloat16 [1024, 1024], P(('col', 'rep'), 'row'), as said below
- virtual: bfloat16 [1024, 1024], P(('col', 'rep'), 'row'), as said below
Outputs:
- polar: float32 [4, 4], replicated
- dressed: bfloat16 [1024, 4, 1024], P(('col', 'rep'), None, 'row')
The draws below stay inside these ranges and needn't reach their ends.
Inputs may be any that keep to these rules, and one draw needn't show every extreme that they name: `tile_pairs`: the 2 entries of one block are distinct: a permutation of its tile pairs. `tile_counts`: some block has all 2 entries live. `occupied`: Symmetric. `virtual`: Symmetric.
All inputs are finite; a program needn't handle non-finite values.
Results may differ from the reference program's by a relative error of at most 0.0049.
Values may be sent and summed in bfloat16 or wider, within the bound.
No kernel may reach another device: no remote copies, remote signals or barrier semaphores. Data moves between devices by JAX's collectives and lax.ppermute only.
A program may use at most 128 MiB of HBM per device.

```python
import math
import jax
import jax.numpy as jnp

TILE = 128
SPAN = 1
AUX = 4
SLOTS = 2
NAO = 1024
N_ROW = 4
N_COL = 2
N_REP = 4
DEVICES = 32


def symmetrize(entries):
    scaled = entries + entries.T
    return (scaled * 0.5 ** 0.5 / math.sqrt(NAO)).astype(jnp.bfloat16)


def draw_occupied(key, part):
    key = jax.random.fold_in(key, 11)
    base_key = jax.random.fold_in(key, 0)
    entries = jax.random.normal(base_key, (NAO, NAO), jnp.float32)
    return symmetrize(entries)


def draw_virtual(key, part):
    key = jax.random.fold_in(key, 12)
    base_key = jax.random.fold_in(key, 0)
    entries = jax.random.normal(base_key, (NAO, NAO), jnp.float32)
    return symmetrize(entries)


def draw_tile_pairs(key, part):
    key = jax.random.fold_in(key, 13)
    device_keys = jax.random.split(key, DEVICES)
    orders = jax.vmap(lambda device_key: jax.random.permutation(device_key, SLOTS))(device_keys)
    return orders.reshape(-1).astype(jnp.int32)


def draw_tile_counts(key, part):
    key = jax.random.fold_in(key, 14)
    first_key, second_key, third_key = jax.random.split(key, 3)
    first = jax.random.randint(first_key, (DEVICES,), 1, SLOTS + 1)
    second = jax.random.randint(second_key, (DEVICES,), 1, SLOTS + 1)
    fullest = jax.random.randint(third_key, (), 0, DEVICES)
    counts = jnp.where(jnp.arange(DEVICES) == fullest, SLOTS, jnp.minimum(first, second))
    return counts.astype(jnp.int32)


def level_of(rng, shape, cuts, least, top_value):
    factor_of, own = 1.0, jax.random.fold_in(rng, 6)
    for dim, blocks in cuts:
        steps = jnp.exp(jax.random.uniform(jax.random.fold_in(own, dim), (blocks,), jnp.float32, least / len(cuts), top_value / len(cuts)))
        factor_of = factor_of * jnp.repeat(steps, shape[dim] // blocks).reshape([-1 if axis == dim else 1 for axis in range(len(shape))])
    return factor_of


def centred(own_key, dims, width, reach, cuts=(), kind=jnp.bfloat16):
    loudness = level_of(own_key, dims, cuts, -0.22, 0.18) if cuts else 1.0
    values = jax.random.normal(own_key, dims, jnp.float32) * width * loudness
    return jnp.minimum(jnp.maximum(values, -reach), reach).astype(kind)


def setup_inputs(seed: int = 0) -> dict:
    seeds = jax.random.split(jax.random.key(seed), 6)
    tensor_tiles = centred(seeds[0], (DEVICES * SLOTS, AUX, TILE, TILE), 2.0, 12.0, ((0, 32),))
    tile_pairs = draw_tile_pairs(jax.random.fold_in(seeds[5], 71), 0)
    tile_counts = draw_tile_counts(jax.random.fold_in(seeds[5], 71), 0)
    occupied = draw_occupied(jax.random.fold_in(seeds[5], 71), 0)
    virtual = draw_virtual(jax.random.fold_in(seeds[5], 71), 0)
    return {"tensor_tiles": tensor_tiles, "tile_pairs": tile_pairs, "tile_counts": tile_counts, "occupied": occupied, "virtual": virtual}


def reference(tensor_tiles, tile_pairs, tile_counts, occupied, virtual):
    nu_tiles = NAO // (N_ROW * TILE)
    groups = N_COL * N_REP
    entry = jnp.arange(DEVICES * SLOTS, dtype=jnp.int32)
    block = (entry // SLOTS).astype(jnp.int32)
    live = (entry % SLOTS) < tile_counts[block]
    first_tile = (block % groups) * SPAN + tile_pairs // nu_tiles
    second_tile = (block // groups) * nu_tiles + tile_pairs % nu_tiles
    kept = jnp.where(live[:, None, None, None], tensor_tiles.astype(jnp.float32), jnp.float32(0.0))
    blocks = jnp.zeros((NAO // TILE, NAO // TILE, AUX, TILE, TILE), jnp.float32)
    blocks = blocks.at[first_tile.astype(jnp.int32), second_tile.astype(jnp.int32)].add(kept)
    tensor = blocks.transpose(2, 0, 3, 1, 4).reshape(AUX, NAO, NAO)
    half_product = jnp.einsum("pmn,ns->spm", tensor, virtual.astype(jnp.float32)).astype(jnp.bfloat16)
    dressed = jnp.einsum("lm,spm->lps", occupied.astype(jnp.float32), half_product.astype(jnp.float32)).astype(jnp.bfloat16)
    polar = jnp.einsum("pls,lqs->pq", tensor, dressed.astype(jnp.float32)) / NAO
    return polar, dressed
```

```python
import functools

import jax
import jax.numpy as jnp
from jax import lax
from jax.experimental import pallas as pl
from jax.experimental.pallas import tpu as pltpu
from jax.sharding import PartitionSpec as P

PLANE = ("col", "rep")
EVERY = ("row", "col", "rep")
VMEM = pl.BlockSpec(memory_space=pltpu.VMEM)
SMEM = pl.BlockSpec(memory_space=pltpu.SMEM)


def flip(value, axes, mask, count):
    return lax.ppermute(value, axes, [(i, i ^ mask) for i in range(count)])


def place_kernel(nu_tiles, pairs_ref, counts_ref, tiles_ref, out_ref):
    slots, _, tile, _ = tiles_ref.shape
    out_ref[...] = jnp.zeros_like(out_ref)
    for t in range(slots):
        pair = pairs_ref[t]

        @pl.when(t < counts_ref[0])
        def _():
            rows = pl.ds(pl.multiple_of(pair // nu_tiles * tile, tile), tile)
            cols = pl.ds(pl.multiple_of(pair % nu_tiles * tile, tile), tile)
            out_ref[:, rows, cols] = tiles_ref[t]


def place(tile_pairs, tile_counts, tensor_tiles, mu, nu):
    _, aux, tile, _ = tensor_tiles.shape
    return pl.pallas_call(
        functools.partial(place_kernel, nu // tile),
        out_shape=jax.ShapeDtypeStruct((aux, mu, nu), tensor_tiles.dtype),
        in_specs=[SMEM, SMEM, VMEM],
        out_specs=VMEM,
        cost_estimate=pl.CostEstimate(flops=0, bytes_accessed=3 * tensor_tiles.size, transcendentals=0),
        name="place",
    )(tile_pairs, tile_counts, tensor_tiles)


def half_kernel(n_row, n_plane, *refs):
    blocks, columns = refs[:n_row], refs[n_row : n_row + n_plane]
    out_ref, panel = refs[n_row + n_plane :]
    mu, nu = columns[0].shape
    aux = blocks[0].shape[0]
    row = lax.axis_index("row")
    plane = lax.axis_index("col") * lax.axis_size("rep") + lax.axis_index("rep")
    for k in range(n_plane):
        at = pl.multiple_of((plane ^ k) * mu, mu)
        panel[pl.ds(at, mu), :] = columns[k][...]
    for p in range(aux):
        total = jnp.zeros((mu, nu), jnp.float32)
        for k in range(n_row):
            at = pl.multiple_of((row ^ k) * nu, nu)
            total += jnp.dot(blocks[k][p], panel[pl.ds(at, nu), :], preferred_element_type=jnp.float32)
        out_ref[:, p * nu : (p + 1) * nu] = total.astype(out_ref.dtype)


def half(blocks, columns):
    aux, mu, nu = blocks[0].shape
    n_row, n_plane = len(blocks), len(columns)
    return pl.pallas_call(
        functools.partial(half_kernel, n_row, n_plane),
        out_shape=jax.ShapeDtypeStruct((mu, aux * nu), blocks[0].dtype),
        in_specs=[VMEM] * (n_row + n_plane),
        out_specs=VMEM,
        scratch_shapes=[pltpu.VMEM((n_plane * mu, nu), blocks[0].dtype)],
        compiler_params=pltpu.CompilerParams(vmem_limit_bytes=48 << 20),
        cost_estimate=pl.CostEstimate(
            flops=2 * aux * mu * nu * nu * n_row, bytes_accessed=4 * n_row * aux * mu * nu, transcendentals=0
        ),
        name="half_product",
    )(*blocks, *columns)


def dress_kernel(n_row, n_plane, *refs):
    weights, halves = refs[:n_row], refs[n_row : n_row + n_plane]
    block_ref, out_ref, share_ref, panel = refs[n_row + n_plane :]
    aux, mu, nu = block_ref.shape
    row = lax.axis_index("row")
    plane = lax.axis_index("col") * lax.axis_size("rep") + lax.axis_index("rep")
    for k in range(n_row):
        at = pl.multiple_of((row ^ k) * nu, nu)
        panel[:, pl.ds(at, nu)] = weights[k][...]
    for q in range(aux):
        total = jnp.zeros((mu, nu), jnp.float32)
        for k in range(n_plane):
            at = pl.multiple_of((plane ^ k) * mu, mu)
            total += jnp.dot(
                panel[:, pl.ds(at, mu)],
                halves[k][:, q * nu : (q + 1) * nu],
                preferred_element_type=jnp.float32,
            )
        rounded = total.astype(out_ref.dtype)
        out_ref[q] = rounded
        wide = rounded.astype(jnp.float32)
        for p in range(aux):
            product = block_ref[p].astype(jnp.float32) * wide
            lanes = jnp.sum(product, axis=0, keepdims=True)
            share_ref[p * aux + q : p * aux + q + 1, :] = jnp.sum(lanes.reshape(1, nu // 128, 128), axis=1)


def dress(weights, halves, block):
    aux, mu, nu = block.shape
    n_row, n_plane = len(weights), len(halves)
    return pl.pallas_call(
        functools.partial(dress_kernel, n_row, n_plane),
        out_shape=(
            jax.ShapeDtypeStruct((aux, mu, nu), block.dtype),
            jax.ShapeDtypeStruct((aux * aux, 128), jnp.float32),
        ),
        in_specs=[VMEM] * (n_row + n_plane + 1),
        out_specs=(VMEM, VMEM),
        scratch_shapes=[pltpu.VMEM((mu, n_row * nu), block.dtype)],
        compiler_params=pltpu.CompilerParams(vmem_limit_bytes=48 << 20),
        cost_estimate=pl.CostEstimate(
            flops=2 * aux * mu * mu * nu * n_plane, bytes_accessed=4 * n_plane * aux * mu * nu, transcendentals=0
        ),
        name="dress",
    )(*weights, *halves, block)


def on_device(tensor_tiles, tile_pairs, tile_counts, occupied, virtual):
    mu, nu = occupied.shape
    n_row, n_plane = lax.axis_size("row"), lax.axis_size("col") * lax.axis_size("rep")
    block = place(tile_pairs, tile_counts, tensor_tiles, mu, nu)
    blocks = [block] + [flip(block, "row", k, n_row) for k in range(1, n_row)]
    columns = [virtual] + [flip(virtual, PLANE, k, n_plane) for k in range(1, n_plane)]
    weights = [occupied] + [flip(occupied, "row", k, n_row) for k in range(1, n_row)]
    own = half(blocks, columns)
    near = [own] + [flip(own, PLANE, k, n_plane) for k in range(2, n_plane, 2)]
    halves = []
    for value in near:
        halves += [value, flip(value, PLANE, 1, n_plane)]
    dressed, share = dress(weights, halves, block)
    share = sum([flip(share, "row", k, n_row) for k in range(1, n_row)], share)
    share = sum([flip(share, PLANE, k, n_plane) for k in range(2, n_plane, 2)], share)
    share = share + flip(share, PLANE, 1, n_plane)
    aux = tensor_tiles.shape[1]
    polar = jnp.sum(share, axis=-1).reshape(aux, aux) / (n_plane * mu)
    return polar, dressed.transpose(1, 0, 2)


def solution(mesh):
    return jax.shard_map(
        on_device,
        mesh=mesh,
        in_specs=(P(EVERY, None, None, None), P(EVERY), P(EVERY), P(PLANE, "row"), P(PLANE, "row")),
        out_specs=(P(), P(PLANE, None, "row")),
        check_vma=False,
    )
```

```python
import functools

import jax
import jax.numpy as jnp
from jax import lax
from jax.experimental import pallas as pl
from jax.experimental.pallas import tpu as pltpu
from jax.sharding import PartitionSpec as P

PLANE = ("col", "rep")
EVERY = ("row", "col", "rep")
VMEM = pl.BlockSpec(memory_space=pltpu.VMEM)
SMEM = pl.BlockSpec(memory_space=pltpu.SMEM)
ROOM = 48 << 20


def flip(value, axes, mask, count):
    return lax.ppermute(value, axes, [(i, i ^ mask) for i in range(count)])


def gather_row(value, n_row):
    if n_row != 4:
        return [[value]] + [[flip(value, "row", k, n_row)] for k in range(1, n_row)]
    one = flip(value, "row", 1, 4)
    middle = lax.ppermute(value, "row", [(1, 2), (2, 1)])
    two = flip(value, "row", 2, 4)
    ends = lax.ppermute(two, "row", [(2, 3), (1, 0)])
    return [[value], [one], [two], [middle, ends]]


def plane_index():
    return lax.axis_index("col") * lax.axis_size("rep") + lax.axis_index("rep")


def total_of(refs):
    value = refs[0][...]
    for ref in refs[1:]:
        value = value + ref[...]
    return value


def nest(groups, refs):
    out, at = [], 0
    for size in groups:
        out.append(refs[at : at + size])
        at += size
    return out, refs[at:]


def place_kernel(nu_tiles, pairs_ref, counts_ref, tiles_ref, own_ref, other_ref, block_ref, bundle_ref):
    slots, aux, tile, _ = tiles_ref.shape
    block_ref[...] = jnp.zeros_like(block_ref)
    for t in range(slots):
        pair = pairs_ref[t]

        @pl.when(t < counts_ref[0])
        def _():
            rows = pl.ds(pl.multiple_of(pair // nu_tiles * tile, tile), tile)
            cols = pl.ds(pl.multiple_of(pair % nu_tiles * tile, tile), tile)
            block_ref[:, rows, cols] = tiles_ref[t]

    bundle_ref[:aux] = block_ref[...]
    bundle_ref[aux] = own_ref[...]
    bundle_ref[aux + 1] = other_ref[...]


def place(tile_pairs, tile_counts, tensor_tiles, own, other):
    _, aux, tile, _ = tensor_tiles.shape
    mu, nu = own.shape
    return pl.pallas_call(
        functools.partial(place_kernel, nu // tile),
        out_shape=(
            jax.ShapeDtypeStruct((aux, mu, nu), own.dtype),
            jax.ShapeDtypeStruct((aux + 2, mu, nu), own.dtype),
        ),
        in_specs=[SMEM, SMEM, VMEM, VMEM, VMEM],
        out_specs=(VMEM, VMEM),
        compiler_params=pltpu.CompilerParams(vmem_limit_bytes=ROOM),
        cost_estimate=pl.CostEstimate(flops=0, bytes_accessed=6 * tensor_tiles.size, transcendentals=0),
        name="place",
    )(tile_pairs, tile_counts, tensor_tiles, own, other)


def join_kernel(groups, *refs):
    pieces, (out_ref,) = nest(groups, refs)
    row = lax.axis_index("row")
    nu = pieces[0][0].shape[1]
    for k, group in enumerate(pieces):
        out_ref[:, pl.ds(pl.multiple_of((row ^ k) * nu, nu), nu)] = total_of(group)


def join(pieces):
    groups = [len(group) for group in pieces]
    flat = [piece for group in pieces for piece in group]
    mu, nu = flat[0].shape
    return pl.pallas_call(
        functools.partial(join_kernel, groups),
        out_shape=jax.ShapeDtypeStruct((mu, nu * len(groups)), flat[0].dtype),
        in_specs=[VMEM] * len(flat),
        out_specs=VMEM,
        compiler_params=pltpu.CompilerParams(vmem_limit_bytes=ROOM),
        cost_estimate=pl.CostEstimate(flops=0, bytes_accessed=4 * mu * nu * len(groups), transcendentals=0),
        name="join",
    )(*flat)


def half_kernel(groups, n_near, *refs):
    blocks, refs = nest(groups, refs)
    bundles, (out_ref, panel) = refs[:n_near], refs[n_near:]
    aux, mu, nu = blocks[0][0].shape
    row, plane = lax.axis_index("row"), plane_index()
    for k in range(n_near):
        for j in range(2):
            at = pl.multiple_of((plane ^ (2 * k + j)) * mu, mu)
            panel[pl.ds(at, mu), :] = bundles[k][aux + j]
    for p in range(aux):
        total = jnp.zeros((mu, nu), jnp.float32)
        for k, group in enumerate(blocks):
            at = pl.multiple_of((row ^ k) * nu, nu)
            piece = total_of([ref.at[p] for ref in group])
            total += jnp.dot(piece, panel[pl.ds(at, nu), :], preferred_element_type=jnp.float32)
        out_ref[:, p * nu : (p + 1) * nu] = total.astype(out_ref.dtype)


def half(blocks, bundles):
    groups = [len(group) for group in blocks]
    flat = [piece for group in blocks for piece in group]
    aux, mu, nu = flat[0].shape
    n_near = len(bundles)
    return pl.pallas_call(
        functools.partial(half_kernel, groups, n_near),
        out_shape=jax.ShapeDtypeStruct((mu, aux * nu), flat[0].dtype),
        in_specs=[VMEM] * (len(flat) + n_near),
        out_specs=VMEM,
        scratch_shapes=[pltpu.VMEM((2 * n_near * mu, nu), flat[0].dtype)],
        compiler_params=pltpu.CompilerParams(vmem_limit_bytes=ROOM),
        cost_estimate=pl.CostEstimate(
            flops=2 * aux * mu * nu * nu * len(groups),
            bytes_accessed=4 * len(groups) * aux * mu * nu,
            transcendentals=0,
        ),
        name="half_product",
    )(*flat, *bundles)


def share_kernel(n_near, *refs):
    bundles = refs[:n_near]
    weights, halves = refs[n_near : n_near + 2], refs[n_near + 2 : n_near + 4]
    out_ref = refs[n_near + 4]
    mu, nu = bundles[0].shape[1:]
    aux = bundles[0].shape[0] - 2
    plane = plane_index()
    for p in range(aux):
        sums = [jnp.zeros((8, nu), jnp.float32) for _ in range(aux)]
        for weight, value in zip(weights, halves):
            mixed = jnp.zeros((mu, nu), jnp.float32)
            for k in range(n_near):
                at = pl.multiple_of((plane ^ (2 * k)) * mu, mu)
                mixed += jnp.dot(weight[:, pl.ds(at, mu)], bundles[k][p], preferred_element_type=jnp.float32)
            for q in range(aux):
                product = mixed * value[:, q * nu : (q + 1) * nu].astype(jnp.float32)
                sums[q] = sums[q] + jnp.sum(product.reshape(mu // 8, 8, nu), axis=0)
        for q in range(aux):
            folded = sum([sums[q][:, i : i + 128] for i in range(128, nu, 128)], sums[q][:, :128])
            out_ref[p * aux + q : p * aux + q + 1, :] = jnp.sum(folded, axis=0, keepdims=True)


def share_of(bundles, weights, halves):
    n_near = len(bundles)
    planes, mu, nu = bundles[0].shape
    aux = planes - 2
    return pl.pallas_call(
        functools.partial(share_kernel, n_near),
        out_shape=jax.ShapeDtypeStruct((aux * aux, 128), jnp.float32),
        in_specs=[VMEM] * (n_near + 4),
        out_specs=VMEM,
        compiler_params=pltpu.CompilerParams(vmem_limit_bytes=ROOM),
        cost_estimate=pl.CostEstimate(
            flops=4 * aux * mu * mu * nu * n_near, bytes_accessed=4 * n_near * aux * mu * nu, transcendentals=0
        ),
        name="polar_share",
    )(*bundles, *weights, *halves)


def dress_kernel(n_plane, nu, weight_ref, *refs):
    halves, out_ref = refs[:n_plane], refs[n_plane]
    aux, mu, _ = out_ref.shape
    plane = plane_index()
    for q in range(aux):
        total = jnp.zeros((mu, nu), jnp.float32)
        for k in range(n_plane):
            at = pl.multiple_of((plane ^ k) * mu, mu)
            total += jnp.dot(
                weight_ref[:, pl.ds(at, mu)],
                halves[k][:, q * nu : (q + 1) * nu],
                preferred_element_type=jnp.float32,
            )
        out_ref[q] = total.astype(out_ref.dtype)


def dress(weight, halves, aux):
    n_plane = len(halves)
    mu, width = halves[0].shape
    nu = width // aux
    return pl.pallas_call(
        functools.partial(dress_kernel, n_plane, nu),
        out_shape=jax.ShapeDtypeStruct((aux, mu, nu), weight.dtype),
        in_specs=[VMEM] * (n_plane + 1),
        out_specs=VMEM,
        compiler_params=pltpu.CompilerParams(vmem_limit_bytes=ROOM),
        cost_estimate=pl.CostEstimate(
            flops=2 * aux * mu * mu * nu * n_plane, bytes_accessed=4 * n_plane * aux * mu * nu, transcendentals=0
        ),
        name="dress",
    )(weight, *halves)


def on_device(tensor_tiles, tile_pairs, tile_counts, occupied, virtual):
    aux = tensor_tiles.shape[1]
    n_row, n_plane = lax.axis_size("row"), lax.axis_size("col") * lax.axis_size("rep")
    near = range(2, n_plane, 2)
    sibling = lambda value: flip(value, PLANE, 1, n_plane)

    weight = join(gather_row(occupied, n_row))
    block, bundle = place(tile_pairs, tile_counts, tensor_tiles, virtual, sibling(virtual))
    blocks = gather_row(block, n_row)
    bundles = [bundle] + [flip(bundle, PLANE, k, n_plane) for k in near]
    own = half(blocks, bundles)
    other = sibling(own)
    halves = [own, other]
    for k in near:
        value = flip(own, PLANE, k, n_plane)
        halves += [value, sibling(value)]

    share = share_of(bundles, (weight, sibling(weight)), (own, other))
    step = 1
    while step < n_row:
        share = share + flip(share, "row", step, n_row)
        step *= 2
    step = 1
    while step < n_plane:
        share = share + flip(share, PLANE, step, n_plane)
        step *= 2
    polar = jnp.sum(share, axis=-1).reshape(aux, aux) / weight.shape[1]
    dressed = dress(weight, halves, aux).transpose(1, 0, 2)
    return polar, dressed


def solution(mesh):
    return jax.shard_map(
        on_device,
        mesh=mesh,
        in_specs=(P(EVERY, None, None, None), P(EVERY), P(EVERY), P(PLANE, "row"), P(PLANE, "row")),
        out_specs=(P(), P(PLANE, None, "row")),
        check_vma=False,
    )
```

```python
import functools

import jax
import jax.numpy as jnp
from jax import lax
from jax.experimental import pallas as pl
from jax.experimental.pallas import tpu as pltpu
from jax.sharding import PartitionSpec as P

PLANE = ("col", "rep")
EVERY = ("row", "col", "rep")
VMEM = pl.BlockSpec(memory_space=pltpu.VMEM)
SMEM = pl.BlockSpec(memory_space=pltpu.SMEM)
ROOM = 48 << 20


def flip(value, axes, mask, count):
    return lax.ppermute(value, axes, [(i, i ^ mask) for i in range(count)])


def after(value, earlier):
    return lax.optimization_barrier((value, earlier))


def gather_row(value, n_row):
    if n_row != 4:
        return [[value]] + [[flip(value, "row", k, n_row)] for k in range(1, n_row)]
    two = flip(value, "row", 2, 4)
    one = flip(value, "row", 1, 4)
    source, two = after(value, two)
    ends = lax.ppermute(two, "row", [(2, 3), (1, 0)])
    middle = lax.ppermute(source, "row", [(1, 2), (2, 1)])
    return [[value], [one], [two], [middle, ends]]


def plane_index():
    return lax.axis_index("col") * lax.axis_size("rep") + lax.axis_index("rep")


def total_of(refs):
    value = refs[0][...]
    for ref in refs[1:]:
        value = value + ref[...]
    return value


def nest(groups, refs):
    out, at = [], 0
    for size in groups:
        out.append(refs[at : at + size])
        at += size
    return out, refs[at:]


def place_kernel(nu_tiles, pairs_ref, counts_ref, tiles_ref, weight_ref, own_ref, other_ref, *refs):
    *targets, sems = refs
    slots, aux, tile, _ = tiles_ref.shape
    line_ref, bundle_ref = targets

    def regions(t):
        pair = pairs_ref[t]
        rows = pl.ds(pl.multiple_of(pair // nu_tiles * tile, tile), tile)
        cols = pl.ds(pl.multiple_of(pair % nu_tiles * tile, tile), tile)
        return [target.at[:aux, rows, cols] for target in targets]

    def copies(t):
        return [pltpu.make_async_copy(tiles_ref.at[t], to, sems.at[t, i]) for i, to in enumerate(regions(t))]

    sides = [
        pltpu.make_async_copy(weight_ref, line_ref.at[aux], sems.at[slots, 0]),
        pltpu.make_async_copy(own_ref, bundle_ref.at[aux], sems.at[slots, 1]),
        pltpu.make_async_copy(other_ref, bundle_ref.at[aux + 1], sems.at[slots, 2]),
    ]
    for t in range(slots):

        @pl.when(t < counts_ref[0])
        def _():
            for copy in copies(t):
                copy.start()

        @pl.when(t >= counts_ref[0])
        def _():
            for target in regions(t):
                target[...] = jnp.zeros((aux, tile, tile), line_ref.dtype)

    for copy in sides:
        copy.start()
    for t in range(slots):

        @pl.when(t < counts_ref[0])
        def _():
            for copy in copies(t):
                copy.wait()

    for copy in sides:
        copy.wait()


def place(tile_pairs, tile_counts, tensor_tiles, weight, own, other):
    slots, aux, tile, _ = tensor_tiles.shape
    mu, nu = own.shape
    anywhere = pl.BlockSpec(memory_space=pl.ANY)
    return pl.pallas_call(
        functools.partial(place_kernel, nu // tile),
        out_shape=(
            jax.ShapeDtypeStruct((aux + 1, mu, nu), own.dtype),
            jax.ShapeDtypeStruct((aux + 2, mu, nu), own.dtype),
        ),
        in_specs=[SMEM, SMEM] + [anywhere] * 4,
        out_specs=(VMEM, VMEM),
        scratch_shapes=[pltpu.SemaphoreType.DMA((slots + 1, 3))],
        cost_estimate=pl.CostEstimate(flops=0, bytes_accessed=6 * tensor_tiles.size, transcendentals=0),
        name="place",
    )(tile_pairs, tile_counts, tensor_tiles, weight, own, other)


def half_kernel(groups, n_near, *refs):
    lines, refs = nest(groups, refs)
    bundles, (out_ref, pack_ref, panel) = refs[:n_near], refs[n_near:]
    planes, mu, nu = lines[0][0].shape
    aux = planes - 1
    row, plane = lax.axis_index("row"), plane_index()
    for k in range(n_near):
        for j in range(2):
            at = pl.multiple_of((plane ^ (2 * k + j)) * mu, mu)
            panel[pl.ds(at, mu), :] = bundles[k][aux + j]
    for p in range(aux):
        total = jnp.zeros((mu, nu), jnp.float32)
        for k, group in enumerate(lines):
            at = pl.multiple_of((row ^ k) * nu, nu)
            piece = total_of([ref.at[p] for ref in group])
            total += jnp.dot(piece, panel[pl.ds(at, nu), :], preferred_element_type=jnp.float32)
        rounded = total.astype(out_ref.dtype)
        out_ref[:, p * nu : (p + 1) * nu] = rounded
        pack_ref[:, p * nu : (p + 1) * nu] = rounded
    for k, group in enumerate(lines):
        at = pl.multiple_of(aux * nu + (row ^ k) * nu, nu)
        pack_ref[:, pl.ds(at, nu)] = total_of([ref.at[aux] for ref in group])


def half(lines, bundles):
    groups = [len(group) for group in lines]
    flat = [piece for group in lines for piece in group]
    planes, mu, nu = flat[0].shape
    aux, n_near = planes - 1, len(bundles)
    return pl.pallas_call(
        functools.partial(half_kernel, groups, n_near),
        out_shape=(
            jax.ShapeDtypeStruct((mu, aux * nu), flat[0].dtype),
            jax.ShapeDtypeStruct((mu, (aux + len(groups)) * nu), flat[0].dtype),
        ),
        in_specs=[VMEM] * (len(flat) + n_near),
        out_specs=(VMEM, VMEM),
        scratch_shapes=[pltpu.VMEM((2 * n_near * mu, nu), flat[0].dtype)],
        compiler_params=pltpu.CompilerParams(vmem_limit_bytes=ROOM),
        cost_estimate=pl.CostEstimate(
            flops=2 * aux * mu * nu * nu * len(groups),
            bytes_accessed=4 * len(groups) * aux * mu * nu,
            transcendentals=0,
        ),
        name="half_product",
    )(*flat, *bundles)


def share_kernel(n_near, *refs):
    bundles = refs[:n_near]
    packs, out_ref = refs[n_near : n_near + 2], refs[n_near + 2]
    mu, nu = bundles[0].shape[1:]
    aux = bundles[0].shape[0] - 2
    plane = plane_index()
    for p in range(aux):
        sums = [jnp.zeros((8, nu), jnp.float32) for _ in range(aux)]
        for pack in packs:
            mixed = jnp.zeros((mu, nu), jnp.float32)
            for k in range(n_near):
                at = pl.multiple_of(aux * nu + (plane ^ (2 * k)) * mu, mu)
                mixed += jnp.dot(pack[:, pl.ds(at, mu)], bundles[k][p], preferred_element_type=jnp.float32)
            for q in range(aux):
                product = mixed * pack[:, q * nu : (q + 1) * nu].astype(jnp.float32)
                sums[q] = sums[q] + jnp.sum(product.reshape(mu // 8, 8, nu), axis=0)
        for q in range(aux):
            folded = sum([sums[q][:, i : i + 128] for i in range(128, nu, 128)], sums[q][:, :128])
            out_ref[p : p + 1, q * 128 : (q + 1) * 128] = jnp.sum(folded, axis=0, keepdims=True)


def share_of(bundles, packs):
    n_near = len(bundles)
    planes, mu, nu = bundles[0].shape
    aux = planes - 2
    return pl.pallas_call(
        functools.partial(share_kernel, n_near),
        out_shape=jax.ShapeDtypeStruct((aux, aux * 128), jnp.float32),
        in_specs=[VMEM] * (n_near + 2),
        out_specs=VMEM,
        compiler_params=pltpu.CompilerParams(vmem_limit_bytes=ROOM),
        cost_estimate=pl.CostEstimate(
            flops=4 * aux * mu * mu * nu * n_near, bytes_accessed=4 * n_near * aux * mu * nu, transcendentals=0
        ),
        name="polar_share",
    )(*bundles, *packs)


def dress_kernel(aux, *refs):
    halves, out_ref = refs[:-1], refs[-1]
    pack_ref = refs[0]
    mu = pack_ref.shape[0]
    nu = out_ref.shape[2]
    plane = plane_index()
    for q in range(aux):
        total = jnp.zeros((mu, nu), jnp.float32)
        for k, value in enumerate(halves):
            at = pl.multiple_of(aux * nu + (plane ^ k) * mu, mu)
            total += jnp.dot(
                pack_ref[:, pl.ds(at, mu)],
                value[:, q * nu : (q + 1) * nu],
                preferred_element_type=jnp.float32,
            )
        out_ref[q] = total.astype(out_ref.dtype)


def dress(halves, aux, nu):
    mu = halves[0].shape[0]
    return pl.pallas_call(
        functools.partial(dress_kernel, aux),
        out_shape=jax.ShapeDtypeStruct((aux, mu, nu), halves[0].dtype),
        in_specs=[VMEM] * len(halves),
        out_specs=VMEM,
        compiler_params=pltpu.CompilerParams(vmem_limit_bytes=ROOM),
        cost_estimate=pl.CostEstimate(
            flops=2 * aux * mu * mu * nu * len(halves),
            bytes_accessed=4 * len(halves) * aux * mu * nu,
            transcendentals=0,
        ),
        name="dress",
    )(*halves)


def finish_kernel(total_ao, first_ref, second_ref, out_ref):
    aux = out_ref.shape[0]
    for q in range(aux):
        lanes = pl.ds(q * 128, 128)
        share = first_ref[:, lanes] + second_ref[:, lanes]
        out_ref[:, q : q + 1] = jnp.sum(share, axis=1, keepdims=True) / total_ao


def finish(first, second, total_ao):
    aux = first.shape[0]
    return pl.pallas_call(
        functools.partial(finish_kernel, total_ao),
        out_shape=jax.ShapeDtypeStruct((aux, aux), jnp.float32),
        in_specs=[VMEM, VMEM],
        out_specs=VMEM,
        name="finish",
    )(first, second)


def on_device(tensor_tiles, tile_pairs, tile_counts, occupied, virtual):
    aux = tensor_tiles.shape[1]
    mu, nu = virtual.shape
    n_row, n_plane = lax.axis_size("row"), lax.axis_size("col") * lax.axis_size("rep")
    near = list(range(2, n_plane, 2))
    sibling = lambda value: flip(value, PLANE, 1, n_plane)

    line, bundle = place(tile_pairs, tile_counts, tensor_tiles, occupied, virtual, sibling(virtual))
    lines = gather_row(line, n_row)
    bundles = [bundle] + [flip(bundle, PLANE, k, n_plane) for k in near]
    own, pack = half(lines, bundles)
    arrivals = [flip(own, PLANE, k, n_plane) for k in near]
    other = sibling(pack)

    share = share_of(bundles, (pack, other))
    step = 1
    while step < n_row:
        share = share + flip(share, "row", step, n_row)
        step *= 2
    share = share + sibling(share)
    halves = [pack, other]
    for value in arrivals:
        halves += [value, sibling(value)]
    step = 2
    while 2 * step < n_plane:
        share = share + flip(share, PLANE, step, n_plane)
        step *= 2
    polar = finish(share, flip(share, PLANE, step, n_plane), n_row * nu)
    dressed = dress(halves, aux, nu).transpose(1, 0, 2)
    return polar, dressed


def solution(mesh):
    return jax.shard_map(
        on_device,
        mesh=mesh,
        in_specs=(P(EVERY, None, None, None), P(EVERY), P(EVERY), P(PLANE, "row"), P(PLANE, "row")),
        out_specs=(P(), P(PLANE, None, "row")),
        check_vma=False,
    )
```

```python
import functools

import jax
import jax.numpy as jnp
from jax import lax
from jax.experimental import pallas as pl
from jax.experimental.pallas import tpu as pltpu
from jax.sharding import PartitionSpec as P

PLANE = ("col", "rep")
EVERY = ("row", "col", "rep")
VMEM = pl.BlockSpec(memory_space=pltpu.VMEM)
SMEM = pl.BlockSpec(memory_space=pltpu.SMEM)
ROOM = 48 << 20


def flip(value, axes, mask, count):
    return lax.ppermute(value, axes, [(i, i ^ mask) for i in range(count)])


def after(value, earlier):
    return lax.optimization_barrier((value, earlier))


def gather_row(value, n_row):
    found = {0: value}
    step = n_row // 2
    while step:
        found.update({k ^ step: flip(held, "row", step, n_row) for k, held in list(found.items())})
        step //= 2
    return [found[k] for k in range(n_row)]


def plane_index():
    return lax.axis_index("col") * lax.axis_size("rep") + lax.axis_index("rep")


def place_kernel(nu_tiles, pairs_ref, counts_ref, tiles_ref, weight_ref, column_ref, line_ref, bundle_ref):
    slots, aux, tile, _ = tiles_ref.shape
    for t in range(slots):
        pair = pairs_ref[t]
        rows = pl.ds(pl.multiple_of(pair // nu_tiles * tile, tile), tile)
        cols = pl.ds(pl.multiple_of(pair % nu_tiles * tile, tile), tile)

        @pl.when(t < counts_ref[0])
        def _():
            for out_ref in (line_ref, bundle_ref):
                out_ref[:aux, rows, cols] = tiles_ref[t]

        @pl.when(t >= counts_ref[0])
        def _():
            for out_ref in (line_ref, bundle_ref):
                out_ref[:aux, rows, cols] = jnp.zeros((aux, tile, tile), out_ref.dtype)

    line_ref[aux] = weight_ref[...]
    bundle_ref[aux] = column_ref[...]


def place(tile_pairs, tile_counts, tensor_tiles, weight, column):
    _, aux, tile, _ = tensor_tiles.shape
    mu, nu = weight.shape
    shape = jax.ShapeDtypeStruct((aux + 1, mu, nu), weight.dtype)
    return pl.pallas_call(
        functools.partial(place_kernel, nu // tile),
        out_shape=(shape, shape),
        in_specs=[SMEM, SMEM, VMEM, VMEM, VMEM],
        out_specs=(VMEM, VMEM),
        compiler_params=pltpu.CompilerParams(vmem_limit_bytes=ROOM),
        cost_estimate=pl.CostEstimate(flops=0, bytes_accessed=6 * tensor_tiles.size, transcendentals=0),
        name="place",
    )(tile_pairs, tile_counts, tensor_tiles, weight, column)


def half_kernel(n_row, n_plane, *refs):
    lines, bundles = refs[:n_row], refs[n_row : n_row + n_plane]
    out_ref, weight_ref, share_ref, panel = refs[n_row + n_plane :]
    planes, mu, nu = lines[0].shape
    aux = planes - 1
    row, plane = lax.axis_index("row"), plane_index()
    for k in range(n_plane):
        panel[pl.ds(pl.multiple_of((plane ^ k) * mu, mu), mu), :] = bundles[k][aux]
    for k in range(n_row):
        weight_ref[:, pl.ds(pl.multiple_of((row ^ k) * nu, nu), nu)] = lines[k][aux]
    for p in range(aux):
        total = jnp.zeros((mu, nu), jnp.float32)
        for k in range(n_row):
            at = pl.multiple_of((row ^ k) * nu, nu)
            total += jnp.dot(lines[k][p], panel[pl.ds(at, nu), :], preferred_element_type=jnp.float32)
        out_ref[:, p * nu : (p + 1) * nu] = total.astype(out_ref.dtype)
    for p in range(aux):
        mixed = jnp.zeros((mu, nu), jnp.float32)
        for k in range(n_plane):
            at = pl.multiple_of((plane ^ k) * mu, mu)
            mixed += jnp.dot(weight_ref[:, pl.ds(at, mu)], bundles[k][p], preferred_element_type=jnp.float32)
        for q in range(aux):
            product = mixed * out_ref[:, q * nu : (q + 1) * nu].astype(jnp.float32)
            lanes = jnp.sum(product.reshape(mu // 8, 8, nu), axis=0)
            folded = sum([lanes[:, i : i + 128] for i in range(128, nu, 128)], lanes[:, :128])
            share_ref[p : p + 1, q * 128 : (q + 1) * 128] = jnp.sum(folded, axis=0, keepdims=True)


def half(lines, bundles):
    planes, mu, nu = lines[0].shape
    aux, n_row, n_plane = planes - 1, len(lines), len(bundles)
    kind = lines[0].dtype
    return pl.pallas_call(
        functools.partial(half_kernel, n_row, n_plane),
        out_shape=(
            jax.ShapeDtypeStruct((mu, aux * nu), kind),
            jax.ShapeDtypeStruct((mu, n_row * nu), kind),
            jax.ShapeDtypeStruct((aux, aux * 128), jnp.float32),
        ),
        in_specs=[VMEM] * (n_row + n_plane),
        out_specs=(VMEM, VMEM, VMEM),
        scratch_shapes=[pltpu.VMEM((n_plane * mu, nu), kind)],
        compiler_params=pltpu.CompilerParams(vmem_limit_bytes=ROOM),
        cost_estimate=pl.CostEstimate(
            flops=4 * aux * mu * nu * nu * n_row, bytes_accessed=8 * n_row * aux * mu * nu, transcendentals=0
        ),
        name="half_product",
    )(*lines, *bundles)


def dress_kernel(n_plane, weight_ref, *refs):
    halves, out_ref = refs[:n_plane], refs[n_plane]
    aux, mu, nu = out_ref.shape
    plane = plane_index()
    for q in range(aux):
        total = jnp.zeros((mu, nu), jnp.float32)
        for k in range(n_plane):
            at = pl.multiple_of((plane ^ k) * mu, mu)
            total += jnp.dot(
                weight_ref[:, pl.ds(at, mu)],
                halves[k][:, q * nu : (q + 1) * nu],
                preferred_element_type=jnp.float32,
            )
        out_ref[q] = total.astype(out_ref.dtype)


def dress(weight, halves, aux):
    mu, width = halves[0].shape
    n_plane = len(halves)
    return pl.pallas_call(
        functools.partial(dress_kernel, n_plane),
        out_shape=jax.ShapeDtypeStruct((aux, mu, width // aux), weight.dtype),
        in_specs=[VMEM] * (n_plane + 1),
        out_specs=VMEM,
        compiler_params=pltpu.CompilerParams(vmem_limit_bytes=ROOM),
        cost_estimate=pl.CostEstimate(
            flops=2 * mu * mu * width * n_plane, bytes_accessed=4 * n_plane * mu * width, transcendentals=0
        ),
        name="dress",
    )(weight, *halves)


def finish_kernel(total_ao, first_ref, second_ref, out_ref):
    aux = out_ref.shape[0]
    for q in range(aux):
        lanes = pl.ds(q * 128, 128)
        share = first_ref[:, lanes] + second_ref[:, lanes]
        out_ref[:, q : q + 1] = jnp.sum(share, axis=1, keepdims=True) / total_ao


def finish(first, second, total_ao):
    aux = first.shape[0]
    return pl.pallas_call(
        functools.partial(finish_kernel, total_ao),
        out_shape=jax.ShapeDtypeStruct((aux, aux), jnp.float32),
        in_specs=[VMEM, VMEM],
        out_specs=VMEM,
        compiler_params=pltpu.CompilerParams(vmem_limit_bytes=ROOM),
        name="finish",
    )(first, second)


def on_device(tensor_tiles, tile_pairs, tile_counts, occupied, virtual):
    aux = tensor_tiles.shape[1]
    nu = virtual.shape[1]
    n_row, n_plane = lax.axis_size("row"), lax.axis_size("col") * lax.axis_size("rep")
    near = list(range(2, n_plane, 2))
    sibling = lambda value: flip(value, PLANE, 1, n_plane)

    line, bundle = place(tile_pairs, tile_counts, tensor_tiles, occupied, virtual)
    lines = gather_row(line, n_row)
    bundles = []
    for value in [bundle] + [flip(bundle, PLANE, k, n_plane) for k in near]:
        bundles += [value, sibling(value)]
    own, weight, share = half(lines, bundles)

    arrivals = [flip(own, PLANE, k, n_plane) for k in near]
    step = 1
    while step < n_row:
        share = share + flip(share, "row", step, n_row)
        step *= 2
    step = 2
    while step < n_plane:
        share = share + flip(share, PLANE, step, n_plane)
        step *= 2
    share, arrivals = after(share, arrivals)
    polar = finish(share, sibling(share), n_row * nu)
    halves = []
    for value in [own] + arrivals:
        halves += [value, sibling(value)]
    dressed = dress(weight, halves, aux).transpose(1, 0, 2)
    return polar, dressed


def solution(mesh):
    return jax.shard_map(
        on_device,
        mesh=mesh,
        in_specs=(P(EVERY, None, None, None), P(EVERY), P(EVERY), P(PLANE, "row"), P(PLANE, "row")),
        out_specs=(P(), P(PLANE, None, "row")),
        check_vma=False,
    )
```

```python
import functools

import jax
import jax.numpy as jnp
from jax import lax
from jax.experimental import pallas as pl
from jax.experimental.pallas import tpu as pltpu
from jax.sharding import PartitionSpec as P

PLANE = ("col", "rep")
EVERY = ("row", "col", "rep")
VMEM = pl.BlockSpec(memory_space=pltpu.VMEM)
SMEM = pl.BlockSpec(memory_space=pltpu.SMEM)
ROOM = 48 << 20


def flip(value, axes, mask, count):
    return lax.ppermute(value, axes, [(i, i ^ mask) for i in range(count)])


def after(value, earlier):
    return lax.optimization_barrier((value, earlier))


def gather_row(value, n_row):
    found = {0: value}
    step = n_row // 2
    while step:
        found.update({k ^ step: flip(held, "row", step, n_row) for k, held in list(found.items())})
        step //= 2
    return [found[k] for k in range(n_row)]


def plane_index():
    return lax.axis_index("col") * lax.axis_size("rep") + lax.axis_index("rep")


def place_kernel(nu_tiles, counts_ref, pairs_any, tiles_any, weight_any, column_any, *refs):
    line_ref, bundle_ref, pairs_ref, tiles_ref, sems = refs
    slots, aux, tile, _ = tiles_ref.shape
    copies = [
        pltpu.make_async_copy(source, target, sems.at[i])
        for i, (source, target) in enumerate(
            [
                (tiles_any, tiles_ref),
                (pairs_any, pairs_ref),
                (weight_any, line_ref.at[aux]),
                (column_any, bundle_ref.at[aux]),
            ]
        )
    ]
    for copy in copies:
        copy.start()
    for copy in copies:
        copy.wait()
    for t in range(slots):
        pair = pairs_ref[t]
        rows = pl.ds(pl.multiple_of(pair // nu_tiles * tile, tile), tile)
        cols = pl.ds(pl.multiple_of(pair % nu_tiles * tile, tile), tile)

        @pl.when(t < counts_ref[0])
        def _():
            for out_ref in (line_ref, bundle_ref):
                out_ref[:aux, rows, cols] = tiles_ref[t]

        @pl.when(t >= counts_ref[0])
        def _():
            for out_ref in (line_ref, bundle_ref):
                out_ref[:aux, rows, cols] = jnp.zeros((aux, tile, tile), out_ref.dtype)


def place(tile_pairs, tile_counts, tensor_tiles, weight, column):
    slots, aux, tile, _ = tensor_tiles.shape
    mu, nu = weight.shape
    shape = jax.ShapeDtypeStruct((aux + 1, mu, nu), weight.dtype)
    stays = [pltpu.with_memory_space_constraint(value, pltpu.HBM) for value in (tile_pairs, tensor_tiles, weight, column)]
    return pl.pallas_call(
        functools.partial(place_kernel, nu // tile),
        out_shape=(shape, shape),
        in_specs=[SMEM] + [pl.BlockSpec(memory_space=pltpu.HBM)] * 4,
        out_specs=(VMEM, VMEM),
        scratch_shapes=[
            pltpu.SMEM(tile_pairs.shape, tile_pairs.dtype),
            pltpu.VMEM(tensor_tiles.shape, tensor_tiles.dtype),
            pltpu.SemaphoreType.DMA((4,)),
        ],
        compiler_params=pltpu.CompilerParams(vmem_limit_bytes=ROOM),
        cost_estimate=pl.CostEstimate(flops=0, bytes_accessed=6 * tensor_tiles.size, transcendentals=0),
        name="place",
    )(tile_counts, *stays)


def half_kernel(n_row, n_plane, *refs):
    lines, bundles = refs[:n_row], refs[n_row : n_row + n_plane]
    out_ref, weight_ref, share_ref, panel = refs[n_row + n_plane :]
    planes, mu, nu = lines[0].shape
    aux = planes - 1
    row, plane = lax.axis_index("row"), plane_index()
    for k in range(n_plane):
        panel[pl.ds(pl.multiple_of((plane ^ k) * mu, mu), mu), :] = bundles[k][aux]
    for k in range(n_row):
        weight_ref[:, pl.ds(pl.multiple_of((row ^ k) * nu, nu), nu)] = lines[k][aux]
    for p in range(aux):
        total = jnp.zeros((mu, nu), jnp.float32)
        for k in range(n_row):
            at = pl.multiple_of((row ^ k) * nu, nu)
            total += jnp.dot(lines[k][p], panel[pl.ds(at, nu), :], preferred_element_type=jnp.float32)
        out_ref[:, p * nu : (p + 1) * nu] = total.astype(out_ref.dtype)
    for p in range(aux):
        mixed = jnp.zeros((mu, nu), jnp.float32)
        for k in range(n_plane):
            at = pl.multiple_of((plane ^ k) * mu, mu)
            mixed += jnp.dot(weight_ref[:, pl.ds(at, mu)], bundles[k][p], preferred_element_type=jnp.float32)
        for q in range(aux):
            product = mixed * out_ref[:, q * nu : (q + 1) * nu].astype(jnp.float32)
            lanes = jnp.sum(product.reshape(mu // 8, 8, nu), axis=0)
            folded = sum([lanes[:, i : i + 128] for i in range(128, nu, 128)], lanes[:, :128])
            share_ref[p : p + 1, q * 128 : (q + 1) * 128] = jnp.sum(folded, axis=0, keepdims=True)


def half(lines, bundles):
    planes, mu, nu = lines[0].shape
    aux, n_row, n_plane = planes - 1, len(lines), len(bundles)
    kind = lines[0].dtype
    return pl.pallas_call(
        functools.partial(half_kernel, n_row, n_plane),
        out_shape=(
            jax.ShapeDtypeStruct((mu, aux * nu), kind),
            jax.ShapeDtypeStruct((mu, n_row * nu), kind),
            jax.ShapeDtypeStruct((aux, aux * 128), jnp.float32),
        ),
        in_specs=[VMEM] * (n_row + n_plane),
        out_specs=(VMEM, VMEM, VMEM),
        scratch_shapes=[pltpu.VMEM((n_plane * mu, nu), kind)],
        compiler_params=pltpu.CompilerParams(vmem_limit_bytes=ROOM),
        cost_estimate=pl.CostEstimate(
            flops=4 * aux * mu * nu * nu * n_row, bytes_accessed=8 * n_row * aux * mu * nu, transcendentals=0
        ),
        name="half_product",
    )(*lines, *bundles)


def dress_kernel(n_plane, weight_ref, *refs):
    halves, out_ref = refs[:n_plane], refs[n_plane]
    mu, aux, nu = out_ref.shape
    plane = plane_index()
    for q in range(aux):
        total = jnp.zeros((mu, nu), jnp.float32)
        for k in range(n_plane):
            at = pl.multiple_of((plane ^ k) * mu, mu)
            total += jnp.dot(
                weight_ref[:, pl.ds(at, mu)],
                halves[k][:, q * nu : (q + 1) * nu],
                preferred_element_type=jnp.float32,
            )
        out_ref[:, q, :] = total.astype(out_ref.dtype)


def dress(weight, halves, aux):
    mu, width = halves[0].shape
    n_plane = len(halves)
    return pl.pallas_call(
        functools.partial(dress_kernel, n_plane),
        out_shape=jax.ShapeDtypeStruct((mu, aux, width // aux), weight.dtype),
        in_specs=[VMEM] * (n_plane + 1),
        out_specs=VMEM,
        compiler_params=pltpu.CompilerParams(vmem_limit_bytes=ROOM),
        cost_estimate=pl.CostEstimate(
            flops=2 * mu * mu * width * n_plane, bytes_accessed=4 * n_plane * mu * width, transcendentals=0
        ),
        name="dress",
    )(weight, *halves)


def finish_kernel(total_ao, first_ref, second_ref, out_ref):
    aux = out_ref.shape[0]
    for q in range(aux):
        lanes = pl.ds(q * 128, 128)
        share = first_ref[:, lanes] + second_ref[:, lanes]
        out_ref[:, q : q + 1] = jnp.sum(share, axis=1, keepdims=True) / total_ao


def finish(first, second, total_ao):
    aux = first.shape[0]
    return pl.pallas_call(
        functools.partial(finish_kernel, total_ao),
        out_shape=jax.ShapeDtypeStruct((aux, aux), jnp.float32),
        in_specs=[VMEM, VMEM],
        out_specs=VMEM,
        compiler_params=pltpu.CompilerParams(vmem_limit_bytes=ROOM),
        name="finish",
    )(first, second)


def on_device(tensor_tiles, tile_pairs, tile_counts, occupied, virtual):
    aux = tensor_tiles.shape[1]
    nu = virtual.shape[1]
    n_row, n_plane = lax.axis_size("row"), lax.axis_size("col") * lax.axis_size("rep")
    near = list(range(2, n_plane, 2))
    sibling = lambda value: flip(value, PLANE, 1, n_plane)

    line, bundle = place(tile_pairs, tile_counts, tensor_tiles, occupied, virtual)
    lines = gather_row(line, n_row)
    bundles = []
    for value in [bundle] + [flip(bundle, PLANE, k, n_plane) for k in near]:
        bundles += [value, sibling(value)]
    own, weight, share = half(lines, bundles)

    share = share + flip(share, "row", 1, n_row)
    share, own = after(share, own)
    arrivals = [flip(own, PLANE, k, n_plane) for k in near]
    step = 2
    while step < n_row:
        share = share + flip(share, "row", step, n_row)
        step *= 2
    step = 1
    while 2 * step < n_plane:
        share = share + flip(share, PLANE, step, n_plane)
        step *= 2
    last = flip(share, PLANE, step, n_plane)
    last, arrivals = after(last, arrivals)
    polar = finish(share, last, n_row * nu)
    halves = []
    for value in [own] + arrivals:
        halves += [value, sibling(value)]
    dressed = dress(weight, halves, aux)
    return polar, dressed


def solution(mesh):
    return jax.shard_map(
        on_device,
        mesh=mesh,
        in_specs=(P(EVERY, None, None, None), P(EVERY), P(EVERY), P(PLANE, "row"), P(PLANE, "row")),
        out_specs=(P(), P(PLANE, None, "row")),
        check_vma=False,
    )
```

```python
import functools

import jax
import jax.numpy as jnp
from jax import lax
from jax.experimental import pallas as pl
from jax.experimental.pallas import tpu as pltpu
from jax.sharding import PartitionSpec as P

PLANE = ("col", "rep")
EVERY = ("row", "col", "rep")
VMEM = pl.BlockSpec(memory_space=pltpu.VMEM)
SMEM = pl.BlockSpec(memory_space=pltpu.SMEM)
ROOM = 48 << 20


def flip(value, axes, mask, count):
    return lax.ppermute(value, axes, [(i, i ^ mask) for i in range(count)])


def after(value, earlier):
    return lax.optimization_barrier((value, earlier))


def gather_row(value, n_row):
    found = {0: value}
    step = n_row // 2
    while step:
        found.update({k ^ step: flip(held, "row", step, n_row) for k, held in list(found.items())})
        step //= 2
    return [found[k] for k in range(n_row)]


def plane_index():
    return lax.axis_index("col") * lax.axis_size("rep") + lax.axis_index("rep")


def place_kernel(nu_tiles, counts_ref, pairs_any, tiles_any, weight_any, column_any, *refs):
    line_ref, bundle_ref, pairs_ref, tiles_ref, sems = refs
    slots, aux, tile, _ = tiles_ref.shape
    copies = [
        pltpu.make_async_copy(source, target, sems.at[i])
        for i, (source, target) in enumerate(
            [
                (tiles_any, tiles_ref),
                (pairs_any, pairs_ref),
                (weight_any, line_ref.at[aux]),
                (column_any, bundle_ref.at[aux]),
            ]
        )
    ]
    for copy in copies:
        copy.start()
    for copy in copies:
        copy.wait()
    for t in range(slots):
        pair = pairs_ref[t]
        rows = pl.ds(pl.multiple_of(pair // nu_tiles * tile, tile), tile)
        cols = pl.ds(pl.multiple_of(pair % nu_tiles * tile, tile), tile)

        @pl.when(t < counts_ref[0])
        def _():
            for out_ref in (line_ref, bundle_ref):
                out_ref[:aux, rows, cols] = tiles_ref[t]

        @pl.when(t >= counts_ref[0])
        def _():
            for out_ref in (line_ref, bundle_ref):
                out_ref[:aux, rows, cols] = jnp.zeros((aux, tile, tile), out_ref.dtype)


def place(tile_pairs, tile_counts, tensor_tiles, weight, column):
    slots, aux, tile, _ = tensor_tiles.shape
    mu, nu = weight.shape
    shape = jax.ShapeDtypeStruct((aux + 1, mu, nu), weight.dtype)
    stays = [pltpu.with_memory_space_constraint(value, pltpu.HBM) for value in (tile_pairs, tensor_tiles, weight, column)]
    return pl.pallas_call(
        functools.partial(place_kernel, nu // tile),
        out_shape=(shape, shape),
        in_specs=[SMEM] + [pl.BlockSpec(memory_space=pltpu.HBM)] * 4,
        out_specs=(VMEM, VMEM),
        scratch_shapes=[
            pltpu.SMEM(tile_pairs.shape, tile_pairs.dtype),
            pltpu.VMEM(tensor_tiles.shape, tensor_tiles.dtype),
            pltpu.SemaphoreType.DMA((4,)),
        ],
        compiler_params=pltpu.CompilerParams(vmem_limit_bytes=ROOM),
        cost_estimate=pl.CostEstimate(flops=0, bytes_accessed=6 * tensor_tiles.size, transcendentals=0),
        name="place",
    )(tile_counts, *stays)


def half_kernel(n_row, n_plane, *refs):
    lines, bundles = refs[:n_row], refs[n_row : n_row + n_plane]
    out_ref, weight_ref, share_ref, panel = refs[n_row + n_plane :]
    planes, mu, nu = lines[0].shape
    aux = planes - 1
    row, plane = lax.axis_index("row"), plane_index()
    for k in range(n_plane):
        panel[pl.ds(pl.multiple_of((plane ^ k) * mu, mu), mu), :] = bundles[k][aux]
    for k in range(n_row):
        weight_ref[:, pl.ds(pl.multiple_of((row ^ k) * nu, nu), nu)] = lines[k][aux]
    for p in range(aux):
        total = jnp.zeros((mu, nu), jnp.float32)
        for k in range(n_row):
            at = pl.multiple_of((row ^ k) * nu, nu)
            total += jnp.dot(lines[k][p], panel[pl.ds(at, nu), :], preferred_element_type=jnp.float32)
        out_ref[:, p * nu : (p + 1) * nu] = total.astype(out_ref.dtype)
    for p in range(aux):
        mixed = jnp.zeros((mu, nu), jnp.float32)
        for k in range(n_plane):
            at = pl.multiple_of((plane ^ k) * mu, mu)
            mixed += jnp.dot(weight_ref[:, pl.ds(at, mu)], bundles[k][p], preferred_element_type=jnp.float32)
        for q in range(aux):
            product = mixed * out_ref[:, q * nu : (q + 1) * nu].astype(jnp.float32)
            lanes = jnp.sum(product.reshape(mu // 8, 8, nu), axis=0)
            folded = sum([lanes[:, i : i + 128] for i in range(128, nu, 128)], lanes[:, :128])
            share_ref[p : p + 1, q * 128 : (q + 1) * 128] = jnp.sum(folded, axis=0, keepdims=True)


def half(lines, bundles):
    planes, mu, nu = lines[0].shape
    aux, n_row, n_plane = planes - 1, len(lines), len(bundles)
    kind = lines[0].dtype
    return pl.pallas_call(
        functools.partial(half_kernel, n_row, n_plane),
        out_shape=(
            jax.ShapeDtypeStruct((mu, aux * nu), kind),
            jax.ShapeDtypeStruct((mu, n_row * nu), kind),
            jax.ShapeDtypeStruct((aux, aux * 128), jnp.float32),
        ),
        in_specs=[VMEM] * (n_row + n_plane),
        out_specs=(VMEM, VMEM, VMEM),
        scratch_shapes=[pltpu.VMEM((n_plane * mu, nu), kind)],
        compiler_params=pltpu.CompilerParams(vmem_limit_bytes=ROOM),
        cost_estimate=pl.CostEstimate(
            flops=4 * aux * mu * nu * nu * n_row, bytes_accessed=8 * n_row * aux * mu * nu, transcendentals=0
        ),
        name="half_product",
    )(*lines, *bundles)


def dress_kernel(n_plane, weight_ref, *refs):
    halves, out_ref = refs[:n_plane], refs[n_plane]
    mu, aux, nu = out_ref.shape
    plane = plane_index()
    for q in range(aux):
        total = jnp.zeros((mu, nu), jnp.float32)
        for k in range(n_plane):
            at = pl.multiple_of((plane ^ k) * mu, mu)
            total += jnp.dot(
                weight_ref[:, pl.ds(at, mu)],
                halves[k][:, q * nu : (q + 1) * nu],
                preferred_element_type=jnp.float32,
            )
        out_ref[:, q, :] = total.astype(out_ref.dtype)


def dress(weight, halves, aux):
    mu, width = halves[0].shape
    n_plane = len(halves)
    return pl.pallas_call(
        functools.partial(dress_kernel, n_plane),
        out_shape=jax.ShapeDtypeStruct((mu, aux, width // aux), weight.dtype),
        in_specs=[VMEM] * (n_plane + 1),
        out_specs=VMEM,
        compiler_params=pltpu.CompilerParams(vmem_limit_bytes=ROOM),
        cost_estimate=pl.CostEstimate(
            flops=2 * mu * mu * width * n_plane, bytes_accessed=4 * n_plane * mu * width, transcendentals=0
        ),
        name="dress",
    )(weight, *halves)


def finish_kernel(total_ao, first_ref, second_ref, out_ref):
    aux = out_ref.shape[0]
    for q in range(aux):
        lanes = pl.ds(q * 128, 128)
        share = first_ref[:, lanes] + second_ref[:, lanes]
        out_ref[:, q : q + 1] = jnp.sum(share, axis=1, keepdims=True) / total_ao


def finish(first, second, total_ao):
    aux = first.shape[0]
    return pl.pallas_call(
        functools.partial(finish_kernel, total_ao),
        out_shape=jax.ShapeDtypeStruct((aux, aux), jnp.float32),
        in_specs=[VMEM, VMEM],
        out_specs=VMEM,
        compiler_params=pltpu.CompilerParams(vmem_limit_bytes=ROOM),
        name="finish",
    )(first, second)


def on_device(tensor_tiles, tile_pairs, tile_counts, occupied, virtual):
    aux = tensor_tiles.shape[1]
    nu = virtual.shape[1]
    n_row, n_plane = lax.axis_size("row"), lax.axis_size("col") * lax.axis_size("rep")
    near = list(range(2, n_plane, 2))
    sibling = lambda value: flip(value, PLANE, 1, n_plane)

    line, bundle = place(tile_pairs, tile_counts, tensor_tiles, occupied, virtual)
    lines = gather_row(line, n_row)
    bundles = []
    for value in [bundle] + [flip(bundle, PLANE, k, n_plane) for k in near]:
        bundles += [value, sibling(value)]
    own, weight, share = half(lines, bundles)

    arrivals = [flip(own, PLANE, k, n_plane) for k in near]
    step = 1
    while step < n_row:
        share = share + flip(share, "row", step, n_row)
        step *= 2
    step = 1
    while 2 * step < n_plane:
        share = share + flip(share, PLANE, step, n_plane)
        step *= 2
    share, arrivals = after(share, arrivals)
    last = flip(share, PLANE, step, n_plane)
    halves = []
    for value in [own] + arrivals:
        halves += [value, sibling(value)]
    last, dressed = after(last, dress(weight, halves, aux))
    polar = finish(share, last, n_row * nu)
    return polar, dressed


def solution(mesh):
    return jax.shard_map(
        on_device,
        mesh=mesh,
        in_specs=(P(EVERY, None, None, None), P(EVERY), P(EVERY), P(PLANE, "row"), P(PLANE, "row")),
        out_specs=(P(), P(PLANE, None, "row")),
        check_vma=False,
    )
```

```python
import functools

import jax
import jax.numpy as jnp
from jax import lax
from jax.experimental import pallas as pl
from jax.experimental.pallas import tpu as pltpu
from jax.sharding import PartitionSpec as P

PLANE = ("col", "rep")
EVERY = ("row", "col", "rep")
VMEM = pl.BlockSpec(memory_space=pltpu.VMEM)
SMEM = pl.BlockSpec(memory_space=pltpu.SMEM)
ROOM = 48 << 20


def flip(value, axes, mask, count):
    return lax.ppermute(value, axes, [(i, i ^ mask) for i in range(count)])


def after(value, earlier):
    return lax.optimization_barrier((value, earlier))


def gather_row(value, n_row):
    found = {0: value}
    step = n_row // 2
    while step:
        found.update({k ^ step: flip(held, "row", step, n_row) for k, held in list(found.items())})
        step //= 2
    return [found[k] for k in range(n_row)]


def plane_index():
    return lax.axis_index("col") * lax.axis_size("rep") + lax.axis_index("rep")


def place_kernel(nu_tiles, counts_ref, pairs_any, tiles_any, weight_any, column_any, *refs):
    line_ref, bundle_ref, pairs_ref, tiles_ref, sems = refs
    slots, aux, tile, _ = tiles_ref.shape
    copies = [
        pltpu.make_async_copy(source, target, sems.at[i])
        for i, (source, target) in enumerate(
            [
                (tiles_any, tiles_ref),
                (pairs_any, pairs_ref),
                (weight_any, line_ref.at[aux]),
                (column_any, bundle_ref.at[aux]),
            ]
        )
    ]
    for copy in copies:
        copy.start()
    for copy in copies:
        copy.wait()
    for t in range(slots):
        pair = pairs_ref[t]
        rows = pl.ds(pl.multiple_of(pair // nu_tiles * tile, tile), tile)
        cols = pl.ds(pl.multiple_of(pair % nu_tiles * tile, tile), tile)

        @pl.when(t < counts_ref[0])
        def _():
            for out_ref in (line_ref, bundle_ref):
                out_ref[:aux, rows, cols] = tiles_ref[t]

        @pl.when(t >= counts_ref[0])
        def _():
            for out_ref in (line_ref, bundle_ref):
                out_ref[:aux, rows, cols] = jnp.zeros((aux, tile, tile), out_ref.dtype)


def place(tile_pairs, tile_counts, tensor_tiles, weight, column):
    slots, aux, tile, _ = tensor_tiles.shape
    mu, nu = weight.shape
    shape = jax.ShapeDtypeStruct((aux + 1, mu, nu), weight.dtype)
    stays = [pltpu.with_memory_space_constraint(value, pltpu.HBM) for value in (tile_pairs, tensor_tiles, weight, column)]
    return pl.pallas_call(
        functools.partial(place_kernel, nu // tile),
        out_shape=(shape, shape),
        in_specs=[SMEM] + [pl.BlockSpec(memory_space=pltpu.HBM)] * 4,
        out_specs=(VMEM, VMEM),
        scratch_shapes=[
            pltpu.SMEM(tile_pairs.shape, tile_pairs.dtype),
            pltpu.VMEM(tensor_tiles.shape, tensor_tiles.dtype),
            pltpu.SemaphoreType.DMA((4,)),
        ],
        compiler_params=pltpu.CompilerParams(vmem_limit_bytes=ROOM),
        cost_estimate=pl.CostEstimate(flops=0, bytes_accessed=6 * tensor_tiles.size, transcendentals=0),
        name="place",
    )(tile_counts, *stays)


def half_kernel(n_row, n_plane, *refs):
    lines, bundles = refs[:n_row], refs[n_row : n_row + n_plane]
    out_ref, weight_ref, share_ref, panel = refs[n_row + n_plane :]
    planes, mu, nu = lines[0].shape
    aux = planes - 1
    row, plane = lax.axis_index("row"), plane_index()
    for k in range(n_plane):
        panel[pl.ds(pl.multiple_of((plane ^ k) * mu, mu), mu), :] = bundles[k][aux]
    for k in range(n_row):
        weight_ref[:, pl.ds(pl.multiple_of((row ^ k) * nu, nu), nu)] = lines[k][aux]
    for p in range(aux):
        total = jnp.zeros((mu, nu), jnp.float32)
        for k in range(n_row):
            at = pl.multiple_of((row ^ k) * nu, nu)
            total += jnp.dot(lines[k][p], panel[pl.ds(at, nu), :], preferred_element_type=jnp.float32)
        out_ref[:, p * nu : (p + 1) * nu] = total.astype(out_ref.dtype)
    for p in range(aux):
        mixed = jnp.zeros((mu, nu), jnp.float32)
        for k in range(n_plane):
            at = pl.multiple_of((plane ^ k) * mu, mu)
            mixed += jnp.dot(weight_ref[:, pl.ds(at, mu)], bundles[k][p], preferred_element_type=jnp.float32)
        for q in range(aux):
            product = mixed * out_ref[:, q * nu : (q + 1) * nu].astype(jnp.float32)
            lanes = jnp.sum(product.reshape(mu // 8, 8, nu), axis=0)
            folded = sum([lanes[:, i : i + 128] for i in range(128, nu, 128)], lanes[:, :128])
            share_ref[p : p + 1, q * 128 : (q + 1) * 128] = jnp.sum(folded, axis=0, keepdims=True)


def half(lines, bundles):
    planes, mu, nu = lines[0].shape
    aux, n_row, n_plane = planes - 1, len(lines), len(bundles)
    kind = lines[0].dtype
    return pl.pallas_call(
        functools.partial(half_kernel, n_row, n_plane),
        out_shape=(
            jax.ShapeDtypeStruct((mu, aux * nu), kind),
            jax.ShapeDtypeStruct((mu, n_row * nu), kind),
            jax.ShapeDtypeStruct((aux, aux * 128), jnp.float32),
        ),
        in_specs=[VMEM] * (n_row + n_plane),
        out_specs=(VMEM, VMEM, VMEM),
        scratch_shapes=[pltpu.VMEM((n_plane * mu, nu), kind)],
        compiler_params=pltpu.CompilerParams(vmem_limit_bytes=ROOM),
        cost_estimate=pl.CostEstimate(
            flops=4 * aux * mu * nu * nu * n_row, bytes_accessed=8 * n_row * aux * mu * nu, transcendentals=0
        ),
        name="half_product",
    )(*lines, *bundles)


def dress_kernel(n_plane, weight_ref, *refs):
    halves, out_ref = refs[:n_plane], refs[n_plane]
    mu, aux, nu = out_ref.shape
    plane = plane_index()
    for q in range(aux):
        total = jnp.zeros((mu, nu), jnp.float32)
        for k in range(n_plane):
            at = pl.multiple_of((plane ^ k) * mu, mu)
            total += jnp.dot(
                weight_ref[:, pl.ds(at, mu)],
                halves[k][:, q * nu : (q + 1) * nu],
                preferred_element_type=jnp.float32,
            )
        out_ref[:, q, :] = total.astype(out_ref.dtype)


def dress(weight, halves, aux):
    mu, width = halves[0].shape
    n_plane = len(halves)
    return pl.pallas_call(
        functools.partial(dress_kernel, n_plane),
        out_shape=jax.ShapeDtypeStruct((mu, aux, width // aux), weight.dtype),
        in_specs=[VMEM] * (n_plane + 1),
        out_specs=VMEM,
        compiler_params=pltpu.CompilerParams(vmem_limit_bytes=ROOM),
        cost_estimate=pl.CostEstimate(
            flops=2 * mu * mu * width * n_plane, bytes_accessed=4 * n_plane * mu * width, transcendentals=0
        ),
        name="dress",
    )(weight, *halves)


def finish_kernel(total_ao, first_ref, second_ref, out_ref):
    aux = out_ref.shape[0]
    for q in range(aux):
        lanes = pl.ds(q * 128, 128)
        share = first_ref[:, lanes] + second_ref[:, lanes]
        out_ref[:, q : q + 1] = jnp.sum(share, axis=1, keepdims=True) / total_ao


def finish(first, second, total_ao):
    aux = first.shape[0]
    return pl.pallas_call(
        functools.partial(finish_kernel, total_ao),
        out_shape=jax.ShapeDtypeStruct((aux, aux), jnp.float32),
        in_specs=[VMEM, VMEM],
        out_specs=VMEM,
        compiler_params=pltpu.CompilerParams(vmem_limit_bytes=ROOM),
        name="finish",
    )(first, second)


def on_device(tensor_tiles, tile_pairs, tile_counts, occupied, virtual):
    aux = tensor_tiles.shape[1]
    nu = virtual.shape[1]
    n_row, n_plane = lax.axis_size("row"), lax.axis_size("col") * lax.axis_size("rep")
    near = list(range(2, n_plane, 2))
    sibling = lambda value: flip(value, PLANE, 1, n_plane)

    line, bundle = place(tile_pairs, tile_counts, tensor_tiles, occupied, virtual)
    lines = gather_row(line, n_row)
    bundles = []
    for value in [bundle] + [flip(bundle, PLANE, k, n_plane) for k in near]:
        bundles += [value, sibling(value)]
    own, weight, share = half(lines, bundles)

    direct = [k for k in near if k & (k - 1) == 0]
    arrivals = {k: flip(own, PLANE, k, n_plane) for k in direct}
    share = sum([flip(share, "row", k, n_row) for k in range(1, n_row)], share)
    share, own = after(share, own)
    arrivals.update({k: flip(own, PLANE, k, n_plane) for k in near if k not in arrivals})
    arrivals = [arrivals[k] for k in near]
    step = 1
    while 2 * step < n_plane:
        share = share + flip(share, PLANE, step, n_plane)
        step *= 2
    share, arrivals = after(share, arrivals)
    last = flip(share, PLANE, step, n_plane)
    halves = []
    for value in [own] + arrivals:
        halves += [value, sibling(value)]
    last, dressed = after(last, dress(weight, halves, aux))
    polar = finish(share, last, n_row * nu)
    return polar, dressed


def solution(mesh):
    return jax.shard_map(
        on_device,
        mesh=mesh,
        in_specs=(P(EVERY, None, None, None), P(EVERY), P(EVERY), P(PLANE, "row"), P(PLANE, "row")),
        out_specs=(P(), P(PLANE, None, "row")),
        check_vma=False,
    )
```

```python
import functools

import jax
import jax.numpy as jnp
from jax import lax
from jax.experimental import pallas as pl
from jax.experimental.pallas import tpu as pltpu
from jax.sharding import PartitionSpec as P

PLANE = ("col", "rep")
EVERY = ("row", "col", "rep")
VMEM = pl.BlockSpec(memory_space=pltpu.VMEM)
SMEM = pl.BlockSpec(memory_space=pltpu.SMEM)
ROOM = 48 << 20


def flip(value, axes, mask, count):
    return lax.ppermute(value, axes, [(i, i ^ mask) for i in range(count)])


def after(value, earlier):
    return lax.optimization_barrier((value, earlier))


def split_kernel(value_ref, first_ref, second_ref):
    cut = first_ref.shape[0]
    first_ref[...] = value_ref[:cut]
    second_ref[...] = value_ref[cut:]


def split(value):
    planes, mu, nu = value.shape
    cut = (planes - 1) // 2
    return pl.pallas_call(
        split_kernel,
        out_shape=[jax.ShapeDtypeStruct((count, mu, nu), value.dtype) for count in (cut, planes - cut)],
        in_specs=[VMEM],
        out_specs=[VMEM, VMEM],
        compiler_params=pltpu.CompilerParams(vmem_limit_bytes=ROOM),
        cost_estimate=pl.CostEstimate(flops=0, bytes_accessed=4 * value.size, transcendentals=0),
        name="split",
    )(value)


def gather_row(value, n_row):
    found = {0: value}
    step = n_row // 2
    while step > 1:
        found.update({k ^ step: flip(held, "row", step, n_row) for k, held in list(found.items())})
        step //= 2
    whole = [found.pop(0), flip(value, "row", 1, n_row)]
    parts = {k: split(held) for k, held in found.items()}
    for i in range(2):
        for k in found:
            parts.setdefault(k ^ 1, []).append(flip(parts[k][i], "row", 1, n_row))
    return whole, [parts[k][0] for k in range(2, n_row)], [parts[k][1] for k in range(2, n_row)]


def plane_index():
    return lax.axis_index("col") * lax.axis_size("rep") + lax.axis_index("rep")


def place_kernel(nu_tiles, counts_ref, pairs_any, tiles_any, weight_any, column_any, *refs):
    line_ref, bundle_ref, pairs_ref, tiles_ref, sems = refs
    slots, aux, tile, _ = tiles_ref.shape
    copies = [
        pltpu.make_async_copy(source, target, sems.at[i])
        for i, (source, target) in enumerate(
            [
                (tiles_any, tiles_ref),
                (pairs_any, pairs_ref),
                (weight_any, line_ref.at[aux]),
                (column_any, bundle_ref.at[aux]),
            ]
        )
    ]
    for copy in copies:
        copy.start()
    for copy in copies:
        copy.wait()
    for t in range(slots):
        pair = pairs_ref[t]
        rows = pl.ds(pl.multiple_of(pair // nu_tiles * tile, tile), tile)
        cols = pl.ds(pl.multiple_of(pair % nu_tiles * tile, tile), tile)

        def store(value):
            line_ref[:aux, rows, cols] = value
            bundle_ref[:aux, rows, cols] = value

        @pl.when(t < counts_ref[0])
        def _():
            store(tiles_ref[t])

        @pl.when(t >= counts_ref[0])
        def _():
            store(jnp.zeros((aux, tile, tile), line_ref.dtype))


def place(tile_pairs, tile_counts, tensor_tiles, weight, column):
    slots, aux, tile, _ = tensor_tiles.shape
    mu, nu = weight.shape
    shape = jax.ShapeDtypeStruct((aux + 1, mu, nu), weight.dtype)
    stays = [pltpu.with_memory_space_constraint(value, pltpu.HBM) for value in (tile_pairs, tensor_tiles, weight, column)]
    return pl.pallas_call(
        functools.partial(place_kernel, nu // tile),
        out_shape=(shape, shape),
        in_specs=[SMEM] + [pl.BlockSpec(memory_space=pltpu.HBM)] * 4,
        out_specs=(VMEM, VMEM),
        scratch_shapes=[
            pltpu.SMEM(tile_pairs.shape, tile_pairs.dtype),
            pltpu.VMEM(tensor_tiles.shape, tensor_tiles.dtype),
            pltpu.SemaphoreType.DMA((4,)),
        ],
        compiler_params=pltpu.CompilerParams(vmem_limit_bytes=ROOM),
        cost_estimate=pl.CostEstimate(flops=0, bytes_accessed=6 * tensor_tiles.size, transcendentals=0),
        name="place",
    )(tile_counts, *stays)


def multiply(pieces, panel, p, out_ref, column):
    mu, nu = pieces[0].shape
    row = lax.axis_index("row")
    total = jnp.zeros((mu, nu), jnp.float32)
    for k, piece in enumerate(pieces):
        at = pl.multiple_of((row ^ k) * nu, nu)
        total += jnp.dot(piece[...], panel[pl.ds(at, nu), :], preferred_element_type=jnp.float32)
    out_ref[:, column * nu : (column + 1) * nu] = total.astype(out_ref.dtype)


def first_kernel(n_row, n_plane, *refs):
    whole, parts, bundles = refs[:2], refs[2:n_row], refs[n_row : n_row + n_plane]
    out_ref, panel = refs[n_row + n_plane :]
    planes, mu, _ = whole[0].shape
    plane = plane_index()
    for k in range(n_plane):
        panel[pl.ds(pl.multiple_of((plane ^ k) * mu, mu), mu), :] = bundles[k][planes - 1]
    for p in range((planes - 1) // 2):
        multiply([ref.at[p] for ref in (*whole, *parts)], panel, p, out_ref, p)


def first_half(whole, parts, bundles):
    planes, mu, nu = whole[0].shape
    cut, n_row, n_plane = (planes - 1) // 2, 2 + len(parts), len(bundles)
    kind = whole[0].dtype
    return pl.pallas_call(
        functools.partial(first_kernel, n_row, n_plane),
        out_shape=(
            jax.ShapeDtypeStruct((mu, cut * nu), kind),
            jax.ShapeDtypeStruct((n_plane * mu, nu), kind),
        ),
        in_specs=[VMEM] * (n_row + n_plane),
        out_specs=(VMEM, VMEM),
        compiler_params=pltpu.CompilerParams(vmem_limit_bytes=ROOM),
        cost_estimate=pl.CostEstimate(
            flops=2 * cut * mu * nu * nu * n_row, bytes_accessed=4 * n_row * cut * mu * nu, transcendentals=0
        ),
        name="half_first",
    )(*whole, *parts, *bundles)


def second_kernel(n_row, n_plane, *refs):
    whole, parts, bundles = refs[:2], refs[2:n_row], refs[n_row : n_row + n_plane]
    first_ref, panel, out_ref, weight_ref, share_ref = refs[n_row + n_plane :]
    planes, mu, nu = whole[0].shape
    aux = planes - 1
    cut = aux // 2
    row, plane = lax.axis_index("row"), plane_index()
    for p in range(cut, aux):
        pieces = [ref.at[p] for ref in whole] + [ref.at[p - cut] for ref in parts]
        multiply(pieces, panel, p, out_ref, p - cut)
    for k, piece in enumerate([ref.at[aux] for ref in whole] + [ref.at[aux - cut] for ref in parts]):
        weight_ref[:, pl.ds(pl.multiple_of((row ^ k) * nu, nu), nu)] = piece[...]
    for p in range(aux):
        mixed = jnp.zeros((mu, nu), jnp.float32)
        for k in range(n_plane):
            at = pl.multiple_of((plane ^ k) * mu, mu)
            mixed += jnp.dot(weight_ref[:, pl.ds(at, mu)], bundles[k][p], preferred_element_type=jnp.float32)
        for q in range(aux):
            value, at = (first_ref, q) if q < cut else (out_ref, q - cut)
            product = mixed * value[:, at * nu : (at + 1) * nu].astype(jnp.float32)
            lanes = jnp.sum(product.reshape(mu // 8, 8, nu), axis=0)
            folded = sum([lanes[:, i : i + 128] for i in range(128, nu, 128)], lanes[:, :128])
            share_ref[p : p + 1, q * 128 : (q + 1) * 128] = jnp.sum(folded, axis=0, keepdims=True)


def second_half(whole, parts, bundles, first, panel):
    planes, mu, nu = whole[0].shape
    aux, n_row, n_plane = planes - 1, 2 + len(parts), len(bundles)
    kind = whole[0].dtype
    return pl.pallas_call(
        functools.partial(second_kernel, n_row, n_plane),
        out_shape=(
            jax.ShapeDtypeStruct((mu, (aux - aux // 2) * nu), kind),
            jax.ShapeDtypeStruct((mu, n_row * nu), kind),
            jax.ShapeDtypeStruct((aux, aux * 128), jnp.float32),
        ),
        in_specs=[VMEM] * (n_row + n_plane + 2),
        out_specs=(VMEM, VMEM, VMEM),
        compiler_params=pltpu.CompilerParams(vmem_limit_bytes=ROOM),
        cost_estimate=pl.CostEstimate(
            flops=3 * aux * mu * nu * nu * n_row, bytes_accessed=6 * n_row * aux * mu * nu, transcendentals=0
        ),
        name="half_second",
    )(*whole, *parts, *bundles, first, panel)


def dress_kernel(n_plane, weight_ref, *refs):
    firsts, seconds, out_ref = refs[:n_plane], refs[n_plane : 2 * n_plane], refs[2 * n_plane]
    mu, aux, nu = out_ref.shape
    cut = firsts[0].shape[1] // nu
    plane = plane_index()
    for q in range(aux):
        halves, at = (firsts, q) if q < cut else (seconds, q - cut)
        total = jnp.zeros((mu, nu), jnp.float32)
        for k in range(n_plane):
            total += jnp.dot(
                weight_ref[:, pl.ds(pl.multiple_of((plane ^ k) * mu, mu), mu)],
                halves[k][:, at * nu : (at + 1) * nu],
                preferred_element_type=jnp.float32,
            )
        out_ref[:, q, :] = total.astype(out_ref.dtype)


def dress(weight, firsts, seconds, aux):
    n_plane = len(firsts)
    mu = weight.shape[0]
    nu = (firsts[0].shape[1] + seconds[0].shape[1]) // aux
    return pl.pallas_call(
        functools.partial(dress_kernel, n_plane),
        out_shape=jax.ShapeDtypeStruct((mu, aux, nu), weight.dtype),
        in_specs=[VMEM] * (2 * n_plane + 1),
        out_specs=VMEM,
        compiler_params=pltpu.CompilerParams(vmem_limit_bytes=ROOM),
        cost_estimate=pl.CostEstimate(
            flops=2 * mu * mu * aux * nu * n_plane, bytes_accessed=4 * n_plane * mu * aux * nu, transcendentals=0
        ),
        name="dress",
    )(weight, *firsts, *seconds)


def finish_kernel(total_ao, first_ref, second_ref, out_ref):
    aux = out_ref.shape[0]
    for q in range(aux):
        lanes = pl.ds(q * 128, 128)
        share = first_ref[:, lanes] + second_ref[:, lanes]
        out_ref[:, q : q + 1] = jnp.sum(share, axis=1, keepdims=True) / total_ao


def finish(first, second, total_ao):
    aux = first.shape[0]
    return pl.pallas_call(
        functools.partial(finish_kernel, total_ao),
        out_shape=jax.ShapeDtypeStruct((aux, aux), jnp.float32),
        in_specs=[VMEM, VMEM],
        out_specs=VMEM,
        compiler_params=pltpu.CompilerParams(vmem_limit_bytes=ROOM),
        name="finish",
    )(first, second)


def on_device(tensor_tiles, tile_pairs, tile_counts, occupied, virtual):
    aux = tensor_tiles.shape[1]
    nu = virtual.shape[1]
    n_row, n_plane = lax.axis_size("row"), lax.axis_size("col") * lax.axis_size("rep")
    near = list(range(2, n_plane, 2))
    sibling = lambda value: flip(value, PLANE, 1, n_plane)

    line, bundle = place(tile_pairs, tile_counts, tensor_tiles, occupied, virtual)
    whole, first_parts, second_parts = gather_row(line, n_row)
    bundles = []
    for value in [bundle] + [flip(bundle, PLANE, k, n_plane) for k in near]:
        bundles += [value, sibling(value)]

    first, panel = first_half(whole, first_parts, bundles)
    firsts = [first] + [flip(first, PLANE, k, n_plane) for k in near]
    second, weight, share = second_half(whole, second_parts, bundles, first, panel)
    second, firsts = after(second, firsts)
    seconds = [second] + [flip(second, PLANE, k, n_plane) for k in near]
    both = lambda values: [held for value in values for held in (value, sibling(value))]

    step = 1
    while step < n_row:
        share = share + flip(share, "row", step, n_row)
        step *= 2
    share, seconds = after(share, seconds)
    step = 1
    while 2 * step < n_plane:
        share = share + flip(share, PLANE, step, n_plane)
        step *= 2
    share, firsts = after(share, both(firsts))
    last = flip(share, PLANE, step, n_plane)
    last, dressed = after(last, dress(weight, firsts, both(seconds), aux))
    polar = finish(share, last, n_row * nu)
    return polar, dressed


def solution(mesh):
    return jax.shard_map(
        on_device,
        mesh=mesh,
        in_specs=(P(EVERY, None, None, None), P(EVERY), P(EVERY), P(PLANE, "row"), P(PLANE, "row")),
        out_specs=(P(), P(PLANE, None, "row")),
        check_vma=False,
    )
```

```python
import functools

import jax
import jax.numpy as jnp
from jax import lax
from jax.experimental import pallas as pl
from jax.experimental.pallas import tpu as pltpu
from jax.sharding import PartitionSpec as P

PLANE = ("col", "rep")
EVERY = ("row", "col", "rep")
VMEM = pl.BlockSpec(memory_space=pltpu.VMEM)
SMEM = pl.BlockSpec(memory_space=pltpu.SMEM)
ROOM = 48 << 20


def flip(value, axes, mask, count):
    return lax.ppermute(value, axes, [(i, i ^ mask) for i in range(count)])


def after(value, earlier):
    return lax.optimization_barrier((value, earlier))


def gather_row(value, n_row):
    found = {0: value}
    step = n_row // 2
    while step:
        found.update({k ^ step: flip(held, "row", step, n_row) for k, held in list(found.items())})
        step //= 2
    return [found[k] for k in range(n_row)]


def plane_index():
    return lax.axis_index("col") * lax.axis_size("rep") + lax.axis_index("rep")


def place_kernel(nu_tiles, counts_ref, pairs_any, tiles_any, column_any, *refs):
    line_ref, bundle_ref, pairs_ref, tiles_ref, sems = refs
    slots, aux, tile, _ = tiles_ref.shape
    copies = [
        pltpu.make_async_copy(source, target, sems.at[i])
        for i, (source, target) in enumerate(
            [
                (tiles_any, tiles_ref),
                (pairs_any, pairs_ref),
                (column_any, bundle_ref.at[aux]),
            ]
        )
    ]
    for copy in copies:
        copy.start()
    for copy in copies:
        copy.wait()
    for t in range(slots):
        pair = pairs_ref[t]
        rows = pl.ds(pl.multiple_of(pair // nu_tiles * tile, tile), tile)
        cols = pl.ds(pl.multiple_of(pair % nu_tiles * tile, tile), tile)

        @pl.when(t < counts_ref[0])
        def _():
            for out_ref in (line_ref, bundle_ref):
                out_ref[:aux, rows, cols] = tiles_ref[t]

        @pl.when(t >= counts_ref[0])
        def _():
            for out_ref in (line_ref, bundle_ref):
                out_ref[:aux, rows, cols] = jnp.zeros((aux, tile, tile), out_ref.dtype)


def place(tile_pairs, tile_counts, tensor_tiles, column):
    slots, aux, tile, _ = tensor_tiles.shape
    mu, nu = column.shape
    shapes = [jax.ShapeDtypeStruct((planes, mu, nu), column.dtype) for planes in (aux, aux + 1)]
    stays = [pltpu.with_memory_space_constraint(value, pltpu.HBM) for value in (tile_pairs, tensor_tiles, column)]
    return pl.pallas_call(
        functools.partial(place_kernel, nu // tile),
        out_shape=shapes,
        in_specs=[SMEM] + [pl.BlockSpec(memory_space=pltpu.HBM)] * 3,
        out_specs=(VMEM, VMEM),
        scratch_shapes=[
            pltpu.SMEM(tile_pairs.shape, tile_pairs.dtype),
            pltpu.VMEM(tensor_tiles.shape, tensor_tiles.dtype),
            pltpu.SemaphoreType.DMA((3,)),
        ],
        compiler_params=pltpu.CompilerParams(vmem_limit_bytes=ROOM),
        cost_estimate=pl.CostEstimate(flops=0, bytes_accessed=6 * tensor_tiles.size, transcendentals=0),
        name="place",
    )(tile_counts, *stays)


def half_kernel(n_row, n_plane, *refs):
    lines, bundles = refs[:n_row], refs[n_row : n_row + n_plane]
    out_ref, panel = refs[n_row + n_plane :]
    aux, mu, nu = lines[0].shape
    row, plane = lax.axis_index("row"), plane_index()
    for k in range(n_plane):
        panel[pl.ds(pl.multiple_of((plane ^ k) * mu, mu), mu), :] = bundles[k][aux]
    for p in range(aux):
        total = jnp.zeros((mu, nu), jnp.float32)
        for k in range(n_row):
            at = pl.multiple_of((row ^ k) * nu, nu)
            total += jnp.dot(lines[k][p], panel[pl.ds(at, nu), :], preferred_element_type=jnp.float32)
        out_ref[:, p * nu : (p + 1) * nu] = total.astype(out_ref.dtype)


def half(lines, bundles):
    aux, mu, nu = lines[0].shape
    n_row, n_plane = len(lines), len(bundles)
    kind = lines[0].dtype
    return pl.pallas_call(
        functools.partial(half_kernel, n_row, n_plane),
        out_shape=jax.ShapeDtypeStruct((mu, aux * nu), kind),
        in_specs=[VMEM] * (n_row + n_plane),
        out_specs=VMEM,
        scratch_shapes=[pltpu.VMEM((n_plane * mu, nu), kind)],
        compiler_params=pltpu.CompilerParams(vmem_limit_bytes=ROOM),
        cost_estimate=pl.CostEstimate(
            flops=2 * aux * mu * nu * nu * n_row, bytes_accessed=4 * n_row * aux * mu * nu, transcendentals=0
        ),
        name="half_product",
    )(*lines, *bundles)


def share_kernel(n_row, n_plane, half_ref, *refs):
    weights, bundles = refs[:n_row], refs[n_row : n_row + n_plane]
    weight_ref, share_ref = refs[n_row + n_plane :]
    mu, nu = weights[0].shape
    aux = bundles[0].shape[0] - 1
    row, plane = lax.axis_index("row"), plane_index()
    for k in range(n_row):
        weight_ref[:, pl.ds(pl.multiple_of((row ^ k) * nu, nu), nu)] = weights[k][...]
    for p in range(aux):
        mixed = jnp.zeros((mu, nu), jnp.float32)
        for k in range(n_plane):
            at = pl.multiple_of((plane ^ k) * mu, mu)
            mixed += jnp.dot(weight_ref[:, pl.ds(at, mu)], bundles[k][p], preferred_element_type=jnp.float32)
        for q in range(aux):
            product = mixed * half_ref[:, q * nu : (q + 1) * nu].astype(jnp.float32)
            lanes = jnp.sum(product.reshape(mu // 8, 8, nu), axis=0)
            folded = sum([lanes[:, i : i + 128] for i in range(128, nu, 128)], lanes[:, :128])
            share_ref[p : p + 1, q * 128 : (q + 1) * 128] = jnp.sum(folded, axis=0, keepdims=True)


def share_of(half_block, weights, bundles):
    mu, nu = weights[0].shape
    aux, n_row, n_plane = bundles[0].shape[0] - 1, len(weights), len(bundles)
    return pl.pallas_call(
        functools.partial(share_kernel, n_row, n_plane),
        out_shape=(
            jax.ShapeDtypeStruct((mu, n_row * nu), weights[0].dtype),
            jax.ShapeDtypeStruct((aux, aux * 128), jnp.float32),
        ),
        in_specs=[VMEM] * (1 + n_row + n_plane),
        out_specs=(VMEM, VMEM),
        compiler_params=pltpu.CompilerParams(vmem_limit_bytes=ROOM),
        cost_estimate=pl.CostEstimate(
            flops=2 * aux * mu * mu * nu * n_plane, bytes_accessed=4 * n_plane * aux * mu * nu, transcendentals=0
        ),
        name="polar_share",
    )(half_block, *weights, *bundles)


def dress_kernel(n_plane, weight_ref, *refs):
    halves, out_ref = refs[:n_plane], refs[n_plane]
    mu, aux, nu = out_ref.shape
    plane = plane_index()
    for q in range(aux):
        total = jnp.zeros((mu, nu), jnp.float32)
        for k in range(n_plane):
            at = pl.multiple_of((plane ^ k) * mu, mu)
            total += jnp.dot(
                weight_ref[:, pl.ds(at, mu)],
                halves[k][:, q * nu : (q + 1) * nu],
                preferred_element_type=jnp.float32,
            )
        out_ref[:, q, :] = total.astype(out_ref.dtype)


def dress(weight, halves, aux):
    mu, width = halves[0].shape
    n_plane = len(halves)
    return pl.pallas_call(
        functools.partial(dress_kernel, n_plane),
        out_shape=jax.ShapeDtypeStruct((mu, aux, width // aux), weight.dtype),
        in_specs=[VMEM] * (n_plane + 1),
        out_specs=VMEM,
        compiler_params=pltpu.CompilerParams(vmem_limit_bytes=ROOM),
        cost_estimate=pl.CostEstimate(
            flops=2 * mu * mu * width * n_plane, bytes_accessed=4 * n_plane * mu * width, transcendentals=0
        ),
        name="dress",
    )(weight, *halves)


def finish_kernel(total_ao, *refs):
    shares, out_ref = refs[:-1], refs[-1]
    aux = out_ref.shape[0]
    for q in range(aux):
        lanes = pl.ds(q * 128, 128)
        total = sum([ref[:, lanes] for ref in shares[1:]], shares[0][:, lanes])
        out_ref[:, q : q + 1] = jnp.sum(total, axis=1, keepdims=True) / total_ao


def finish(shares, total_ao):
    aux = shares[0].shape[0]
    return pl.pallas_call(
        functools.partial(finish_kernel, total_ao),
        out_shape=jax.ShapeDtypeStruct((aux, aux), jnp.float32),
        in_specs=[VMEM] * len(shares),
        out_specs=VMEM,
        compiler_params=pltpu.CompilerParams(vmem_limit_bytes=ROOM),
        name="finish",
    )(*shares)


def on_device(tensor_tiles, tile_pairs, tile_counts, occupied, virtual):
    aux = tensor_tiles.shape[1]
    nu = virtual.shape[1]
    n_row, n_plane = lax.axis_size("row"), lax.axis_size("col") * lax.axis_size("rep")
    near = list(range(2, n_plane, 2))
    sibling = lambda value: flip(value, PLANE, 1, n_plane)

    line, bundle = place(tile_pairs, tile_counts, tensor_tiles, virtual)
    lines = gather_row(line, n_row)
    occupied, lines[1] = after(occupied, lines[1])
    bundles = []
    for value in [bundle] + [flip(bundle, PLANE, k, n_plane) for k in near]:
        bundles += [value, sibling(value)]
    own = half(lines, bundles)
    weights = gather_row(occupied, n_row)
    arrivals = []
    for k in near:
        if k & (k - 1):
            own, weights[-2] = after(own, weights[-2])
        arrivals.append(flip(own, PLANE, k, n_plane))
    weight, share = share_of(own, weights, bundles)
    step = 1
    while step < n_row:
        share = share + flip(share, "row", step, n_row)
        step *= 2
    share = share + sibling(share)
    share, arrivals = after(share, arrivals)
    shares = [share] + [flip(share, PLANE, k, n_plane) for k in near]
    halves = []
    for value in [own] + arrivals:
        halves += [value, sibling(value)]
    shares, dressed = after(shares, dress(weight, halves, aux))
    polar = finish(shares, n_row * nu)
    return polar, dressed


def solution(mesh):
    return jax.shard_map(
        on_device,
        mesh=mesh,
        in_specs=(P(EVERY, None, None, None), P(EVERY), P(EVERY), P(PLANE, "row"), P(PLANE, "row")),
        out_specs=(P(), P(PLANE, None, "row")),
        check_vma=False,
    )
```

```python
import functools

import jax
import jax.numpy as jnp
from jax import lax
from jax.experimental import pallas as pl
from jax.experimental.pallas import tpu as pltpu
from jax.sharding import PartitionSpec as P

PLANE = ("col", "rep")
EVERY = ("row", "col", "rep")
VMEM = pl.BlockSpec(memory_space=pltpu.VMEM)
SMEM = pl.BlockSpec(memory_space=pltpu.SMEM)
ROOM = 48 << 20


def flip(value, axes, mask, count):
    return lax.ppermute(value, axes, [(i, i ^ mask) for i in range(count)])


def after(value, earlier):
    return lax.optimization_barrier((value, earlier))


def gather_row(value, n_row):
    found = {0: value}
    step = n_row // 2
    while step:
        found.update({k ^ step: flip(held, "row", step, n_row) for k, held in list(found.items())})
        step //= 2
    return [found[k] for k in range(n_row)]


def plane_index():
    return lax.axis_index("col") * lax.axis_size("rep") + lax.axis_index("rep")


def place_kernel(nu_tiles, counts_ref, pairs_any, tiles_any, weight_any, column_any, *refs):
    line_ref, bundle_ref, pairs_ref, tiles_ref, sems = refs
    slots, aux, tile, _ = tiles_ref.shape
    copies = [
        pltpu.make_async_copy(source, target, sems.at[i])
        for i, (source, target) in enumerate(
            [
                (tiles_any, tiles_ref),
                (pairs_any, pairs_ref),
                (weight_any, line_ref.at[aux]),
                (column_any, bundle_ref.at[aux]),
            ]
        )
    ]
    for copy in copies:
        copy.start()
    for copy in copies:
        copy.wait()
    for t in range(slots):
        pair = pairs_ref[t]
        rows = pl.ds(pl.multiple_of(pair // nu_tiles * tile, tile), tile)
        cols = pl.ds(pl.multiple_of(pair % nu_tiles * tile, tile), tile)

        @pl.when(t < counts_ref[0])
        def _():
            for out_ref in (line_ref, bundle_ref):
                out_ref[:aux, rows, cols] = tiles_ref[t]

        @pl.when(t >= counts_ref[0])
        def _():
            for out_ref in (line_ref, bundle_ref):
                out_ref[:aux, rows, cols] = jnp.zeros((aux, tile, tile), out_ref.dtype)


def place(tile_pairs, tile_counts, tensor_tiles, weight, column):
    slots, aux, tile, _ = tensor_tiles.shape
    mu, nu = weight.shape
    shape = jax.ShapeDtypeStruct((aux + 1, mu, nu), weight.dtype)
    stays = [pltpu.with_memory_space_constraint(value, pltpu.HBM) for value in (tile_pairs, tensor_tiles, weight, column)]
    return pl.pallas_call(
        functools.partial(place_kernel, nu // tile),
        out_shape=(shape, shape),
        in_specs=[SMEM] + [pl.BlockSpec(memory_space=pltpu.HBM)] * 4,
        out_specs=(VMEM, VMEM),
        scratch_shapes=[
            pltpu.SMEM(tile_pairs.shape, tile_pairs.dtype),
            pltpu.VMEM(tensor_tiles.shape, tensor_tiles.dtype),
            pltpu.SemaphoreType.DMA((4,)),
        ],
        compiler_params=pltpu.CompilerParams(vmem_limit_bytes=ROOM),
        cost_estimate=pl.CostEstimate(flops=0, bytes_accessed=6 * tensor_tiles.size, transcendentals=0),
        name="place",
    )(tile_counts, *stays)


def half_kernel(n_row, n_plane, *refs):
    lines, bundles = refs[:n_row], refs[n_row : n_row + n_plane]
    out_ref, panel = refs[n_row + n_plane :]
    planes, mu, nu = lines[0].shape
    aux = planes - 1
    row, plane = lax.axis_index("row"), plane_index()
    for k in range(n_plane):
        panel[pl.ds(pl.multiple_of((plane ^ k) * mu, mu), mu), :] = bundles[k][aux]
    for p in range(aux):
        total = jnp.zeros((mu, nu), jnp.float32)
        for k in range(n_row):
            at = pl.multiple_of((row ^ k) * nu, nu)
            total += jnp.dot(lines[k][p], panel[pl.ds(at, nu), :], preferred_element_type=jnp.float32)
        out_ref[:, p * nu : (p + 1) * nu] = total.astype(out_ref.dtype)


def half(lines, bundles):
    planes, mu, nu = lines[0].shape
    aux = planes - 1
    n_row, n_plane = len(lines), len(bundles)
    kind = lines[0].dtype
    return pl.pallas_call(
        functools.partial(half_kernel, n_row, n_plane),
        out_shape=jax.ShapeDtypeStruct((mu, aux * nu), kind),
        in_specs=[VMEM] * (n_row + n_plane),
        out_specs=VMEM,
        scratch_shapes=[pltpu.VMEM((n_plane * mu, nu), kind)],
        compiler_params=pltpu.CompilerParams(vmem_limit_bytes=ROOM),
        cost_estimate=pl.CostEstimate(
            flops=2 * aux * mu * nu * nu * n_row, bytes_accessed=4 * n_row * aux * mu * nu, transcendentals=0
        ),
        name="half_product",
    )(*lines, *bundles)


def share_kernel(n_row, n_plane, half_ref, *refs):
    weights, bundles = refs[:n_row], refs[n_row : n_row + n_plane]
    weight_ref, share_ref = refs[n_row + n_plane :]
    planes, mu, nu = weights[0].shape
    aux = planes - 1
    row, plane = lax.axis_index("row"), plane_index()
    for k in range(n_row):
        weight_ref[:, pl.ds(pl.multiple_of((row ^ k) * nu, nu), nu)] = weights[k][weights[k].shape[0] - 1]
    for p in range(aux):
        mixed = jnp.zeros((mu, nu), jnp.float32)
        for k in range(n_plane):
            at = pl.multiple_of((plane ^ k) * mu, mu)
            mixed += jnp.dot(weight_ref[:, pl.ds(at, mu)], bundles[k][p], preferred_element_type=jnp.float32)
        for q in range(aux):
            product = mixed * half_ref[:, q * nu : (q + 1) * nu].astype(jnp.float32)
            lanes = jnp.sum(product.reshape(mu // 8, 8, nu), axis=0)
            folded = sum([lanes[:, i : i + 128] for i in range(128, nu, 128)], lanes[:, :128])
            share_ref[p : p + 1, q * 128 : (q + 1) * 128] = jnp.sum(folded, axis=0, keepdims=True)


def share_of(half_block, weights, bundles):
    planes, mu, nu = weights[0].shape
    aux, n_row, n_plane = planes - 1, len(weights), len(bundles)
    return pl.pallas_call(
        functools.partial(share_kernel, n_row, n_plane),
        out_shape=(
            jax.ShapeDtypeStruct((mu, n_row * nu), weights[0].dtype),
            jax.ShapeDtypeStruct((aux, aux * 128), jnp.float32),
        ),
        in_specs=[VMEM] * (1 + n_row + n_plane),
        out_specs=(VMEM, VMEM),
        compiler_params=pltpu.CompilerParams(vmem_limit_bytes=ROOM),
        cost_estimate=pl.CostEstimate(
            flops=2 * aux * mu * mu * nu * n_plane, bytes_accessed=4 * n_plane * aux * mu * nu, transcendentals=0
        ),
        name="polar_share",
    )(half_block, *weights, *bundles)


def dress_kernel(n_plane, total_ao, weight_ref, *refs):
    halves, shares = refs[:n_plane], refs[n_plane : n_plane + 2]
    out_ref, polar_ref = refs[n_plane + 2 :]
    mu, aux, nu = out_ref.shape
    plane = plane_index()
    for q in range(aux):
        total = jnp.zeros((mu, nu), jnp.float32)
        for k in range(n_plane):
            total += jnp.dot(
                weight_ref[:, pl.ds(pl.multiple_of((plane ^ k) * mu, mu), mu)],
                halves[k][:, q * nu : (q + 1) * nu],
                preferred_element_type=jnp.float32,
            )
        out_ref[:, q, :] = total.astype(out_ref.dtype)
        lanes = pl.ds(q * 128, 128)
        share = shares[0][:, lanes] + shares[1][:, lanes]
        polar_ref[:, q : q + 1] = jnp.sum(share, axis=1, keepdims=True) / total_ao


def dress(weight, halves, shares, total_ao):
    mu, width = halves[0].shape
    aux, n_plane = shares[0].shape[0], len(halves)
    return pl.pallas_call(
        functools.partial(dress_kernel, n_plane, total_ao),
        out_shape=(
            jax.ShapeDtypeStruct((mu, aux, width // aux), weight.dtype),
            jax.ShapeDtypeStruct((aux, aux), jnp.float32),
        ),
        in_specs=[VMEM] * (n_plane + 3),
        out_specs=(VMEM, VMEM),
        compiler_params=pltpu.CompilerParams(vmem_limit_bytes=ROOM),
        cost_estimate=pl.CostEstimate(
            flops=2 * mu * mu * width * n_plane, bytes_accessed=4 * n_plane * mu * width, transcendentals=0
        ),
        name="dress",
    )(weight, *halves, *shares)


def on_device(tensor_tiles, tile_pairs, tile_counts, occupied, virtual):
    aux = tensor_tiles.shape[1]
    nu = virtual.shape[1]
    n_row, n_plane = lax.axis_size("row"), lax.axis_size("col") * lax.axis_size("rep")
    near = list(range(2, n_plane, 2))
    sibling = lambda value: flip(value, PLANE, 1, n_plane)

    line, bundle = place(tile_pairs, tile_counts, tensor_tiles, occupied, virtual)
    lines = gather_row(line, n_row)
    bundles = []
    for value in [bundle] + [flip(bundle, PLANE, k, n_plane) for k in near]:
        bundles += [value, sibling(value)]
    own = half(lines, bundles)

    direct = [k for k in near if k & (k - 1) == 0]
    arrivals = {k: flip(own, PLANE, k, n_plane) for k in direct}
    weight, share = share_of(own, lines, bundles)
    share = sum([flip(share, PLANE, k, n_plane) for k in near], share)
    (share, own), found = after((share, own), [arrivals[k] for k in direct])
    halves = {0: own, **dict(zip(direct, found))}
    rest = [k for k in near if k not in halves]
    arrivals = [flip(own, PLANE, k, n_plane) for k in rest]
    step = 1
    while step < n_row:
        share = share + flip(share, "row", step, n_row)
        step *= 2
    share, found = after(share, arrivals)
    halves.update(zip(rest, found))
    shares = (share, sibling(share))
    halves.update({k ^ 1: sibling(halves[k]) for k in [0] + near})
    dressed, polar = dress(weight, [halves[k] for k in range(n_plane)], shares, n_row * nu)
    return polar, dressed


def solution(mesh):
    return jax.shard_map(
        on_device,
        mesh=mesh,
        in_specs=(P(EVERY, None, None, None), P(EVERY), P(EVERY), P(PLANE, "row"), P(PLANE, "row")),
        out_specs=(P(), P(PLANE, None, "row")),
        check_vma=False,
    )
```

```python
import functools

import jax
import jax.numpy as jnp
from jax import lax
from jax.experimental import pallas as pl
from jax.experimental.pallas import tpu as pltpu
from jax.sharding import PartitionSpec as P

PLANE = ("col", "rep")
EVERY = ("row", "col", "rep")
VMEM = pl.BlockSpec(memory_space=pltpu.VMEM)
SMEM = pl.BlockSpec(memory_space=pltpu.SMEM)
ROOM = 48 << 20


def flip(value, axes, mask, count):
    return lax.ppermute(value, axes, [(i, i ^ mask) for i in range(count)])


def after(value, earlier):
    return lax.optimization_barrier((value, earlier))


def gather_row(value, n_row, beside):
    found = {0: value}
    step = n_row // 2
    while step > 1:
        found.update({k ^ step: flip(held, "row", step, n_row) for k, held in list(found.items())})
        step //= 2
    found[1] = flip(value, "row", 1, n_row)
    found, beside = after(found, beside)
    found.update({k ^ 1: flip(held, "row", 1, n_row) for k, held in list(found.items()) if k > 1})
    return [found[k] for k in range(n_row)], beside


def plane_index():
    return lax.axis_index("col") * lax.axis_size("rep") + lax.axis_index("rep")


def place_kernel(nu_tiles, counts_ref, pairs_any, tiles_any, block_ref, pairs_ref, tiles_ref, sems):
    slots, aux, tile, _ = tiles_ref.shape
    copies = [
        pltpu.make_async_copy(source, target, sems.at[i])
        for i, (source, target) in enumerate([(tiles_any, tiles_ref), (pairs_any, pairs_ref)])
    ]
    for copy in copies:
        copy.start()
    for copy in copies:
        copy.wait()
    for t in range(slots):
        pair = pairs_ref[t]
        rows = pl.ds(pl.multiple_of(pair // nu_tiles * tile, tile), tile)
        cols = pl.ds(pl.multiple_of(pair % nu_tiles * tile, tile), tile)

        @pl.when(t < counts_ref[0])
        def _():
            block_ref[:, rows, cols] = tiles_ref[t]

        @pl.when(t >= counts_ref[0])
        def _():
            block_ref[:, rows, cols] = jnp.zeros((aux, tile, tile), block_ref.dtype)


def place(tile_pairs, tile_counts, tensor_tiles, mu, nu):
    _, aux, tile, _ = tensor_tiles.shape
    stays = [pltpu.with_memory_space_constraint(value, pltpu.HBM) for value in (tile_pairs, tensor_tiles)]
    return pl.pallas_call(
        functools.partial(place_kernel, nu // tile),
        out_shape=jax.ShapeDtypeStruct((aux, mu, nu), tensor_tiles.dtype),
        in_specs=[SMEM] + [pl.BlockSpec(memory_space=pltpu.HBM)] * 2,
        out_specs=VMEM,
        scratch_shapes=[
            pltpu.SMEM(tile_pairs.shape, tile_pairs.dtype),
            pltpu.VMEM(tensor_tiles.shape, tensor_tiles.dtype),
            pltpu.SemaphoreType.DMA((2,)),
        ],
        compiler_params=pltpu.CompilerParams(vmem_limit_bytes=ROOM),
        cost_estimate=pl.CostEstimate(flops=0, bytes_accessed=6 * tensor_tiles.size, transcendentals=0),
        name="place",
    )(tile_counts, *stays)


def half_kernel(n_row, n_plane, *refs):
    lines, columns = refs[:n_row], refs[n_row : n_row + n_plane]
    out_ref, panel = refs[n_row + n_plane :]
    aux, mu, nu = lines[0].shape
    row, plane = lax.axis_index("row"), plane_index()
    for k in range(n_plane):
        panel[pl.ds(pl.multiple_of((plane ^ k) * mu, mu), mu), :] = columns[k][...]
    for p in range(aux):
        total = jnp.zeros((mu, nu), jnp.float32)
        for k in range(n_row):
            at = pl.multiple_of((row ^ k) * nu, nu)
            total += jnp.dot(lines[k][p], panel[pl.ds(at, nu), :], preferred_element_type=jnp.float32)
        out_ref[:, p * nu : (p + 1) * nu] = total.astype(out_ref.dtype)


def half(lines, columns):
    aux, mu, nu = lines[0].shape
    n_row, n_plane = len(lines), len(columns)
    kind = lines[0].dtype
    return pl.pallas_call(
        functools.partial(half_kernel, n_row, n_plane),
        out_shape=jax.ShapeDtypeStruct((mu, aux * nu), kind),
        in_specs=[VMEM] * (n_row + n_plane),
        out_specs=VMEM,
        scratch_shapes=[pltpu.VMEM((n_plane * mu, nu), kind)],
        compiler_params=pltpu.CompilerParams(vmem_limit_bytes=ROOM),
        cost_estimate=pl.CostEstimate(
            flops=2 * aux * mu * nu * nu * n_row, bytes_accessed=4 * n_row * aux * mu * nu, transcendentals=0
        ),
        name="half_product",
    )(*lines, *columns)


def dress_kernel(n_row, n_plane, n_all, total_ao, *refs):
    weights, halves, (block_ref,) = refs[:n_row], refs[n_row : n_row + n_plane], refs[n_row + n_plane : n_row + n_plane + 1]
    out_ref, share_ref, panel = refs[n_row + n_plane + 1 :]
    mu, aux, nu = out_ref.shape
    row, plane = lax.axis_index("row"), plane_index()
    for k in range(n_row):
        panel[:, pl.ds(pl.multiple_of((row ^ k) * nu, nu), nu)] = weights[k][...]
    rows = lax.broadcasted_iota(jnp.int32, share_ref.shape[1:], 0)
    lanes = lax.broadcasted_iota(jnp.int32, share_ref.shape[1:], 1)
    share = jnp.zeros(share_ref.shape[1:], jnp.float32)
    for q in range(aux):
        total = jnp.zeros((mu, nu), jnp.float32)
        for k in range(n_plane):
            total += jnp.dot(
                panel[:, pl.ds(pl.multiple_of((plane ^ k) * mu, mu), mu)],
                halves[k][:, q * nu : (q + 1) * nu],
                preferred_element_type=jnp.float32,
            )
        rounded = total.astype(out_ref.dtype)
        out_ref[:, q, :] = rounded
        wide = rounded.astype(jnp.float32)
        for p in range(aux):
            product = block_ref[p].astype(jnp.float32) * wide
            folded = jnp.sum(product.reshape(mu // 8, 8, nu), axis=0)
            own = jnp.sum(jnp.sum(folded, axis=0, keepdims=True), axis=1, keepdims=True) / total_ao
            share = jnp.where((rows == p) & (lanes == q), own, share)
    for i in range(n_all):
        share_ref[i] = share


def dress(weights, halves, block, n_all, total_ao):
    aux, mu, nu = block.shape
    n_row, n_plane = len(weights), len(halves)
    return pl.pallas_call(
        functools.partial(dress_kernel, n_row, n_plane, n_all, total_ao),
        out_shape=(
            jax.ShapeDtypeStruct((mu, aux, nu), block.dtype),
            jax.ShapeDtypeStruct((n_all, 8, 128), jnp.float32),
        ),
        in_specs=[VMEM] * (n_row + n_plane + 1),
        out_specs=(VMEM, VMEM),
        scratch_shapes=[pltpu.VMEM((mu, n_row * nu), block.dtype)],
        compiler_params=pltpu.CompilerParams(vmem_limit_bytes=ROOM),
        cost_estimate=pl.CostEstimate(
            flops=2 * aux * mu * mu * nu * n_plane, bytes_accessed=4 * n_plane * aux * mu * nu, transcendentals=0
        ),
        name="dress",
    )(*weights, *halves, block)


def finish_kernel(shares_ref, out_ref):
    aux = out_ref.shape[0]
    out_ref[...] = jnp.sum(shares_ref[...], axis=0)[:aux, :aux]


def finish(shares, aux):
    return pl.pallas_call(
        finish_kernel,
        out_shape=jax.ShapeDtypeStruct((aux, aux), jnp.float32),
        in_specs=[VMEM],
        out_specs=VMEM,
        compiler_params=pltpu.CompilerParams(vmem_limit_bytes=ROOM),
        name="finish",
    )(shares)


def on_device(tensor_tiles, tile_pairs, tile_counts, occupied, virtual):
    aux = tensor_tiles.shape[1]
    mu, nu = virtual.shape
    n_row, n_plane = lax.axis_size("row"), lax.axis_size("col") * lax.axis_size("rep")
    near = list(range(2, n_plane, 2))
    sibling = lambda value: flip(value, PLANE, 1, n_plane)

    block = place(tile_pairs, tile_counts, tensor_tiles, mu, nu)
    columns = [virtual] + [flip(virtual, PLANE, k, n_plane) for k in range(1, n_plane)]
    lines, columns = gather_row(block, n_row, columns)
    own = half(lines, columns)
    arrivals = [flip(own, PLANE, k, n_plane) for k in near]
    occupied, own = after(occupied, own)
    weights, _ = gather_row(occupied, n_row, [])
    weights, arrivals = after(weights, arrivals)
    halves = []
    for value in [own] + arrivals:
        halves += [value, sibling(value)]
    dressed, shares = dress(weights, halves, block, n_row * n_plane, n_row * nu)
    polar = finish(lax.all_to_all(shares, EVERY, 0, 0), aux)
    return polar, dressed


def solution(mesh):
    return jax.shard_map(
        on_device,
        mesh=mesh,
        in_specs=(P(EVERY, None, None, None), P(EVERY), P(EVERY), P(PLANE, "row"), P(PLANE, "row")),
        out_specs=(P(), P(PLANE, None, "row")),
        check_vma=False,
    )
```

```python
import functools

import jax
import jax.numpy as jnp
from jax import lax
from jax.experimental import pallas as pl
from jax.experimental.pallas import tpu as pltpu
from jax.sharding import PartitionSpec as P

PLANE = ("col", "rep")
EVERY = ("row", "col", "rep")
VMEM = pl.BlockSpec(memory_space=pltpu.VMEM)
SMEM = pl.BlockSpec(memory_space=pltpu.SMEM)
ROOM = 48 << 20


def flip(value, axes, mask, count):
    return lax.ppermute(value, axes, [(i, i ^ mask) for i in range(count)])


def after(value, earlier):
    return lax.optimization_barrier((value, earlier))


def gather_row(value, n_row):
    found = {0: value}
    step = n_row // 2
    while step:
        found.update({k ^ step: flip(held, "row", step, n_row) for k, held in list(found.items())})
        step //= 2
    return [found[k] for k in range(n_row)]


def plane_index():
    return lax.axis_index("col") * lax.axis_size("rep") + lax.axis_index("rep")


def place_kernel(nu_tiles, counts_ref, pairs_any, tiles_any, weight_any, column_any, *refs):
    line_ref, bundle_ref, pairs_ref, tiles_ref, sems = refs
    slots, aux, tile, _ = tiles_ref.shape
    copies = [
        pltpu.make_async_copy(source, target, sems.at[i])
        for i, (source, target) in enumerate(
            [
                (tiles_any, tiles_ref),
                (pairs_any, pairs_ref),
                (weight_any, line_ref.at[aux]),
                (column_any, bundle_ref.at[aux]),
            ]
        )
    ]
    for copy in copies:
        copy.start()
    for copy in copies:
        copy.wait()
    for t in range(slots):
        pair = pairs_ref[t]
        rows = pl.ds(pl.multiple_of(pair // nu_tiles * tile, tile), tile)
        cols = pl.ds(pl.multiple_of(pair % nu_tiles * tile, tile), tile)

        @pl.when(t < counts_ref[0])
        def _():
            for out_ref in (line_ref, bundle_ref):
                out_ref[:aux, rows, cols] = tiles_ref[t]

        @pl.when(t >= counts_ref[0])
        def _():
            for out_ref in (line_ref, bundle_ref):
                out_ref[:aux, rows, cols] = jnp.zeros((aux, tile, tile), out_ref.dtype)


def place(tile_pairs, tile_counts, tensor_tiles, weight, column):
    slots, aux, tile, _ = tensor_tiles.shape
    mu, nu = weight.shape
    shape = jax.ShapeDtypeStruct((aux + 1, mu, nu), weight.dtype)
    stays = [pltpu.with_memory_space_constraint(value, pltpu.HBM) for value in (tile_pairs, tensor_tiles, weight, column)]
    return pl.pallas_call(
        functools.partial(place_kernel, nu // tile),
        out_shape=(shape, shape),
        in_specs=[SMEM] + [pl.BlockSpec(memory_space=pltpu.HBM)] * 4,
        out_specs=(VMEM, VMEM),
        scratch_shapes=[
            pltpu.SMEM(tile_pairs.shape, tile_pairs.dtype),
            pltpu.VMEM(tensor_tiles.shape, tensor_tiles.dtype),
            pltpu.SemaphoreType.DMA((4,)),
        ],
        compiler_params=pltpu.CompilerParams(vmem_limit_bytes=ROOM),
        cost_estimate=pl.CostEstimate(flops=0, bytes_accessed=6 * tensor_tiles.size, transcendentals=0),
        name="place",
    )(tile_counts, *stays)


def half_kernel(n_row, n_plane, *refs):
    lines, bundles = refs[:n_row], refs[n_row : n_row + n_plane]
    out_ref, panel = refs[n_row + n_plane :]
    planes, mu, nu = lines[0].shape
    aux = planes - 1
    row, plane = lax.axis_index("row"), plane_index()
    for k in range(n_plane):
        panel[pl.ds(pl.multiple_of((plane ^ k) * mu, mu), mu), :] = bundles[k][aux]
    for p in range(aux):
        total = jnp.zeros((mu, nu), jnp.float32)
        for k in range(n_row):
            at = pl.multiple_of((row ^ k) * nu, nu)
            total += jnp.dot(lines[k][p], panel[pl.ds(at, nu), :], preferred_element_type=jnp.float32)
        out_ref[:, p * nu : (p + 1) * nu] = total.astype(out_ref.dtype)


def half(lines, bundles):
    planes, mu, nu = lines[0].shape
    aux = planes - 1
    n_row, n_plane = len(lines), len(bundles)
    kind = lines[0].dtype
    return pl.pallas_call(
        functools.partial(half_kernel, n_row, n_plane),
        out_shape=jax.ShapeDtypeStruct((mu, aux * nu), kind),
        in_specs=[VMEM] * (n_row + n_plane),
        out_specs=VMEM,
        scratch_shapes=[pltpu.VMEM((n_plane * mu, nu), kind)],
        compiler_params=pltpu.CompilerParams(vmem_limit_bytes=ROOM),
        cost_estimate=pl.CostEstimate(
            flops=2 * aux * mu * nu * nu * n_row, bytes_accessed=4 * n_row * aux * mu * nu, transcendentals=0
        ),
        name="half_product",
    )(*lines, *bundles)


def share_kernel(n_row, n_plane, half_ref, *refs):
    weights, bundles = refs[:n_row], refs[n_row : n_row + n_plane]
    weight_ref, share_ref = refs[n_row + n_plane :]
    planes, mu, nu = weights[0].shape
    aux = planes - 1
    row, plane = lax.axis_index("row"), plane_index()
    rows = lax.broadcasted_iota(jnp.int32, share_ref.shape[1:], 0)
    lanes = lax.broadcasted_iota(jnp.int32, share_ref.shape[1:], 1)
    share = jnp.zeros(share_ref.shape[1:], jnp.float32)
    for k in range(n_row):
        weight_ref[:, pl.ds(pl.multiple_of((row ^ k) * nu, nu), nu)] = weights[k][weights[k].shape[0] - 1]
    for p in range(aux):
        mixed = jnp.zeros((mu, nu), jnp.float32)
        for k in range(n_plane):
            at = pl.multiple_of((plane ^ k) * mu, mu)
            mixed += jnp.dot(weight_ref[:, pl.ds(at, mu)], bundles[k][p], preferred_element_type=jnp.float32)
        for q in range(aux):
            product = mixed * half_ref[:, q * nu : (q + 1) * nu].astype(jnp.float32)
            folded = jnp.sum(product.reshape(mu // 8, 8, nu), axis=0)
            own = jnp.sum(jnp.sum(folded, axis=0, keepdims=True), axis=1, keepdims=True)
            share = jnp.where((rows == p) & (lanes == q), own, share)
    for i in range(n_plane):
        share_ref[i] = share


def share_of(half_block, weights, bundles):
    planes, mu, nu = weights[0].shape
    aux, n_row, n_plane = planes - 1, len(weights), len(bundles)
    return pl.pallas_call(
        functools.partial(share_kernel, n_row, n_plane),
        out_shape=(
            jax.ShapeDtypeStruct((mu, n_row * nu), weights[0].dtype),
            jax.ShapeDtypeStruct((n_plane, 8, 128), jnp.float32),
        ),
        in_specs=[VMEM] * (1 + n_row + n_plane),
        out_specs=(VMEM, VMEM),
        compiler_params=pltpu.CompilerParams(vmem_limit_bytes=ROOM),
        cost_estimate=pl.CostEstimate(
            flops=2 * aux * mu * mu * nu * n_plane, bytes_accessed=4 * n_plane * aux * mu * nu, transcendentals=0
        ),
        name="polar_share",
    )(half_block, *weights, *bundles)


def dress_kernel(n_plane, total_ao, weight_ref, *refs):
    halves, (shares_ref, out_ref, polar_ref) = refs[:n_plane], refs[n_plane:]
    mu, aux, nu = out_ref.shape
    plane = plane_index()
    for q in range(aux):
        total = jnp.zeros((mu, nu), jnp.float32)
        for k in range(n_plane):
            total += jnp.dot(
                weight_ref[:, pl.ds(pl.multiple_of((plane ^ k) * mu, mu), mu)],
                halves[k][:, q * nu : (q + 1) * nu],
                preferred_element_type=jnp.float32,
            )
        out_ref[:, q, :] = total.astype(out_ref.dtype)
    polar_ref[...] = jnp.sum(shares_ref[...], axis=0)[:aux, :aux] / total_ao


def dress(weight, halves, shares, aux, total_ao):
    mu, width = halves[0].shape
    n_plane = len(halves)
    return pl.pallas_call(
        functools.partial(dress_kernel, n_plane, total_ao),
        out_shape=(
            jax.ShapeDtypeStruct((mu, aux, width // aux), weight.dtype),
            jax.ShapeDtypeStruct((aux, aux), jnp.float32),
        ),
        in_specs=[VMEM] * (n_plane + 2),
        out_specs=(VMEM, VMEM),
        compiler_params=pltpu.CompilerParams(vmem_limit_bytes=ROOM),
        cost_estimate=pl.CostEstimate(
            flops=2 * mu * mu * width * n_plane, bytes_accessed=4 * n_plane * mu * width, transcendentals=0
        ),
        name="dress",
    )(weight, *halves, shares)


def on_device(tensor_tiles, tile_pairs, tile_counts, occupied, virtual):
    aux = tensor_tiles.shape[1]
    nu = virtual.shape[1]
    n_row, n_plane = lax.axis_size("row"), lax.axis_size("col") * lax.axis_size("rep")
    near = list(range(2, n_plane, 2))
    sibling = lambda value: flip(value, PLANE, 1, n_plane)

    line, bundle = place(tile_pairs, tile_counts, tensor_tiles, occupied, virtual)
    lines = gather_row(line, n_row)
    bundles = []
    for value in [bundle] + [flip(bundle, PLANE, k, n_plane) for k in near]:
        bundles += [value, sibling(value)]
    own = half(lines, bundles)

    direct = [k for k in near if k & (k - 1) == 0]
    arrivals = {k: flip(own, PLANE, k, n_plane) for k in direct}
    weight, share = share_of(own, lines, bundles)
    share = jnp.sum(lax.all_to_all(share, PLANE, 0, 0), axis=0)
    (share, own), found = after((share, own), [arrivals[k] for k in direct])
    halves = {0: own, **dict(zip(direct, found))}
    rest = [k for k in near if k not in halves]
    arrivals = [flip(own, PLANE, k, n_plane) for k in rest]
    shares = lax.all_to_all(jnp.broadcast_to(share, (n_row, *share.shape)), "row", 0, 0)
    shares, found = after(shares, arrivals)
    halves.update(zip(rest, found))
    halves.update({k ^ 1: sibling(halves[k]) for k in [0] + near})
    dressed, polar = dress(weight, [halves[k] for k in range(n_plane)], shares, aux, n_row * nu)
    return polar, dressed


def solution(mesh):
    return jax.shard_map(
        on_device,
        mesh=mesh,
        in_specs=(P(EVERY, None, None, None), P(EVERY), P(EVERY), P(PLANE, "row"), P(PLANE, "row")),
        out_specs=(P(), P(PLANE, None, "row")),
        check_vma=False,
    )
```

```python
import functools

import jax
import jax.numpy as jnp
from jax import lax
from jax.experimental import pallas as pl
from jax.experimental.pallas import tpu as pltpu
from jax.sharding import PartitionSpec as P

PLANE = ("col", "rep")
EVERY = ("row", "col", "rep")
VMEM = pl.BlockSpec(memory_space=pltpu.VMEM)
SMEM = pl.BlockSpec(memory_space=pltpu.SMEM)
ROOM = 48 << 20


def flip(value, axes, mask, count):
    return lax.ppermute(value, axes, [(i, i ^ mask) for i in range(count)])


def after(value, earlier):
    return lax.optimization_barrier((value, earlier))


def gather_row(value, n_row):
    found = {0: value}
    step = n_row // 2
    while step:
        found.update({k ^ step: flip(held, "row", step, n_row) for k, held in list(found.items())})
        step //= 2
    return [found[k] for k in range(n_row)]


def others(value, n_plane):
    near = list(range(2, n_plane, 2))
    total = 0.0
    for even, odd in zip(near[::2], near[1::2] + [0]):
        pairs = [(i, i ^ even) for i in range(0, n_plane, 2)]
        pairs += [(i, i ^ odd) for i in range(1, n_plane, 2) if odd]
        total = total + lax.ppermute(value, PLANE, pairs)
    return total


def plane_index():
    return lax.axis_index("col") * lax.axis_size("rep") + lax.axis_index("rep")


def place_kernel(nu_tiles, counts_ref, pairs_any, tiles_any, weight_any, column_any, *refs):
    line_ref, bundle_ref, pairs_ref, tiles_ref, sems = refs
    slots, aux, tile, _ = tiles_ref.shape
    copies = [
        pltpu.make_async_copy(source, target, sems.at[i])
        for i, (source, target) in enumerate(
            [
                (tiles_any, tiles_ref),
                (pairs_any, pairs_ref),
                (weight_any, line_ref.at[aux]),
                (column_any, bundle_ref.at[aux]),
            ]
        )
    ]
    for copy in copies:
        copy.start()
    for copy in copies:
        copy.wait()
    for t in range(slots):
        pair = pairs_ref[t]
        rows = pl.ds(pl.multiple_of(pair // nu_tiles * tile, tile), tile)
        cols = pl.ds(pl.multiple_of(pair % nu_tiles * tile, tile), tile)

        @pl.when(t < counts_ref[0])
        def _():
            for out_ref in (line_ref, bundle_ref):
                out_ref[:aux, rows, cols] = tiles_ref[t]

        @pl.when(t >= counts_ref[0])
        def _():
            for out_ref in (line_ref, bundle_ref):
                out_ref[:aux, rows, cols] = jnp.zeros((aux, tile, tile), out_ref.dtype)


def place(tile_pairs, tile_counts, tensor_tiles, weight, column):
    slots, aux, tile, _ = tensor_tiles.shape
    mu, nu = weight.shape
    shape = jax.ShapeDtypeStruct((aux + 1, mu, nu), weight.dtype)
    stays = [pltpu.with_memory_space_constraint(value, pltpu.HBM) for value in (tile_pairs, tensor_tiles, weight, column)]
    return pl.pallas_call(
        functools.partial(place_kernel, nu // tile),
        out_shape=(shape, shape),
        in_specs=[SMEM] + [pl.BlockSpec(memory_space=pltpu.HBM)] * 4,
        out_specs=(VMEM, VMEM),
        scratch_shapes=[
            pltpu.SMEM(tile_pairs.shape, tile_pairs.dtype),
            pltpu.VMEM(tensor_tiles.shape, tensor_tiles.dtype),
            pltpu.SemaphoreType.DMA((4,)),
        ],
        compiler_params=pltpu.CompilerParams(vmem_limit_bytes=ROOM),
        cost_estimate=pl.CostEstimate(flops=0, bytes_accessed=6 * tensor_tiles.size, transcendentals=0),
        name="place",
    )(tile_counts, *stays)


def half_kernel(n_row, n_plane, *refs):
    lines, bundles = refs[:n_row], refs[n_row : n_row + n_plane]
    out_ref, panel = refs[n_row + n_plane :]
    planes, mu, nu = lines[0].shape
    aux = planes - 1
    row, plane = lax.axis_index("row"), plane_index()
    for k in range(n_plane):
        panel[pl.ds(pl.multiple_of((plane ^ k) * mu, mu), mu), :] = bundles[k][aux]
    for p in range(aux):
        total = jnp.zeros((mu, nu), jnp.float32)
        for k in range(n_row):
            at = pl.multiple_of((row ^ k) * nu, nu)
            total += jnp.dot(lines[k][p], panel[pl.ds(at, nu), :], preferred_element_type=jnp.float32)
        out_ref[:, p * nu : (p + 1) * nu] = total.astype(out_ref.dtype)


def half(lines, bundles):
    planes, mu, nu = lines[0].shape
    aux = planes - 1
    n_row, n_plane = len(lines), len(bundles)
    kind = lines[0].dtype
    return pl.pallas_call(
        functools.partial(half_kernel, n_row, n_plane),
        out_shape=jax.ShapeDtypeStruct((mu, aux * nu), kind),
        in_specs=[VMEM] * (n_row + n_plane),
        out_specs=VMEM,
        scratch_shapes=[pltpu.VMEM((n_plane * mu, nu), kind)],
        compiler_params=pltpu.CompilerParams(vmem_limit_bytes=ROOM),
        cost_estimate=pl.CostEstimate(
            flops=2 * aux * mu * nu * nu * n_row, bytes_accessed=4 * n_row * aux * mu * nu, transcendentals=0
        ),
        name="half_product",
    )(*lines, *bundles)


def share_kernel(n_row, n_plane, half_ref, *refs):
    weights, bundles = refs[:n_row], refs[n_row : n_row + n_plane]
    weight_ref, share_ref = refs[n_row + n_plane :]
    planes, mu, nu = weights[0].shape
    aux = planes - 1
    row, plane = lax.axis_index("row"), plane_index()
    for k in range(n_row):
        weight_ref[:, pl.ds(pl.multiple_of((row ^ k) * nu, nu), nu)] = weights[k][weights[k].shape[0] - 1]
    for p in range(aux):
        mixed = jnp.zeros((mu, nu), jnp.float32)
        for k in range(n_plane):
            at = pl.multiple_of((plane ^ k) * mu, mu)
            mixed += jnp.dot(weight_ref[:, pl.ds(at, mu)], bundles[k][p], preferred_element_type=jnp.float32)
        for q in range(aux):
            product = mixed * half_ref[:, q * nu : (q + 1) * nu].astype(jnp.float32)
            lanes = jnp.sum(product.reshape(mu // 8, 8, nu), axis=0)
            folded = sum([lanes[:, i : i + 128] for i in range(128, nu, 128)], lanes[:, :128])
            share_ref[p : p + 1, q * 128 : (q + 1) * 128] = jnp.sum(folded, axis=0, keepdims=True)


def share_of(half_block, weights, bundles):
    planes, mu, nu = weights[0].shape
    aux, n_row, n_plane = planes - 1, len(weights), len(bundles)
    return pl.pallas_call(
        functools.partial(share_kernel, n_row, n_plane),
        out_shape=(
            jax.ShapeDtypeStruct((mu, n_row * nu), weights[0].dtype),
            jax.ShapeDtypeStruct((aux, aux * 128), jnp.float32),
        ),
        in_specs=[VMEM] * (1 + n_row + n_plane),
        out_specs=(VMEM, VMEM),
        compiler_params=pltpu.CompilerParams(vmem_limit_bytes=ROOM),
        cost_estimate=pl.CostEstimate(
            flops=2 * aux * mu * mu * nu * n_plane, bytes_accessed=4 * n_plane * aux * mu * nu, transcendentals=0
        ),
        name="polar_share",
    )(half_block, *weights, *bundles)


def dress_kernel(n_plane, total_ao, weight_ref, *refs):
    halves, shares = refs[:n_plane], refs[n_plane:-2]
    out_ref, polar_ref = refs[-2:]
    mu, aux, nu = out_ref.shape
    plane = plane_index()
    for q in range(aux):
        total = jnp.zeros((mu, nu), jnp.float32)
        for k in range(n_plane):
            total += jnp.dot(
                weight_ref[:, pl.ds(pl.multiple_of((plane ^ k) * mu, mu), mu)],
                halves[k][:, q * nu : (q + 1) * nu],
                preferred_element_type=jnp.float32,
            )
        out_ref[:, q, :] = total.astype(out_ref.dtype)
        lanes = pl.ds(q * 128, 128)
        share = sum([ref[:, lanes] for ref in shares[1:]], shares[0][:, lanes])
        polar_ref[:, q : q + 1] = jnp.sum(share, axis=1, keepdims=True) / total_ao


def dress(weight, halves, shares, total_ao):
    mu, width = halves[0].shape
    aux, n_plane = shares[0].shape[0], len(halves)
    return pl.pallas_call(
        functools.partial(dress_kernel, n_plane, total_ao),
        out_shape=(
            jax.ShapeDtypeStruct((mu, aux, width // aux), weight.dtype),
            jax.ShapeDtypeStruct((aux, aux), jnp.float32),
        ),
        in_specs=[VMEM] * (1 + n_plane + len(shares)),
        out_specs=(VMEM, VMEM),
        compiler_params=pltpu.CompilerParams(vmem_limit_bytes=ROOM),
        cost_estimate=pl.CostEstimate(
            flops=2 * mu * mu * width * n_plane, bytes_accessed=4 * n_plane * mu * width, transcendentals=0
        ),
        name="dress",
    )(weight, *halves, *shares)


def on_device(tensor_tiles, tile_pairs, tile_counts, occupied, virtual):
    aux = tensor_tiles.shape[1]
    nu = virtual.shape[1]
    n_row, n_plane = lax.axis_size("row"), lax.axis_size("col") * lax.axis_size("rep")
    near = list(range(2, n_plane, 2))
    sibling = lambda value: flip(value, PLANE, 1, n_plane)

    line, bundle = place(tile_pairs, tile_counts, tensor_tiles, occupied, virtual)
    lines = gather_row(line, n_row)
    bundles = []
    for value in [bundle] + [flip(bundle, PLANE, k, n_plane) for k in near]:
        bundles += [value, sibling(value)]
    own = half(lines, bundles)

    arrivals = [flip(own, PLANE, k, n_plane) for k in near]
    weight, share = share_of(own, lines, bundles)
    step = 1
    while step < n_row:
        share = share + flip(share, "row", step, n_row)
        step *= 2
    share = share + sibling(share)
    rest, arrivals = after(others(share, n_plane), arrivals)
    halves = []
    for value in [own] + arrivals:
        halves += [value, sibling(value)]
    dressed, polar = dress(weight, halves, (share, rest, sibling(rest)), n_row * nu)
    return polar, dressed


def solution(mesh):
    return jax.shard_map(
        on_device,
        mesh=mesh,
        in_specs=(P(EVERY, None, None, None), P(EVERY), P(EVERY), P(PLANE, "row"), P(PLANE, "row")),
        out_specs=(P(), P(PLANE, None, "row")),
        check_vma=False,
    )
```

```python
import functools

import jax
import jax.numpy as jnp
from jax import lax
from jax.experimental import pallas as pl
from jax.experimental.pallas import tpu as pltpu
from jax.sharding import PartitionSpec as P

PLANE = ("col", "rep")
EVERY = ("row", "col", "rep")
VMEM = pl.BlockSpec(memory_space=pltpu.VMEM)
SMEM = pl.BlockSpec(memory_space=pltpu.SMEM)
ROOM = 48 << 20


def flip(value, axes, mask, count):
    return lax.ppermute(value, axes, [(i, i ^ mask) for i in range(count)])


def after(value, earlier):
    return lax.optimization_barrier((value, earlier))


def gather_row(value, n_row):
    found = {0: value}
    step = n_row // 2
    while step:
        found.update({k ^ step: flip(held, "row", step, n_row) for k, held in list(found.items())})
        step //= 2
    return [found[k] for k in range(n_row)]


def plane_index():
    return lax.axis_index("col") * lax.axis_size("rep") + lax.axis_index("rep")


def place_kernel(nu_tiles, counts_ref, pairs_any, tiles_any, weight_any, column_any, *refs):
    line_ref, bundle_ref, pairs_ref, tiles_ref, sems = refs
    slots, aux, tile, _ = tiles_ref.shape
    cut = line_ref.shape[0] - 1
    copies = [
        pltpu.make_async_copy(source, target, sems.at[i])
        for i, (source, target) in enumerate(
            [
                (tiles_any, tiles_ref),
                (pairs_any, pairs_ref),
                (weight_any, line_ref.at[cut]),
                (column_any, bundle_ref.at[aux - cut]),
            ]
        )
    ]
    for copy in copies:
        copy.start()
    for copy in copies:
        copy.wait()
    for t in range(slots):
        pair = pairs_ref[t]
        rows = pl.ds(pl.multiple_of(pair // nu_tiles * tile, tile), tile)
        cols = pl.ds(pl.multiple_of(pair % nu_tiles * tile, tile), tile)

        @pl.when(t < counts_ref[0])
        def _():
            line_ref[:cut, rows, cols] = tiles_ref[t, :cut]
            bundle_ref[: aux - cut, rows, cols] = tiles_ref[t, cut:]

        @pl.when(t >= counts_ref[0])
        def _():
            line_ref[:cut, rows, cols] = jnp.zeros((cut, tile, tile), line_ref.dtype)
            bundle_ref[: aux - cut, rows, cols] = jnp.zeros((aux - cut, tile, tile), line_ref.dtype)


def place(tile_pairs, tile_counts, tensor_tiles, weight, column):
    slots, aux, tile, _ = tensor_tiles.shape
    mu, nu = weight.shape
    cut = aux // 2
    stays = [
        pltpu.with_memory_space_constraint(value, pltpu.HBM) for value in (tile_pairs, tensor_tiles, weight, column)
    ]
    return pl.pallas_call(
        functools.partial(place_kernel, nu // tile),
        out_shape=[jax.ShapeDtypeStruct((count + 1, mu, nu), weight.dtype) for count in (cut, aux - cut)],
        in_specs=[SMEM] + [pl.BlockSpec(memory_space=pltpu.HBM)] * 4,
        out_specs=[VMEM, VMEM],
        scratch_shapes=[
            pltpu.SMEM(tile_pairs.shape, tile_pairs.dtype),
            pltpu.VMEM(tensor_tiles.shape, tensor_tiles.dtype),
            pltpu.SemaphoreType.DMA((4,)),
        ],
        compiler_params=pltpu.CompilerParams(vmem_limit_bytes=ROOM),
        cost_estimate=pl.CostEstimate(flops=0, bytes_accessed=6 * tensor_tiles.size, transcendentals=0),
        name="place",
    )(tile_counts, *stays)


def dot(left, right):
    return jnp.dot(left, right, preferred_element_type=jnp.float32)


def mix_kernel(n_row, n_plane, *refs):
    lines, bundles = refs[:n_row], refs[n_row : n_row + n_plane]
    half_ref, mixed_ref, weight_ref, panel_ref = refs[n_row + n_plane :]
    planes, mu, nu = lines[0].shape
    cut, rest = planes - 1, bundles[0].shape[0] - 1
    row, plane = lax.axis_index("row"), plane_index()
    for k in range(n_plane):
        panel_ref[pl.ds(pl.multiple_of((plane ^ k) * mu, mu), mu), :] = bundles[k][rest]
    for k in range(n_row):
        weight_ref[:, pl.ds(pl.multiple_of((row ^ k) * nu, nu), nu)] = lines[k][cut]
    for p in range(cut):
        total = jnp.zeros((mu, nu), jnp.float32)
        for k in range(n_row):
            at = pl.multiple_of((row ^ k) * nu, nu)
            total += dot(lines[k][p], panel_ref[pl.ds(at, nu), :])
        half_ref[:, p * nu : (p + 1) * nu] = total.astype(half_ref.dtype)
    for p in range(rest):
        total = jnp.zeros((mu, nu), jnp.float32)
        for k in range(n_plane):
            at = pl.multiple_of((plane ^ k) * mu, mu)
            total += dot(weight_ref[:, pl.ds(at, mu)], bundles[k][p])
        mixed_ref[:, p * nu : (p + 1) * nu] = total.astype(mixed_ref.dtype)


def mix(lines, bundles):
    planes, mu, nu = lines[0].shape
    cut, rest = planes - 1, bundles[0].shape[0] - 1
    n_row, n_plane = len(lines), len(bundles)
    kind = lines[0].dtype
    return pl.pallas_call(
        functools.partial(mix_kernel, n_row, n_plane),
        out_shape=(
            jax.ShapeDtypeStruct((mu, cut * nu), kind),
            jax.ShapeDtypeStruct((mu, rest * nu), kind),
            jax.ShapeDtypeStruct((mu, n_row * nu), kind),
            jax.ShapeDtypeStruct((n_plane * mu, nu), kind),
        ),
        in_specs=[VMEM] * (n_row + n_plane),
        out_specs=[VMEM] * 4,
        compiler_params=pltpu.CompilerParams(vmem_limit_bytes=ROOM),
        cost_estimate=pl.CostEstimate(
            flops=2 * (cut + rest) * mu * nu * nu * n_row,
            bytes_accessed=4 * n_row * (cut + rest) * mu * nu,
            transcendentals=0,
        ),
        name="mix",
    )(*lines, *bundles)


def dress_kernel(n_row, n_plane, n_all, total_ao, weight_ref, panel_ref, line_ref, bundle_ref, *refs):
    halves, mixed = refs[:n_plane], refs[n_plane : n_plane + n_row]
    out_ref, share_ref = refs[n_plane + n_row :]
    mu, aux, nu = out_ref.shape
    cut = line_ref.shape[0] - 1
    row, plane = lax.axis_index("row"), plane_index()
    rows = lax.broadcasted_iota(jnp.int32, share_ref.shape[1:], 0)
    lanes = lax.broadcasted_iota(jnp.int32, share_ref.shape[1:], 1)
    share = jnp.zeros(share_ref.shape[1:], jnp.float32)
    for q in range(aux):
        total = jnp.zeros((mu, nu), jnp.float32)
        if q < cut:
            for k in range(n_plane):
                at = pl.multiple_of((plane ^ k) * mu, mu)
                total += dot(weight_ref[:, pl.ds(at, mu)], halves[k][:, q * nu : (q + 1) * nu])
        else:
            for k in range(n_row):
                at = pl.multiple_of((row ^ k) * nu, nu)
                total += dot(mixed[k][:, (q - cut) * nu : (q - cut + 1) * nu], panel_ref[pl.ds(at, nu), :])
        rounded = total.astype(out_ref.dtype)
        out_ref[:, q, :] = rounded
        wide = rounded.astype(jnp.float32) if q < cut else total
        for p in range(aux):
            block = line_ref[p] if p < cut else bundle_ref[p - cut]
            folded = jnp.sum((block.astype(jnp.float32) * wide).reshape(mu // 8, 8, nu), axis=0)
            own = jnp.sum(jnp.sum(folded, axis=0, keepdims=True), axis=1, keepdims=True) / total_ao
            share = jnp.where((rows == p) & (lanes == q), own, share)
    for i in range(n_all):
        share_ref[i] = share


def dress(weight, panel, line, bundle, halves, mixed, n_all):
    planes, mu, nu = line.shape
    aux = planes - 1 + bundle.shape[0] - 1
    n_row, n_plane = len(mixed), len(halves)
    return pl.pallas_call(
        functools.partial(dress_kernel, n_row, n_plane, n_all, weight.shape[1]),
        out_shape=(
            jax.ShapeDtypeStruct((mu, aux, nu), line.dtype),
            jax.ShapeDtypeStruct((n_all, 8, 128), jnp.float32),
        ),
        in_specs=[VMEM] * (4 + n_plane + n_row),
        out_specs=(VMEM, VMEM),
        compiler_params=pltpu.CompilerParams(vmem_limit_bytes=ROOM),
        cost_estimate=pl.CostEstimate(
            flops=2 * aux * mu * mu * nu * n_plane, bytes_accessed=4 * n_plane * aux * mu * nu, transcendentals=0
        ),
        name="dress",
    )(weight, panel, line, bundle, *halves, *mixed)


def finish_kernel(shares_ref, out_ref):
    aux = out_ref.shape[0]
    out_ref[...] = jnp.sum(shares_ref[...], axis=0)[:aux, :aux]


def finish(shares, aux):
    return pl.pallas_call(
        finish_kernel,
        out_shape=jax.ShapeDtypeStruct((aux, aux), jnp.float32),
        in_specs=[VMEM],
        out_specs=VMEM,
        compiler_params=pltpu.CompilerParams(vmem_limit_bytes=ROOM),
        name="finish",
    )(shares)


def on_device(tensor_tiles, tile_pairs, tile_counts, occupied, virtual):
    aux = tensor_tiles.shape[1]
    n_row, n_plane = lax.axis_size("row"), lax.axis_size("col") * lax.axis_size("rep")
    near = list(range(2, n_plane, 2))
    sibling = lambda value: flip(value, PLANE, 1, n_plane)

    def gather_plane(value):
        values = [value] + [flip(value, PLANE, k, n_plane) for k in near]
        return [held for value in values for held in (value, sibling(value))]

    line, bundle = place(tile_pairs, tile_counts, tensor_tiles, occupied, virtual)
    half, mixed, weight, panel = mix(gather_row(line, n_row), gather_plane(bundle))
    halves, mixed = gather_plane(half), gather_row(mixed, n_row)
    dressed, shares = dress(weight, panel, line, bundle, halves, mixed, n_row * n_plane)
    polar = finish(lax.all_to_all(shares, EVERY, 0, 0), aux)
    return polar, dressed


def solution(mesh):
    return jax.shard_map(
        on_device,
        mesh=mesh,
        in_specs=(P(EVERY, None, None, None), P(EVERY), P(EVERY), P(PLANE, "row"), P(PLANE, "row")),
        out_specs=(P(), P(PLANE, None, "row")),
        check_vma=False,
    )
```

```python
import functools

import jax
import jax.numpy as jnp
from jax import lax
from jax.experimental import pallas as pl
from jax.experimental.pallas import tpu as pltpu
from jax.sharding import PartitionSpec as P

PLANE = ("col", "rep")
EVERY = ("row", "col", "rep")
VMEM = pl.BlockSpec(memory_space=pltpu.VMEM)
SMEM = pl.BlockSpec(memory_space=pltpu.SMEM)
ROOM = 48 << 20


def flip(value, axes, mask, count):
    return lax.ppermute(value, axes, [(i, i ^ mask) for i in range(count)])


def after(value, earlier):
    return lax.optimization_barrier((value, earlier))


def gather_row(value, n_row):
    found = {0: value}
    step = n_row // 2
    while step:
        found.update({k ^ step: flip(held, "row", step, n_row) for k, held in list(found.items())})
        step //= 2
    return [found[k] for k in range(n_row)]


def plane_index():
    return lax.axis_index("col") * lax.axis_size("rep") + lax.axis_index("rep")


def place_kernel(nu_tiles, counts_ref, pairs_any, tiles_any, weight_any, column_any, *refs):
    line_ref, bundle_ref, pairs_ref, tiles_ref, sems = refs
    slots, aux, tile, _ = tiles_ref.shape
    cut = line_ref.shape[0] - 1
    copies = [
        pltpu.make_async_copy(source, target, sems.at[i])
        for i, (source, target) in enumerate(
            [
                (tiles_any, tiles_ref),
                (pairs_any, pairs_ref),
                (weight_any, line_ref.at[cut]),
                (column_any, bundle_ref.at[aux - cut]),
            ]
        )
    ]
    for copy in copies:
        copy.start()
    for copy in copies:
        copy.wait()
    for t in range(slots):
        pair = pairs_ref[t]
        rows = pl.ds(pl.multiple_of(pair // nu_tiles * tile, tile), tile)
        cols = pl.ds(pl.multiple_of(pair % nu_tiles * tile, tile), tile)

        @pl.when(t < counts_ref[0])
        def _():
            line_ref[:cut, rows, cols] = tiles_ref[t, :cut]
            bundle_ref[: aux - cut, rows, cols] = tiles_ref[t, cut:]

        @pl.when(t >= counts_ref[0])
        def _():
            line_ref[:cut, rows, cols] = jnp.zeros((cut, tile, tile), line_ref.dtype)
            bundle_ref[: aux - cut, rows, cols] = jnp.zeros((aux - cut, tile, tile), line_ref.dtype)


def place(tile_pairs, tile_counts, tensor_tiles, weight, column):
    slots, aux, tile, _ = tensor_tiles.shape
    mu, nu = weight.shape
    cut = aux // 2
    stays = [
        pltpu.with_memory_space_constraint(value, pltpu.HBM) for value in (tile_pairs, tensor_tiles, weight, column)
    ]
    return pl.pallas_call(
        functools.partial(place_kernel, nu // tile),
        out_shape=[jax.ShapeDtypeStruct((count + 1, mu, nu), weight.dtype) for count in (cut, aux - cut)],
        in_specs=[SMEM] + [pl.BlockSpec(memory_space=pltpu.HBM)] * 4,
        out_specs=[VMEM, VMEM],
        scratch_shapes=[
            pltpu.SMEM(tile_pairs.shape, tile_pairs.dtype),
            pltpu.VMEM(tensor_tiles.shape, tensor_tiles.dtype),
            pltpu.SemaphoreType.DMA((4,)),
        ],
        compiler_params=pltpu.CompilerParams(vmem_limit_bytes=ROOM),
        cost_estimate=pl.CostEstimate(flops=0, bytes_accessed=6 * tensor_tiles.size, transcendentals=0),
        name="place",
    )(tile_counts, *stays)


def dot(left, right):
    return jnp.dot(left, right, preferred_element_type=jnp.float32)


def mix_kernel(n_row, n_plane, *refs):
    lines, bundles = refs[:n_row], refs[n_row : n_row + n_plane]
    half_ref, mixed_ref, weight_ref, panel_ref = refs[n_row + n_plane :]
    planes, mu, nu = lines[0].shape
    cut, rest = planes - 1, bundles[0].shape[0] - 1
    row, plane = lax.axis_index("row"), plane_index()
    for k in range(n_plane):
        panel_ref[pl.ds(pl.multiple_of((plane ^ k) * mu, mu), mu), :] = bundles[k][rest]
    for k in range(n_row):
        weight_ref[:, pl.ds(pl.multiple_of((row ^ k) * nu, nu), nu)] = lines[k][cut]
    for p in range(cut):
        total = jnp.zeros((mu, nu), jnp.float32)
        for k in range(n_row):
            at = pl.multiple_of((row ^ k) * nu, nu)
            total += dot(lines[k][p], panel_ref[pl.ds(at, nu), :])
        half_ref[:, p * nu : (p + 1) * nu] = total.astype(half_ref.dtype)
    for p in range(rest):
        total = jnp.zeros((mu, nu), jnp.float32)
        for k in range(n_plane):
            at = pl.multiple_of((plane ^ k) * mu, mu)
            total += dot(weight_ref[:, pl.ds(at, mu)], bundles[k][p])
        mixed_ref[:, p * nu : (p + 1) * nu] = total.astype(mixed_ref.dtype)


def mix(lines, bundles):
    planes, mu, nu = lines[0].shape
    cut, rest = planes - 1, bundles[0].shape[0] - 1
    n_row, n_plane = len(lines), len(bundles)
    kind = lines[0].dtype
    return pl.pallas_call(
        functools.partial(mix_kernel, n_row, n_plane),
        out_shape=(
            jax.ShapeDtypeStruct((mu, cut * nu), kind),
            jax.ShapeDtypeStruct((mu, rest * nu), kind),
            jax.ShapeDtypeStruct((mu, n_row * nu), kind),
            jax.ShapeDtypeStruct((n_plane * mu, nu), kind),
        ),
        in_specs=[VMEM] * (n_row + n_plane),
        out_specs=[VMEM] * 4,
        compiler_params=pltpu.CompilerParams(vmem_limit_bytes=ROOM),
        cost_estimate=pl.CostEstimate(
            flops=2 * (cut + rest) * mu * nu * nu * n_row,
            bytes_accessed=4 * n_row * (cut + rest) * mu * nu,
            transcendentals=0,
        ),
        name="mix",
    )(*lines, *bundles)


def dress_kernel(n_row, n_plane, n_all, total_ao, weight_ref, panel_ref, line_ref, bundle_ref, *refs):
    halves, mixed = refs[:n_plane], refs[n_plane : n_plane + n_row]
    out_ref, share_ref = refs[n_plane + n_row :]
    aux, mu, nu = out_ref.shape
    cut = line_ref.shape[0] - 1
    row, plane = lax.axis_index("row"), plane_index()
    rows = lax.broadcasted_iota(jnp.int32, share_ref.shape[1:], 0)
    lanes = lax.broadcasted_iota(jnp.int32, share_ref.shape[1:], 1)
    share = jnp.zeros(share_ref.shape[1:], jnp.float32)
    for q in range(aux):
        total = jnp.zeros((mu, nu), jnp.float32)
        if q < cut:
            for k in range(n_plane):
                at = pl.multiple_of((plane ^ k) * mu, mu)
                total += dot(weight_ref[:, pl.ds(at, mu)], halves[k][:, q * nu : (q + 1) * nu])
        else:
            for k in range(n_row):
                at = pl.multiple_of((row ^ k) * nu, nu)
                total += dot(mixed[k][:, (q - cut) * nu : (q - cut + 1) * nu], panel_ref[pl.ds(at, nu), :])
        rounded = total.astype(out_ref.dtype)
        out_ref[q] = rounded
        wide = rounded.astype(jnp.float32) if q < cut else total
        for p in range(aux):
            block = line_ref[p] if p < cut else bundle_ref[p - cut]
            folded = jnp.sum((block.astype(jnp.float32) * wide).reshape(mu // 8, 8, nu), axis=0)
            own = jnp.sum(jnp.sum(folded, axis=0, keepdims=True), axis=1, keepdims=True) / total_ao
            share = jnp.where((rows == p) & (lanes == q), own, share)
    for i in range(n_all):
        share_ref[i] = share


def dress(weight, panel, line, bundle, halves, mixed, n_all):
    planes, mu, nu = line.shape
    aux = planes - 1 + bundle.shape[0] - 1
    n_row, n_plane = len(mixed), len(halves)
    return pl.pallas_call(
        functools.partial(dress_kernel, n_row, n_plane, n_all, weight.shape[1]),
        out_shape=(
            jax.ShapeDtypeStruct((aux, mu, nu), line.dtype),
            jax.ShapeDtypeStruct((n_all, 8, 128), jnp.float32),
        ),
        in_specs=[VMEM] * (4 + n_plane + n_row),
        out_specs=(VMEM, VMEM),
        compiler_params=pltpu.CompilerParams(vmem_limit_bytes=ROOM),
        cost_estimate=pl.CostEstimate(
            flops=2 * aux * mu * mu * nu * n_plane, bytes_accessed=4 * n_plane * aux * mu * nu, transcendentals=0
        ),
        name="dress",
    )(weight, panel, line, bundle, *halves, *mixed)


def spread_kernel(shares_ref, out_ref):
    total = jnp.sum(shares_ref[...], axis=0)
    for i in range(out_ref.shape[0]):
        out_ref[i] = total


def spread(shares, count):
    return pl.pallas_call(
        spread_kernel,
        out_shape=jax.ShapeDtypeStruct((count, *shares.shape[1:]), jnp.float32),
        in_specs=[VMEM],
        out_specs=VMEM,
        compiler_params=pltpu.CompilerParams(vmem_limit_bytes=ROOM),
        name="spread",
    )(shares)


def finish_kernel(shares_ref, out_ref):
    aux = out_ref.shape[0]
    out_ref[...] = jnp.sum(shares_ref[...], axis=0)[:aux, :aux]


def finish(shares, aux):
    return pl.pallas_call(
        finish_kernel,
        out_shape=jax.ShapeDtypeStruct((aux, aux), jnp.float32),
        in_specs=[VMEM],
        out_specs=VMEM,
        compiler_params=pltpu.CompilerParams(vmem_limit_bytes=ROOM),
        name="finish",
    )(shares)


def on_device(tensor_tiles, tile_pairs, tile_counts, occupied, virtual):
    aux = tensor_tiles.shape[1]
    n_row, n_plane = lax.axis_size("row"), lax.axis_size("col") * lax.axis_size("rep")
    near = list(range(2, n_plane, 2))
    sibling = lambda value: flip(value, PLANE, 1, n_plane)

    def gather_plane(value):
        values = [value] + [flip(value, PLANE, k, n_plane) for k in near]
        return [held for value in values for held in (value, sibling(value))]

    line, bundle = place(tile_pairs, tile_counts, tensor_tiles, occupied, virtual)
    half, mixed, weight, panel = mix(gather_row(line, n_row), gather_plane(bundle))
    halves, mixed = gather_plane(half), gather_row(mixed, n_row)
    dressed, shares = dress(weight, panel, line, bundle, halves, mixed, n_row)
    shares = spread(lax.all_to_all(shares, "row", 0, 0), n_plane)
    polar = finish(lax.all_to_all(shares, PLANE, 0, 0), aux)
    return polar, dressed.transpose(1, 0, 2)


def solution(mesh):
    return jax.shard_map(
        on_device,
        mesh=mesh,
        in_specs=(P(EVERY, None, None, None), P(EVERY), P(EVERY), P(PLANE, "row"), P(PLANE, "row")),
        out_specs=(P(), P(PLANE, None, "row")),
        check_vma=False,
    )
```

```python
import functools

import jax
import jax.numpy as jnp
from jax import lax
from jax.experimental import pallas as pl
from jax.experimental.pallas import tpu as pltpu
from jax.sharding import PartitionSpec as P

PLANE = ("col", "rep")
EVERY = ("row", "col", "rep")
VMEM = pl.BlockSpec(memory_space=pltpu.VMEM)
SMEM = pl.BlockSpec(memory_space=pltpu.SMEM)
ROOM = 48 << 20


def flip(value, axes, mask, count):
    return lax.ppermute(value, axes, [(i, i ^ mask) for i in range(count)])


def after(value, earlier):
    return lax.optimization_barrier((value, earlier))


def gather_row(value, n_row):
    found = {0: value}
    step = n_row // 2
    while step:
        found.update({k ^ step: flip(held, "row", step, n_row) for k, held in list(found.items())})
        step //= 2
    return [found[k] for k in range(n_row)]


def late(n_row):
    return list(range(3, n_row, 2))


def plane_index():
    return lax.axis_index("col") * lax.axis_size("rep") + lax.axis_index("rep")


def place_kernel(nu_tiles, counts_ref, pairs_any, tiles_any, weight_any, column_any, *refs):
    line_ref, bundle_ref, pairs_ref, tiles_ref, sems = refs
    slots, aux, tile, _ = tiles_ref.shape
    cut = line_ref.shape[0] - 1
    copies = [
        pltpu.make_async_copy(source, target, sems.at[i])
        for i, (source, target) in enumerate(
            [
                (tiles_any, tiles_ref),
                (pairs_any, pairs_ref),
                (weight_any, line_ref.at[cut]),
                (column_any, bundle_ref.at[aux - cut]),
            ]
        )
    ]
    for copy in copies:
        copy.start()
    for copy in copies:
        copy.wait()
    for t in range(slots):
        pair = pairs_ref[t]
        rows = pl.ds(pl.multiple_of(pair // nu_tiles * tile, tile), tile)
        cols = pl.ds(pl.multiple_of(pair % nu_tiles * tile, tile), tile)

        @pl.when(t < counts_ref[0])
        def _():
            line_ref[:cut, rows, cols] = tiles_ref[t, :cut]
            bundle_ref[: aux - cut, rows, cols] = tiles_ref[t, cut:]

        @pl.when(t >= counts_ref[0])
        def _():
            line_ref[:cut, rows, cols] = jnp.zeros((cut, tile, tile), line_ref.dtype)
            bundle_ref[: aux - cut, rows, cols] = jnp.zeros((aux - cut, tile, tile), line_ref.dtype)


def place(tile_pairs, tile_counts, tensor_tiles, weight, column):
    slots, aux, tile, _ = tensor_tiles.shape
    mu, nu = weight.shape
    cut = aux // 2
    stays = [
        pltpu.with_memory_space_constraint(value, pltpu.HBM) for value in (tile_pairs, tensor_tiles, weight, column)
    ]
    return pl.pallas_call(
        functools.partial(place_kernel, nu // tile),
        out_shape=[jax.ShapeDtypeStruct((count + 1, mu, nu), weight.dtype) for count in (cut, aux - cut)],
        in_specs=[SMEM] + [pl.BlockSpec(memory_space=pltpu.HBM)] * 4,
        out_specs=[VMEM, VMEM],
        scratch_shapes=[
            pltpu.SMEM(tile_pairs.shape, tile_pairs.dtype),
            pltpu.VMEM(tensor_tiles.shape, tensor_tiles.dtype),
            pltpu.SemaphoreType.DMA((4,)),
        ],
        compiler_params=pltpu.CompilerParams(vmem_limit_bytes=ROOM),
        cost_estimate=pl.CostEstimate(flops=0, bytes_accessed=6 * tensor_tiles.size, transcendentals=0),
        name="place",
    )(tile_counts, *stays)


def dot(left, right):
    return jnp.dot(left, right, preferred_element_type=jnp.float32)


def mix_kernel(n_row, n_plane, *refs):
    lines, bundles = refs[:n_row], refs[n_row : n_row + n_plane]
    half_ref, mixed_ref, both_ref, weight_ref, panel_ref = refs[n_row + n_plane :]
    planes, mu, nu = lines[0].shape
    cut, rest = planes - 1, bundles[0].shape[0] - 1
    row, plane = lax.axis_index("row"), plane_index()
    for k in range(n_plane):
        panel_ref[pl.ds(pl.multiple_of((plane ^ k) * mu, mu), mu), :] = bundles[k][rest]
    for k in range(n_row):
        weight_ref[:, pl.ds(pl.multiple_of((row ^ k) * nu, nu), nu)] = lines[k][cut]
    for p in range(cut):
        total = jnp.zeros((mu, nu), jnp.float32)
        for k in range(n_row):
            at = pl.multiple_of((row ^ k) * nu, nu)
            total += dot(lines[k][p], panel_ref[pl.ds(at, nu), :])
        half_ref[:, p * nu : (p + 1) * nu] = total.astype(half_ref.dtype)
    for p in range(rest):
        total = jnp.zeros((mu, nu), jnp.float32)
        for k in range(n_plane):
            at = pl.multiple_of((plane ^ k) * mu, mu)
            total += dot(weight_ref[:, pl.ds(at, mu)], bundles[k][p])
        mixed_ref[:, p * nu : (p + 1) * nu] = total.astype(mixed_ref.dtype)
        both_ref[:, p * nu : (p + 1) * nu] = total.astype(both_ref.dtype)
        for i, k in enumerate(late(n_row)):
            at = pl.multiple_of((row ^ k) * nu, nu)
            turned = lax.dot_general(
                bundles[0][p], panel_ref[pl.ds(at, nu), :], (((1,), (1,)), ((), ())), preferred_element_type=jnp.float32
            )
            place_at = ((i + 1) * rest + p) * nu
            both_ref[:, place_at : place_at + nu] = turned.astype(both_ref.dtype)


def mix(lines, bundles):
    planes, mu, nu = lines[0].shape
    cut, rest = planes - 1, bundles[0].shape[0] - 1
    n_row, n_plane = len(lines), len(bundles)
    kind = lines[0].dtype
    return pl.pallas_call(
        functools.partial(mix_kernel, n_row, n_plane),
        out_shape=(
            jax.ShapeDtypeStruct((mu, cut * nu), kind),
            jax.ShapeDtypeStruct((mu, rest * nu), kind),
            jax.ShapeDtypeStruct((mu, (1 + len(late(n_row))) * rest * nu), kind),
            jax.ShapeDtypeStruct((mu, n_row * nu), kind),
            jax.ShapeDtypeStruct((n_plane * mu, nu), kind),
        ),
        in_specs=[VMEM] * (n_row + n_plane),
        out_specs=[VMEM] * 5,
        compiler_params=pltpu.CompilerParams(vmem_limit_bytes=ROOM),
        cost_estimate=pl.CostEstimate(
            flops=2 * (cut + rest) * mu * nu * nu * n_row,
            bytes_accessed=4 * n_row * (cut + rest) * mu * nu,
            transcendentals=0,
        ),
        name="mix",
    )(*lines, *bundles)


def share_kernel(n_row, n_plane, weight_ref, panel_ref, line_ref, bundle_ref, near_ref, *refs):
    halves, far = refs[:n_plane], refs[n_plane : n_plane + n_row // 2]
    first_ref, part_ref, share_ref = refs[n_plane + n_row // 2 :]
    cut, mu, nu = first_ref.shape
    rest = part_ref.shape[0]
    aux = cut + rest
    row, plane = lax.axis_index("row"), plane_index()
    known = {2 * i: ref for i, ref in enumerate(far)}
    known[1] = near_ref

    def product(left, right):
        folded = jnp.sum((left.astype(jnp.float32) * right).reshape(mu // 8, 8, nu), axis=0)
        return sum([folded[:, i : i + 128] for i in range(128, nu, 128)], folded[:, :128])

    def store(p, q, value):
        share_ref[p : p + 1, q * 128 : (q + 1) * 128] = jnp.sum(value, axis=0, keepdims=True)

    for q in range(cut):
        total = jnp.zeros((mu, nu), jnp.float32)
        for k in range(n_plane):
            at = pl.multiple_of((plane ^ k) * mu, mu)
            total += dot(weight_ref[:, pl.ds(at, mu)], halves[k][:, q * nu : (q + 1) * nu])
        rounded = total.astype(first_ref.dtype)
        first_ref[q] = rounded
        for p in range(aux):
            value = product(line_ref[p] if p < cut else bundle_ref[p - cut], rounded.astype(jnp.float32))
            store(p, q, value)
            if p >= cut:
                store(q, p, value)
    for q in range(rest):
        total = jnp.zeros((mu, nu), jnp.float32)
        for k, ref in known.items():
            at = pl.multiple_of((row ^ k) * nu, nu)
            total += dot(ref[:, q * nu : (q + 1) * nu], panel_ref[pl.ds(at, nu), :])
        part_ref[q] = total
        for p in range(rest):
            value = product(bundle_ref[p], total)
            for i, k in enumerate(late(n_row)):
                at = ((i + 1) * rest + p) * nu
                other = known[k ^ 1][:, q * nu : (q + 1) * nu]
                value += product(near_ref[:, at : at + nu], other.astype(jnp.float32))
            store(cut + p, cut + q, value)


def share_of(weight, panel, line, bundle, near, halves, far):
    planes, mu, nu = line.shape
    cut, rest = planes - 1, bundle.shape[0] - 1
    n_row, n_plane = 2 * len(far), len(halves)
    return pl.pallas_call(
        functools.partial(share_kernel, n_row, n_plane),
        out_shape=(
            jax.ShapeDtypeStruct((cut, mu, nu), line.dtype),
            jax.ShapeDtypeStruct((rest, mu, nu), jnp.float32),
            jax.ShapeDtypeStruct((cut + rest, (cut + rest) * 128), jnp.float32),
        ),
        in_specs=[VMEM] * (5 + n_plane + len(far)),
        out_specs=[VMEM] * 3,
        compiler_params=pltpu.CompilerParams(vmem_limit_bytes=ROOM),
        cost_estimate=pl.CostEstimate(
            flops=2 * (cut + rest) * mu * mu * nu * n_plane,
            bytes_accessed=4 * n_plane * (cut + rest) * mu * nu,
            transcendentals=0,
        ),
        name="polar_share",
    )(weight, panel, line, bundle, near, *halves, *far)


def dress_kernel(n_row, panel_ref, first_ref, part_ref, *refs):
    blocks, out_ref = refs[:-1], refs[-1]
    cut, _, nu = first_ref.shape
    row = lax.axis_index("row")
    for q in range(cut):
        out_ref[:, q, :] = first_ref[q]
    for q in range(part_ref.shape[0]):
        total = part_ref[q]
        for k, ref in zip(late(n_row), blocks):
            at = pl.multiple_of((row ^ k) * nu, nu)
            total += dot(ref[:, q * nu : (q + 1) * nu], panel_ref[pl.ds(at, nu), :])
        out_ref[:, cut + q, :] = total.astype(out_ref.dtype)


def dress(panel, first, part, blocks, n_row):
    cut, mu, nu = first.shape
    aux = cut + part.shape[0]
    return pl.pallas_call(
        functools.partial(dress_kernel, n_row),
        out_shape=jax.ShapeDtypeStruct((mu, aux, nu), first.dtype),
        in_specs=[VMEM] * (3 + len(blocks)),
        out_specs=VMEM,
        compiler_params=pltpu.CompilerParams(vmem_limit_bytes=ROOM),
        cost_estimate=pl.CostEstimate(flops=2 * mu * nu * nu * aux, bytes_accessed=8 * mu * aux * nu, transcendentals=0),
        name="dress",
    )(panel, first, part, *blocks)


def finish_kernel(total_ao, first_ref, second_ref, out_ref):
    aux = out_ref.shape[0]
    for q in range(aux):
        lanes = pl.ds(q * 128, 128)
        share = first_ref[:, lanes] + second_ref[:, lanes]
        out_ref[:, q : q + 1] = jnp.sum(share, axis=1, keepdims=True) / total_ao


def finish(first, second, total_ao):
    aux = first.shape[0]
    return pl.pallas_call(
        functools.partial(finish_kernel, total_ao),
        out_shape=jax.ShapeDtypeStruct((aux, aux), jnp.float32),
        in_specs=[VMEM, VMEM],
        out_specs=VMEM,
        compiler_params=pltpu.CompilerParams(vmem_limit_bytes=ROOM),
        name="finish",
    )(first, second)


def on_device(tensor_tiles, tile_pairs, tile_counts, occupied, virtual):
    aux = tensor_tiles.shape[1]
    n_row, n_plane = lax.axis_size("row"), lax.axis_size("col") * lax.axis_size("rep")
    near = list(range(2, n_plane, 2))
    sibling = lambda value: flip(value, PLANE, 1, n_plane)

    def gather_plane(value):
        values = [value] + [flip(value, PLANE, k, n_plane) for k in near]
        return [held for value in values for held in (value, sibling(value))]

    line, bundle = place(tile_pairs, tile_counts, tensor_tiles, occupied, virtual)
    half, mixed, both, weight, panel = mix(gather_row(line, n_row), gather_plane(bundle))
    far = {0: mixed}
    step = n_row // 2
    while step > 1:
        far.update({k ^ step: flip(held, "row", step, n_row) for k, held in list(far.items())})
        step //= 2
    beside = flip(both, "row", 1, n_row)
    blocks = [flip(far[k ^ 1], "row", 1, n_row) for k in late(n_row)]
    first, part, share = share_of(
        weight, panel, line, bundle, beside, gather_plane(half), [far[k] for k in range(0, n_row, 2)]
    )
    step = 1
    while step < n_plane:
        share = share + flip(share, PLANE, step, n_plane)
        step *= 2
    step = 1
    while 2 * step < n_row:
        share = share + flip(share, "row", step, n_row)
        step *= 2
    last, dressed = after(flip(share, "row", step, n_row), dress(panel, first, part, blocks, n_row))
    polar = finish(share, last, weight.shape[1])
    return polar, dressed


def solution(mesh):
    return jax.shard_map(
        on_device,
        mesh=mesh,
        in_specs=(P(EVERY, None, None, None), P(EVERY), P(EVERY), P(PLANE, "row"), P(PLANE, "row")),
        out_specs=(P(), P(PLANE, None, "row")),
        check_vma=False,
    )
```

```python
import functools

import jax
import jax.numpy as jnp
from jax import lax
from jax.experimental import pallas as pl
from jax.experimental.pallas import tpu as pltpu
from jax.sharding import PartitionSpec as P

PLANE = ("col", "rep")
EVERY = ("row", "col", "rep")
VMEM = pl.BlockSpec(memory_space=pltpu.VMEM)
SMEM = pl.BlockSpec(memory_space=pltpu.SMEM)
ROOM = 48 << 20


def flip(value, axes, mask, count):
    return lax.ppermute(value, axes, [(i, i ^ mask) for i in range(count)])


def after(value, earlier):
    return lax.optimization_barrier((value, earlier))


def split_kernel(value_ref, block_ref, weight_ref):
    aux = block_ref.shape[0]
    block_ref[...] = value_ref[:aux]
    weight_ref[...] = value_ref[aux:]


def split(value):
    planes, mu, nu = value.shape
    return pl.pallas_call(
        split_kernel,
        out_shape=[jax.ShapeDtypeStruct((count, mu, nu), value.dtype) for count in (planes - 1, 1)],
        in_specs=[VMEM],
        out_specs=[VMEM, VMEM],
        compiler_params=pltpu.CompilerParams(vmem_limit_bytes=ROOM),
        cost_estimate=pl.CostEstimate(flops=0, bytes_accessed=4 * value.size, transcendentals=0),
        name="split",
    )(value)


def gather_row(value, n_row):
    found = {0: value}
    step = n_row // 2
    while step > 1:
        found.update({k ^ step: flip(held, "row", step, n_row) for k, held in list(found.items())})
        step //= 2
    whole = [found.pop(0), flip(value, "row", 1, n_row)]
    pieces = {k: split(held) for k, held in found.items()}
    for k in found:
        pieces[k ^ 1] = [flip(piece, "row", 1, n_row) for piece in pieces[k]]
    return whole, [pieces[k][0] for k in range(2, n_row)], [pieces[k][1] for k in range(2, n_row)]


def plane_index():
    return lax.axis_index("col") * lax.axis_size("rep") + lax.axis_index("rep")


def place_kernel(nu_tiles, counts_ref, pairs_any, tiles_any, weight_any, column_any, *refs):
    line_ref, bundle_ref, pairs_ref, tiles_ref, sems = refs
    slots, aux, tile, _ = tiles_ref.shape
    copies = [
        pltpu.make_async_copy(source, target, sems.at[i])
        for i, (source, target) in enumerate(
            [
                (tiles_any, tiles_ref),
                (pairs_any, pairs_ref),
                (weight_any, line_ref.at[aux]),
                (column_any, bundle_ref.at[aux]),
            ]
        )
    ]
    for copy in copies:
        copy.start()
    for copy in copies:
        copy.wait()
    for t in range(slots):
        pair = pairs_ref[t]
        rows = pl.ds(pl.multiple_of(pair // nu_tiles * tile, tile), tile)
        cols = pl.ds(pl.multiple_of(pair % nu_tiles * tile, tile), tile)

        @pl.when(t < counts_ref[0])
        def _():
            for out_ref in (line_ref, bundle_ref):
                out_ref[:aux, rows, cols] = tiles_ref[t]

        @pl.when(t >= counts_ref[0])
        def _():
            for out_ref in (line_ref, bundle_ref):
                out_ref[:aux, rows, cols] = jnp.zeros((aux, tile, tile), out_ref.dtype)


def place(tile_pairs, tile_counts, tensor_tiles, weight, column):
    slots, aux, tile, _ = tensor_tiles.shape
    mu, nu = weight.shape
    shape = jax.ShapeDtypeStruct((aux + 1, mu, nu), weight.dtype)
    stays = [pltpu.with_memory_space_constraint(value, pltpu.HBM) for value in (tile_pairs, tensor_tiles, weight, column)]
    return pl.pallas_call(
        functools.partial(place_kernel, nu // tile),
        out_shape=(shape, shape),
        in_specs=[SMEM] + [pl.BlockSpec(memory_space=pltpu.HBM)] * 4,
        out_specs=(VMEM, VMEM),
        scratch_shapes=[
            pltpu.SMEM(tile_pairs.shape, tile_pairs.dtype),
            pltpu.VMEM(tensor_tiles.shape, tensor_tiles.dtype),
            pltpu.SemaphoreType.DMA((4,)),
        ],
        compiler_params=pltpu.CompilerParams(vmem_limit_bytes=ROOM),
        cost_estimate=pl.CostEstimate(flops=0, bytes_accessed=6 * tensor_tiles.size, transcendentals=0),
        name="place",
    )(tile_counts, *stays)


def half_kernel(n_row, n_plane, *refs):
    lines, columns = refs[:n_row], refs[n_row : n_row + n_plane]
    out_ref, panel = refs[n_row + n_plane :]
    planes, mu, nu = lines[0].shape
    aux = planes - 1
    row, plane = lax.axis_index("row"), plane_index()
    for k in range(n_plane):
        panel[pl.ds(pl.multiple_of((plane ^ k) * mu, mu), mu), :] = columns[k][columns[k].shape[0] - 1]
    for p in range(aux):
        total = jnp.zeros((mu, nu), jnp.float32)
        for k in range(n_row):
            at = pl.multiple_of((row ^ k) * nu, nu)
            total += jnp.dot(lines[k][p], panel[pl.ds(at, nu), :], preferred_element_type=jnp.float32)
        out_ref[:, p * nu : (p + 1) * nu] = total.astype(out_ref.dtype)


def half(lines, columns):
    planes, mu, nu = lines[0].shape
    aux = planes - 1
    n_row, n_plane = len(lines), len(columns)
    kind = lines[0].dtype
    return pl.pallas_call(
        functools.partial(half_kernel, n_row, n_plane),
        out_shape=jax.ShapeDtypeStruct((mu, aux * nu), kind),
        in_specs=[VMEM] * (n_row + n_plane),
        out_specs=VMEM,
        scratch_shapes=[pltpu.VMEM((n_plane * mu, nu), kind)],
        compiler_params=pltpu.CompilerParams(vmem_limit_bytes=ROOM),
        cost_estimate=pl.CostEstimate(
            flops=2 * aux * mu * nu * nu * n_row, bytes_accessed=4 * n_row * aux * mu * nu, transcendentals=0
        ),
        name="half_product",
    )(*lines, *columns)


def share_kernel(n_row, n_plane, half_ref, *refs):
    weights, bundles = refs[:n_row], refs[n_row : n_row + n_plane]
    weight_ref, share_ref = refs[n_row + n_plane :]
    planes, mu, nu = weights[0].shape
    aux = planes - 1
    row, plane = lax.axis_index("row"), plane_index()
    for k in range(n_row):
        weight_ref[:, pl.ds(pl.multiple_of((row ^ k) * nu, nu), nu)] = weights[k][weights[k].shape[0] - 1]
    for p in range(aux):
        mixed = jnp.zeros((mu, nu), jnp.float32)
        for k in range(n_plane):
            at = pl.multiple_of((plane ^ k) * mu, mu)
            mixed += jnp.dot(weight_ref[:, pl.ds(at, mu)], bundles[k][p], preferred_element_type=jnp.float32)
        for q in range(aux):
            product = mixed * half_ref[:, q * nu : (q + 1) * nu].astype(jnp.float32)
            lanes = jnp.sum(product.reshape(mu // 8, 8, nu), axis=0)
            folded = sum([lanes[:, i : i + 128] for i in range(128, nu, 128)], lanes[:, :128])
            share_ref[p : p + 1, q * 128 : (q + 1) * 128] = jnp.sum(folded, axis=0, keepdims=True)


def share_of(half_block, weights, bundles):
    planes, mu, nu = weights[0].shape
    aux, n_row, n_plane = planes - 1, len(weights), len(bundles)
    return pl.pallas_call(
        functools.partial(share_kernel, n_row, n_plane),
        out_shape=(
            jax.ShapeDtypeStruct((mu, n_row * nu), weights[0].dtype),
            jax.ShapeDtypeStruct((aux, aux * 128), jnp.float32),
        ),
        in_specs=[VMEM] * (1 + n_row + n_plane),
        out_specs=(VMEM, VMEM),
        compiler_params=pltpu.CompilerParams(vmem_limit_bytes=ROOM),
        cost_estimate=pl.CostEstimate(
            flops=2 * aux * mu * mu * nu * n_plane, bytes_accessed=4 * n_plane * aux * mu * nu, transcendentals=0
        ),
        name="polar_share",
    )(half_block, *weights, *bundles)


def dress_kernel(n_plane, weight_ref, *refs):
    halves, out_ref = refs[:n_plane], refs[n_plane]
    mu, aux, nu = out_ref.shape
    plane = plane_index()
    for q in range(aux):
        total = jnp.zeros((mu, nu), jnp.float32)
        for k in range(n_plane):
            at = pl.multiple_of((plane ^ k) * mu, mu)
            total += jnp.dot(
                weight_ref[:, pl.ds(at, mu)],
                halves[k][:, q * nu : (q + 1) * nu],
                preferred_element_type=jnp.float32,
            )
        out_ref[:, q, :] = total.astype(out_ref.dtype)


def dress(weight, halves, aux):
    mu, width = halves[0].shape
    n_plane = len(halves)
    return pl.pallas_call(
        functools.partial(dress_kernel, n_plane),
        out_shape=jax.ShapeDtypeStruct((mu, aux, width // aux), weight.dtype),
        in_specs=[VMEM] * (n_plane + 1),
        out_specs=VMEM,
        compiler_params=pltpu.CompilerParams(vmem_limit_bytes=ROOM),
        cost_estimate=pl.CostEstimate(
            flops=2 * mu * mu * width * n_plane, bytes_accessed=4 * n_plane * mu * width, transcendentals=0
        ),
        name="dress",
    )(weight, *halves)


def finish_kernel(total_ao, first_ref, second_ref, out_ref):
    aux = out_ref.shape[0]
    for q in range(aux):
        lanes = pl.ds(q * 128, 128)
        share = first_ref[:, lanes] + second_ref[:, lanes]
        out_ref[:, q : q + 1] = jnp.sum(share, axis=1, keepdims=True) / total_ao


def finish(first, second, total_ao):
    aux = first.shape[0]
    return pl.pallas_call(
        functools.partial(finish_kernel, total_ao),
        out_shape=jax.ShapeDtypeStruct((aux, aux), jnp.float32),
        in_specs=[VMEM, VMEM],
        out_specs=VMEM,
        compiler_params=pltpu.CompilerParams(vmem_limit_bytes=ROOM),
        name="finish",
    )(first, second)


def on_device(tensor_tiles, tile_pairs, tile_counts, occupied, virtual):
    aux = tensor_tiles.shape[1]
    nu = virtual.shape[1]
    n_row, n_plane = lax.axis_size("row"), lax.axis_size("col") * lax.axis_size("rep")
    near = list(range(2, n_plane, 2))
    sibling = lambda value: flip(value, PLANE, 1, n_plane)

    line, bundle = place(tile_pairs, tile_counts, tensor_tiles, occupied, virtual)
    whole, blocks, weights = gather_row(line, n_row)
    bundles, columns = [], []
    for value in [bundle] + [flip(bundle, PLANE, k, n_plane) for k in near]:
        piece, column = split(value)
        bundles += [value, sibling(piece)]
        columns += [value, sibling(column)]
    own = half(whole + blocks, columns)
    arrivals = [flip(own, PLANE, k, n_plane) for k in near]
    weight, share = share_of(own, whole + weights, bundles)

    step = 1
    while step < n_row:
        share = share + flip(share, "row", step, n_row)
        step *= 2
    step = 1
    while 2 * step < n_plane:
        share = share + flip(share, PLANE, step, n_plane)
        step *= 2
    share, arrivals = after(share, arrivals)
    last = flip(share, PLANE, step, n_plane)
    halves = []
    for value in [own] + arrivals:
        halves += [value, sibling(value)]
    last, dressed = after(last, dress(weight, halves, aux))
    polar = finish(share, last, n_row * nu)
    return polar, dressed


def solution(mesh):
    return jax.shard_map(
        on_device,
        mesh=mesh,
        in_specs=(P(EVERY, None, None, None), P(EVERY), P(EVERY), P(PLANE, "row"), P(PLANE, "row")),
        out_specs=(P(), P(PLANE, None, "row")),
        check_vma=False,
    )
```

```python
import functools

import jax
import jax.numpy as jnp
from jax import lax
from jax.experimental import pallas as pl
from jax.experimental.pallas import tpu as pltpu
from jax.sharding import PartitionSpec as P

PLANE = ("col", "rep")
EVERY = ("row", "col", "rep")
VMEM = pl.BlockSpec(memory_space=pltpu.VMEM)
SMEM = pl.BlockSpec(memory_space=pltpu.SMEM)
ROOM = 48 << 20


def flip(value, axes, mask, count):
    return lax.ppermute(value, axes, [(i, i ^ mask) for i in range(count)])


def after(value, earlier):
    return lax.optimization_barrier((value, earlier))


def gather_row(value, n_row):
    found = {0: value}
    step = n_row // 2
    while step:
        found.update({k ^ step: flip(held, "row", step, n_row) for k, held in list(found.items())})
        step //= 2
    return [found[k] for k in range(n_row)]


def plane_index():
    return lax.axis_index("col") * lax.axis_size("rep") + lax.axis_index("rep")


def place_kernel(nu_tiles, counts_ref, pairs_any, tiles_any, weight_any, column_any, *refs):
    line_ref, bundle_ref, pairs_ref, tiles_ref, sems = refs
    slots, aux, tile, _ = tiles_ref.shape
    copies = [
        pltpu.make_async_copy(source, target, sems.at[i])
        for i, (source, target) in enumerate(
            [
                (tiles_any, tiles_ref),
                (pairs_any, pairs_ref),
                (weight_any, line_ref.at[aux]),
                (column_any, bundle_ref.at[aux]),
            ]
        )
    ]
    for copy in copies:
        copy.start()
    for copy in copies:
        copy.wait()
    for t in range(slots):
        pair = pairs_ref[t]
        rows = pl.ds(pl.multiple_of(pair // nu_tiles * tile, tile), tile)
        cols = pl.ds(pl.multiple_of(pair % nu_tiles * tile, tile), tile)

        @pl.when(t < counts_ref[0])
        def _():
            for out_ref in (line_ref, bundle_ref):
                out_ref[:aux, rows, cols] = tiles_ref[t]

        @pl.when(t >= counts_ref[0])
        def _():
            for out_ref in (line_ref, bundle_ref):
                out_ref[:aux, rows, cols] = jnp.zeros((aux, tile, tile), out_ref.dtype)


def place(tile_pairs, tile_counts, tensor_tiles, weight, column):
    slots, aux, tile, _ = tensor_tiles.shape
    mu, nu = weight.shape
    shape = jax.ShapeDtypeStruct((aux + 1, mu, nu), weight.dtype)
    stays = [pltpu.with_memory_space_constraint(value, pltpu.HBM) for value in (tile_pairs, tensor_tiles, weight, column)]
    return pl.pallas_call(
        functools.partial(place_kernel, nu // tile),
        out_shape=(shape, shape),
        in_specs=[SMEM] + [pl.BlockSpec(memory_space=pltpu.HBM)] * 4,
        out_specs=(VMEM, VMEM),
        scratch_shapes=[
            pltpu.SMEM(tile_pairs.shape, tile_pairs.dtype),
            pltpu.VMEM(tensor_tiles.shape, tensor_tiles.dtype),
            pltpu.SemaphoreType.DMA((4,)),
        ],
        compiler_params=pltpu.CompilerParams(vmem_limit_bytes=ROOM),
        cost_estimate=pl.CostEstimate(flops=0, bytes_accessed=6 * tensor_tiles.size, transcendentals=0),
        name="place",
    )(tile_counts, *stays)


def half_kernel(n_row, n_plane, *refs):
    lines, bundles = refs[:n_row], refs[n_row : n_row + n_plane]
    out_ref, panel = refs[n_row + n_plane :]
    planes, mu, nu = lines[0].shape
    aux = planes - 1
    row, plane = lax.axis_index("row"), plane_index()
    for k in range(n_plane):
        panel[pl.ds(pl.multiple_of((plane ^ k) * mu, mu), mu), :] = bundles[k][aux]
    for p in range(aux):
        total = jnp.zeros((mu, nu), jnp.float32)
        for k in range(n_row):
            at = pl.multiple_of((row ^ k) * nu, nu)
            total += jnp.dot(lines[k][p], panel[pl.ds(at, nu), :], preferred_element_type=jnp.float32)
        out_ref[:, p * nu : (p + 1) * nu] = total.astype(out_ref.dtype)


def half(lines, bundles):
    planes, mu, nu = lines[0].shape
    aux = planes - 1
    n_row, n_plane = len(lines), len(bundles)
    kind = lines[0].dtype
    return pl.pallas_call(
        functools.partial(half_kernel, n_row, n_plane),
        out_shape=jax.ShapeDtypeStruct((mu, aux * nu), kind),
        in_specs=[VMEM] * (n_row + n_plane),
        out_specs=VMEM,
        scratch_shapes=[pltpu.VMEM((n_plane * mu, nu), kind)],
        compiler_params=pltpu.CompilerParams(vmem_limit_bytes=ROOM),
        cost_estimate=pl.CostEstimate(
            flops=2 * aux * mu * nu * nu * n_row, bytes_accessed=4 * n_row * aux * mu * nu, transcendentals=0
        ),
        name="half_product",
    )(*lines, *bundles)


def share_kernel(n_row, n_plane, half_ref, *refs):
    weights, bundles = refs[:n_row], refs[n_row : n_row + n_plane]
    weight_ref, share_ref = refs[n_row + n_plane :]
    planes, mu, nu = weights[0].shape
    aux = planes - 1
    row, plane = lax.axis_index("row"), plane_index()
    rows = lax.broadcasted_iota(jnp.int32, share_ref.shape[1:], 0)
    lanes = lax.broadcasted_iota(jnp.int32, share_ref.shape[1:], 1)
    share = jnp.zeros(share_ref.shape[1:], jnp.float32)
    for k in range(n_row):
        weight_ref[:, pl.ds(pl.multiple_of((row ^ k) * nu, nu), nu)] = weights[k][weights[k].shape[0] - 1]
    for p in range(aux):
        mixed = jnp.zeros((mu, nu), jnp.float32)
        for k in range(n_plane):
            at = pl.multiple_of((plane ^ k) * mu, mu)
            mixed += jnp.dot(weight_ref[:, pl.ds(at, mu)], bundles[k][p], preferred_element_type=jnp.float32)
        for q in range(aux):
            product = mixed * half_ref[:, q * nu : (q + 1) * nu].astype(jnp.float32)
            folded = jnp.sum(product.reshape(mu // 8, 8, nu), axis=0)
            own = jnp.sum(jnp.sum(folded, axis=0, keepdims=True), axis=1, keepdims=True)
            share = jnp.where((rows == p) & (lanes == q), own, share)
    for i in range(n_row * n_plane):
        share_ref[i] = share


def share_of(half_block, weights, bundles):
    planes, mu, nu = weights[0].shape
    aux, n_row, n_plane = planes - 1, len(weights), len(bundles)
    return pl.pallas_call(
        functools.partial(share_kernel, n_row, n_plane),
        out_shape=(
            jax.ShapeDtypeStruct((mu, n_row * nu), weights[0].dtype),
            jax.ShapeDtypeStruct((n_row * n_plane, 8, 128), jnp.float32),
        ),
        in_specs=[VMEM] * (1 + n_row + n_plane),
        out_specs=(VMEM, VMEM),
        compiler_params=pltpu.CompilerParams(vmem_limit_bytes=ROOM),
        cost_estimate=pl.CostEstimate(
            flops=2 * aux * mu * mu * nu * n_plane, bytes_accessed=4 * n_plane * aux * mu * nu, transcendentals=0
        ),
        name="polar_share",
    )(half_block, *weights, *bundles)


def dress_kernel(n_plane, total_ao, weight_ref, *refs):
    halves, (shares_ref, out_ref, polar_ref) = refs[:n_plane], refs[n_plane:]
    mu, aux, nu = out_ref.shape
    plane = plane_index()
    for q in range(aux):
        total = jnp.zeros((mu, nu), jnp.float32)
        for k in range(n_plane):
            total += jnp.dot(
                weight_ref[:, pl.ds(pl.multiple_of((plane ^ k) * mu, mu), mu)],
                halves[k][:, q * nu : (q + 1) * nu],
                preferred_element_type=jnp.float32,
            )
        out_ref[:, q, :] = total.astype(out_ref.dtype)
    polar_ref[...] = jnp.sum(shares_ref[...], axis=0)[:aux, :aux] / total_ao


def dress(weight, halves, shares, aux, total_ao):
    mu, width = halves[0].shape
    n_plane = len(halves)
    return pl.pallas_call(
        functools.partial(dress_kernel, n_plane, total_ao),
        out_shape=(
            jax.ShapeDtypeStruct((mu, aux, width // aux), weight.dtype),
            jax.ShapeDtypeStruct((aux, aux), jnp.float32),
        ),
        in_specs=[VMEM] * (n_plane + 2),
        out_specs=(VMEM, VMEM),
        compiler_params=pltpu.CompilerParams(vmem_limit_bytes=ROOM),
        cost_estimate=pl.CostEstimate(
            flops=2 * mu * mu * width * n_plane, bytes_accessed=4 * n_plane * mu * width, transcendentals=0
        ),
        name="dress",
    )(weight, *halves, shares)


def on_device(tensor_tiles, tile_pairs, tile_counts, occupied, virtual):
    aux = tensor_tiles.shape[1]
    nu = virtual.shape[1]
    n_row, n_plane = lax.axis_size("row"), lax.axis_size("col") * lax.axis_size("rep")
    near = list(range(2, n_plane, 2))
    sibling = lambda value: flip(value, PLANE, 1, n_plane)

    line, bundle = place(tile_pairs, tile_counts, tensor_tiles, occupied, virtual)
    lines = gather_row(line, n_row)
    bundles = []
    for value in [bundle] + [flip(bundle, PLANE, k, n_plane) for k in near]:
        bundles += [value, sibling(value)]
    own = half(lines, bundles)

    arrivals = [flip(own, PLANE, k, n_plane) for k in near]
    other = sibling(own)
    weight, share = share_of(own, lines, bundles)
    shares, (other, arrivals) = after(lax.all_to_all(share, EVERY, 0, 0), (other, arrivals))
    halves = [own, other]
    for value in arrivals:
        halves += [value, sibling(value)]
    dressed, polar = dress(weight, halves, shares, aux, n_row * nu)
    return polar, dressed


def solution(mesh):
    return jax.shard_map(
        on_device,
        mesh=mesh,
        in_specs=(P(EVERY, None, None, None), P(EVERY), P(EVERY), P(PLANE, "row"), P(PLANE, "row")),
        out_specs=(P(), P(PLANE, None, "row")),
        check_vma=False,
    )
```

```python
import functools

import jax
import jax.numpy as jnp
from jax import lax
from jax.experimental import pallas as pl
from jax.experimental.pallas import tpu as pltpu
from jax.sharding import PartitionSpec as P

PLANE = ("col", "rep")
EVERY = ("row", "col", "rep")
VMEM = pl.BlockSpec(memory_space=pltpu.VMEM)
SMEM = pl.BlockSpec(memory_space=pltpu.SMEM)
ROOM = 48 << 20


def flip(value, axes, mask, count):
    return lax.ppermute(value, axes, [(i, i ^ mask) for i in range(count)])


def after(value, earlier):
    return lax.optimization_barrier((value, earlier))


def gather_row(value, n_row):
    found = {0: value}
    step = n_row // 2
    while step:
        found.update({k ^ step: flip(held, "row", step, n_row) for k, held in list(found.items())})
        step //= 2
    return [found[k] for k in range(n_row)]


def plane_index():
    return lax.axis_index("col") * lax.axis_size("rep") + lax.axis_index("rep")


def place_kernel(nu_tiles, counts_ref, pairs_any, tiles_any, weight_any, column_any, *refs):
    line_ref, bundle_ref, pairs_ref, tiles_ref, sems = refs
    slots, aux, tile, _ = tiles_ref.shape
    copies = [
        pltpu.make_async_copy(source, target, sems.at[i])
        for i, (source, target) in enumerate(
            [
                (tiles_any, tiles_ref),
                (pairs_any, pairs_ref),
                (weight_any, line_ref.at[aux]),
                (column_any, bundle_ref.at[aux]),
            ]
        )
    ]
    for copy in copies:
        copy.start()
    for copy in copies:
        copy.wait()
    for t in range(slots):
        pair = pairs_ref[t]
        rows = pl.ds(pl.multiple_of(pair // nu_tiles * tile, tile), tile)
        cols = pl.ds(pl.multiple_of(pair % nu_tiles * tile, tile), tile)

        @pl.when(t < counts_ref[0])
        def _():
            for out_ref in (line_ref, bundle_ref):
                out_ref[:aux, rows, cols] = tiles_ref[t]

        @pl.when(t >= counts_ref[0])
        def _():
            for out_ref in (line_ref, bundle_ref):
                out_ref[:aux, rows, cols] = jnp.zeros((aux, tile, tile), out_ref.dtype)


def place(tile_pairs, tile_counts, tensor_tiles, weight, column):
    slots, aux, tile, _ = tensor_tiles.shape
    mu, nu = weight.shape
    shape = jax.ShapeDtypeStruct((aux + 1, mu, nu), weight.dtype)
    stays = [pltpu.with_memory_space_constraint(value, pltpu.HBM) for value in (tile_pairs, tensor_tiles, weight, column)]
    return pl.pallas_call(
        functools.partial(place_kernel, nu // tile),
        out_shape=(shape, shape),
        in_specs=[SMEM] + [pl.BlockSpec(memory_space=pltpu.HBM)] * 4,
        out_specs=(VMEM, VMEM),
        scratch_shapes=[
            pltpu.SMEM(tile_pairs.shape, tile_pairs.dtype),
            pltpu.VMEM(tensor_tiles.shape, tensor_tiles.dtype),
            pltpu.SemaphoreType.DMA((4,)),
        ],
        compiler_params=pltpu.CompilerParams(vmem_limit_bytes=ROOM),
        cost_estimate=pl.CostEstimate(flops=0, bytes_accessed=6 * tensor_tiles.size, transcendentals=0),
        name="place",
    )(tile_counts, *stays)


def half_kernel(n_row, n_plane, *refs):
    lines, bundles = refs[:n_row], refs[n_row : n_row + n_plane]
    out_ref, panel = refs[n_row + n_plane :]
    planes, mu, nu = lines[0].shape
    aux = planes - 1
    row, plane = lax.axis_index("row"), plane_index()
    for k in range(n_plane):
        panel[pl.ds(pl.multiple_of((plane ^ k) * mu, mu), mu), :] = bundles[k][aux]
    for p in range(aux):
        total = jnp.zeros((mu, nu), jnp.float32)
        for k in range(n_row):
            at = pl.multiple_of((row ^ k) * nu, nu)
            total += jnp.dot(lines[k][p], panel[pl.ds(at, nu), :], preferred_element_type=jnp.float32)
        out_ref[:, p * nu : (p + 1) * nu] = total.astype(out_ref.dtype)


def half(lines, bundles):
    planes, mu, nu = lines[0].shape
    aux = planes - 1
    n_row, n_plane = len(lines), len(bundles)
    kind = lines[0].dtype
    return pl.pallas_call(
        functools.partial(half_kernel, n_row, n_plane),
        out_shape=jax.ShapeDtypeStruct((mu, aux * nu), kind),
        in_specs=[VMEM] * (n_row + n_plane),
        out_specs=VMEM,
        scratch_shapes=[pltpu.VMEM((n_plane * mu, nu), kind)],
        compiler_params=pltpu.CompilerParams(vmem_limit_bytes=ROOM),
        cost_estimate=pl.CostEstimate(
            flops=2 * aux * mu * nu * nu * n_row, bytes_accessed=4 * n_row * aux * mu * nu, transcendentals=0
        ),
        name="half_product",
    )(*lines, *bundles)


def share_kernel(n_row, n_plane, half_ref, *refs):
    weights, bundles = refs[:n_row], refs[n_row : n_row + n_plane]
    weight_ref, share_ref = refs[n_row + n_plane :]
    planes, mu, nu = weights[0].shape
    aux = planes - 1
    row, plane = lax.axis_index("row"), plane_index()
    rows = lax.broadcasted_iota(jnp.int32, share_ref.shape[1:], 0)
    lanes = lax.broadcasted_iota(jnp.int32, share_ref.shape[1:], 1)
    share = jnp.zeros(share_ref.shape[1:], jnp.float32)
    for k in range(n_row):
        weight_ref[:, pl.ds(pl.multiple_of((row ^ k) * nu, nu), nu)] = weights[k][weights[k].shape[0] - 1]
    for p in range(aux):
        mixed = jnp.zeros((mu, nu), jnp.float32)
        for k in range(n_plane):
            at = pl.multiple_of((plane ^ k) * mu, mu)
            mixed += jnp.dot(weight_ref[:, pl.ds(at, mu)], bundles[k][p], preferred_element_type=jnp.float32)
        for q in range(aux):
            product = mixed * half_ref[:, q * nu : (q + 1) * nu].astype(jnp.float32)
            folded = jnp.sum(product.reshape(mu // 8, 8, nu), axis=0)
            own = jnp.sum(jnp.sum(folded, axis=0, keepdims=True), axis=1, keepdims=True)
            share = jnp.where((rows == p) & (lanes == q), own, share)
    for i in range(n_row * n_plane):
        share_ref[i] = share


def share_of(half_block, weights, bundles):
    planes, mu, nu = weights[0].shape
    aux, n_row, n_plane = planes - 1, len(weights), len(bundles)
    return pl.pallas_call(
        functools.partial(share_kernel, n_row, n_plane),
        out_shape=(
            jax.ShapeDtypeStruct((mu, n_row * nu), weights[0].dtype),
            jax.ShapeDtypeStruct((n_row * n_plane, 8, 128), jnp.float32),
        ),
        in_specs=[VMEM] * (1 + n_row + n_plane),
        out_specs=(VMEM, VMEM),
        compiler_params=pltpu.CompilerParams(vmem_limit_bytes=ROOM),
        cost_estimate=pl.CostEstimate(
            flops=2 * aux * mu * mu * nu * n_plane, bytes_accessed=4 * n_plane * aux * mu * nu, transcendentals=0
        ),
        name="polar_share",
    )(half_block, *weights, *bundles)


def dress_kernel(n_plane, weight_ref, *refs):
    halves, out_ref = refs[:n_plane], refs[n_plane]
    mu, aux, nu = out_ref.shape
    plane = plane_index()
    for q in range(aux):
        total = jnp.zeros((mu, nu), jnp.float32)
        for k in range(n_plane):
            total += jnp.dot(
                weight_ref[:, pl.ds(pl.multiple_of((plane ^ k) * mu, mu), mu)],
                halves[k][:, q * nu : (q + 1) * nu],
                preferred_element_type=jnp.float32,
            )
        out_ref[:, q, :] = total.astype(out_ref.dtype)


def dress(weight, halves, aux):
    mu, width = halves[0].shape
    n_plane = len(halves)
    return pl.pallas_call(
        functools.partial(dress_kernel, n_plane),
        out_shape=jax.ShapeDtypeStruct((mu, aux, width // aux), weight.dtype),
        in_specs=[VMEM] * (n_plane + 1),
        out_specs=VMEM,
        compiler_params=pltpu.CompilerParams(vmem_limit_bytes=ROOM),
        cost_estimate=pl.CostEstimate(
            flops=2 * mu * mu * width * n_plane, bytes_accessed=4 * n_plane * mu * width, transcendentals=0
        ),
        name="dress",
    )(weight, *halves)


def finish_kernel(total_ao, shares_ref, out_ref):
    aux = out_ref.shape[0]
    out_ref[...] = jnp.sum(shares_ref[...], axis=0)[:aux, :aux] / total_ao


def finish(shares, aux, total_ao):
    return pl.pallas_call(
        functools.partial(finish_kernel, total_ao),
        out_shape=jax.ShapeDtypeStruct((aux, aux), jnp.float32),
        in_specs=[VMEM],
        out_specs=VMEM,
        compiler_params=pltpu.CompilerParams(vmem_limit_bytes=ROOM),
        name="finish",
    )(shares)


def on_device(tensor_tiles, tile_pairs, tile_counts, occupied, virtual):
    aux = tensor_tiles.shape[1]
    nu = virtual.shape[1]
    n_row, n_plane = lax.axis_size("row"), lax.axis_size("col") * lax.axis_size("rep")
    near = list(range(2, n_plane, 2))
    sibling = lambda value: flip(value, PLANE, 1, n_plane)

    line, bundle = place(tile_pairs, tile_counts, tensor_tiles, occupied, virtual)
    lines = gather_row(line, n_row)
    bundles = []
    for value in [bundle] + [flip(bundle, PLANE, k, n_plane) for k in near]:
        bundles += [value, sibling(value)]
    own = half(lines, bundles)

    arrivals = [flip(own, PLANE, k, n_plane) for k in near]
    weight, share = share_of(own, lines, bundles)
    shares = lax.all_to_all(share, EVERY, 0, 0)
    halves = []
    for value in [own] + arrivals:
        halves += [value, sibling(value)]
    dressed = dress(weight, halves, aux)
    polar = finish(shares, aux, n_row * nu)
    return polar, dressed


def solution(mesh):
    return jax.shard_map(
        on_device,
        mesh=mesh,
        in_specs=(P(EVERY, None, None, None), P(EVERY), P(EVERY), P(PLANE, "row"), P(PLANE, "row")),
        out_specs=(P(), P(PLANE, None, "row")),
        check_vma=False,
    )
```

```python
import functools

import jax
import jax.numpy as jnp
from jax import lax
from jax.experimental import pallas as pl
from jax.experimental.pallas import tpu as pltpu
from jax.sharding import PartitionSpec as P

PLANE = ("col", "rep")
EVERY = ("row", "col", "rep")
VMEM = pl.BlockSpec(memory_space=pltpu.VMEM)
SMEM = pl.BlockSpec(memory_space=pltpu.SMEM)
ROOM = 48 << 20


def flip(value, axes, mask, count):
    return lax.ppermute(value, axes, [(i, i ^ mask) for i in range(count)])


def after(value, earlier):
    return lax.optimization_barrier((value, earlier))


def gather_row(value, n_row):
    found = {0: value}
    step = n_row // 2
    while step:
        found.update({k ^ step: flip(held, "row", step, n_row) for k, held in list(found.items())})
        step //= 2
    return [found[k] for k in range(n_row)]


def plane_index():
    return lax.axis_index("col") * lax.axis_size("rep") + lax.axis_index("rep")


def place_kernel(nu_tiles, counts_ref, pairs_any, tiles_any, weight_any, column_any, *refs):
    line_ref, bundle_ref, pairs_ref, tiles_ref, sems = refs
    slots, aux, tile, _ = tiles_ref.shape
    copies = [
        pltpu.make_async_copy(source, target, sems.at[i])
        for i, (source, target) in enumerate(
            [
                (tiles_any, tiles_ref),
                (pairs_any, pairs_ref),
                (weight_any, line_ref.at[aux]),
                (column_any, bundle_ref.at[aux]),
            ]
        )
    ]
    for copy in copies:
        copy.start()
    for copy in copies:
        copy.wait()
    for t in range(slots):
        pair = pairs_ref[t]
        rows = pl.ds(pl.multiple_of(pair // nu_tiles * tile, tile), tile)
        cols = pl.ds(pl.multiple_of(pair % nu_tiles * tile, tile), tile)

        @pl.when(t < counts_ref[0])
        def _():
            for out_ref in (line_ref, bundle_ref):
                out_ref[:aux, rows, cols] = tiles_ref[t]

        @pl.when(t >= counts_ref[0])
        def _():
            for out_ref in (line_ref, bundle_ref):
                out_ref[:aux, rows, cols] = jnp.zeros((aux, tile, tile), out_ref.dtype)


def place(tile_pairs, tile_counts, tensor_tiles, weight, column):
    slots, aux, tile, _ = tensor_tiles.shape
    mu, nu = weight.shape
    shape = jax.ShapeDtypeStruct((aux + 1, mu, nu), weight.dtype)
    stays = [pltpu.with_memory_space_constraint(value, pltpu.HBM) for value in (tile_pairs, tensor_tiles, weight, column)]
    return pl.pallas_call(
        functools.partial(place_kernel, nu // tile),
        out_shape=(shape, shape),
        in_specs=[SMEM] + [pl.BlockSpec(memory_space=pltpu.HBM)] * 4,
        out_specs=(VMEM, VMEM),
        scratch_shapes=[
            pltpu.SMEM(tile_pairs.shape, tile_pairs.dtype),
            pltpu.VMEM(tensor_tiles.shape, tensor_tiles.dtype),
            pltpu.SemaphoreType.DMA((4,)),
        ],
        compiler_params=pltpu.CompilerParams(vmem_limit_bytes=ROOM),
        cost_estimate=pl.CostEstimate(flops=0, bytes_accessed=6 * tensor_tiles.size, transcendentals=0),
        name="place",
    )(tile_counts, *stays)


def half_kernel(n_row, n_plane, *refs):
    lines, bundles = refs[:n_row], refs[n_row : n_row + n_plane]
    out_ref, panel = refs[n_row + n_plane :]
    planes, mu, nu = lines[0].shape
    aux = planes - 1
    row, plane = lax.axis_index("row"), plane_index()
    for k in range(n_plane):
        panel[pl.ds(pl.multiple_of((plane ^ k) * mu, mu), mu), :] = bundles[k][aux]
    for p in range(aux):
        total = jnp.zeros((mu, nu), jnp.float32)
        for k in range(n_row):
            at = pl.multiple_of((row ^ k) * nu, nu)
            total += jnp.dot(lines[k][p], panel[pl.ds(at, nu), :], preferred_element_type=jnp.float32)
        out_ref[:, p * nu : (p + 1) * nu] = total.astype(out_ref.dtype)


def half(lines, bundles):
    planes, mu, nu = lines[0].shape
    aux = planes - 1
    n_row, n_plane = len(lines), len(bundles)
    kind = lines[0].dtype
    return pl.pallas_call(
        functools.partial(half_kernel, n_row, n_plane),
        out_shape=jax.ShapeDtypeStruct((mu, aux * nu), kind),
        in_specs=[VMEM] * (n_row + n_plane),
        out_specs=VMEM,
        scratch_shapes=[pltpu.VMEM((n_plane * mu, nu), kind)],
        compiler_params=pltpu.CompilerParams(vmem_limit_bytes=ROOM),
        cost_estimate=pl.CostEstimate(
            flops=2 * aux * mu * nu * nu * n_row, bytes_accessed=4 * n_row * aux * mu * nu, transcendentals=0
        ),
        name="half_product",
    )(*lines, *bundles)


def share_kernel(n_row, n_plane, half_ref, *refs):
    weights, bundles = refs[:n_row], refs[n_row : n_row + n_plane]
    weight_ref, share_ref = refs[n_row + n_plane :]
    planes, mu, nu = weights[0].shape
    aux = planes - 1
    row, plane = lax.axis_index("row"), plane_index()
    lanes = lax.broadcasted_iota(jnp.int32, share_ref.shape[1:], 1)
    share = jnp.zeros(share_ref.shape[1:], jnp.float32)
    for k in range(n_row):
        weight_ref[:, pl.ds(pl.multiple_of((row ^ k) * nu, nu), nu)] = weights[k][weights[k].shape[0] - 1]
    for p in range(aux):
        mixed = jnp.zeros((mu, nu), jnp.float32)
        for k in range(n_plane):
            at = pl.multiple_of((plane ^ k) * mu, mu)
            mixed += jnp.dot(weight_ref[:, pl.ds(at, mu)], bundles[k][p], preferred_element_type=jnp.float32)
        for q in range(aux):
            product = mixed * half_ref[:, q * nu : (q + 1) * nu].astype(jnp.float32)
            folded = jnp.sum(product.reshape(mu // 8, 8, nu), axis=0)
            own = jnp.sum(jnp.sum(folded, axis=0, keepdims=True), axis=1, keepdims=True)
            share = jnp.where(lanes == p * aux + q, own, share)
    for i in range(n_row * n_plane):
        share_ref[i] = share


def share_of(half_block, weights, bundles):
    planes, mu, nu = weights[0].shape
    aux, n_row, n_plane = planes - 1, len(weights), len(bundles)
    return pl.pallas_call(
        functools.partial(share_kernel, n_row, n_plane),
        out_shape=(
            jax.ShapeDtypeStruct((mu, n_row * nu), weights[0].dtype),
            jax.ShapeDtypeStruct((n_row * n_plane, 1, 128), jnp.float32),
        ),
        in_specs=[VMEM] * (1 + n_row + n_plane),
        out_specs=(VMEM, VMEM),
        compiler_params=pltpu.CompilerParams(vmem_limit_bytes=ROOM),
        cost_estimate=pl.CostEstimate(
            flops=2 * aux * mu * mu * nu * n_plane, bytes_accessed=4 * n_plane * aux * mu * nu, transcendentals=0
        ),
        name="polar_share",
    )(half_block, *weights, *bundles)


def dress_kernel(n_plane, total_ao, weight_ref, *refs):
    halves, (shares_ref, out_ref, polar_ref) = refs[:n_plane], refs[n_plane:]
    mu, aux, nu = out_ref.shape
    plane = plane_index()
    sums = []
    for q in range(aux):
        total = jnp.zeros((mu, nu), jnp.float32)
        for k in range(n_plane):
            total += jnp.dot(
                weight_ref[:, pl.ds(pl.multiple_of((plane ^ k) * mu, mu), mu)],
                halves[k][:, q * nu : (q + 1) * nu],
                preferred_element_type=jnp.float32,
            )
        sums.append(total)
    out_ref[...] = jnp.stack(sums, axis=1).astype(out_ref.dtype)
    polar = jnp.sum(shares_ref[...], axis=0) / total_ao
    for p in range(aux):
        polar_ref[p : p + 1, :] = polar[:, p * aux : (p + 1) * aux]


def dress(weight, halves, shares, aux, total_ao):
    mu, width = halves[0].shape
    n_plane = len(halves)
    return pl.pallas_call(
        functools.partial(dress_kernel, n_plane, total_ao),
        out_shape=(
            jax.ShapeDtypeStruct((mu, aux, width // aux), weight.dtype),
            jax.ShapeDtypeStruct((aux, aux), jnp.float32),
        ),
        in_specs=[VMEM] * (n_plane + 2),
        out_specs=(VMEM, VMEM),
        compiler_params=pltpu.CompilerParams(vmem_limit_bytes=ROOM),
        cost_estimate=pl.CostEstimate(
            flops=2 * mu * mu * width * n_plane, bytes_accessed=4 * n_plane * mu * width, transcendentals=0
        ),
        name="dress",
    )(weight, *halves, shares)


def on_device(tensor_tiles, tile_pairs, tile_counts, occupied, virtual):
    aux = tensor_tiles.shape[1]
    nu = virtual.shape[1]
    n_row, n_plane = lax.axis_size("row"), lax.axis_size("col") * lax.axis_size("rep")
    near = list(range(2, n_plane, 2))
    sibling = lambda value: flip(value, PLANE, 1, n_plane)

    line, bundle = place(tile_pairs, tile_counts, tensor_tiles, occupied, virtual)
    lines = gather_row(line, n_row)
    bundles = []
    for value in [bundle] + [flip(bundle, PLANE, k, n_plane) for k in near]:
        bundles += [value, sibling(value)]
    own = half(lines, bundles)

    arrivals = [flip(own, PLANE, k, n_plane) for k in near]
    other = sibling(own)
    weight, share = share_of(own, lines, bundles)
    shares, (other, arrivals) = after(lax.all_to_all(share, EVERY, 0, 0), (other, arrivals))
    halves = [own, other]
    for value in arrivals:
        halves += [value, sibling(value)]
    dressed, polar = dress(weight, halves, shares, aux, n_row * nu)
    return polar, dressed


def solution(mesh):
    return jax.shard_map(
        on_device,
        mesh=mesh,
        in_specs=(P(EVERY, None, None, None), P(EVERY), P(EVERY), P(PLANE, "row"), P(PLANE, "row")),
        out_specs=(P(), P(PLANE, None, "row")),
        check_vma=False,
    )
```

```python
import functools

import jax
import jax.numpy as jnp
from jax import lax
from jax.experimental import pallas as pl
from jax.experimental.pallas import tpu as pltpu
from jax.sharding import PartitionSpec as P

PLANE = ("col", "rep")
EVERY = ("row", "col", "rep")
VMEM = pl.BlockSpec(memory_space=pltpu.VMEM)
SMEM = pl.BlockSpec(memory_space=pltpu.SMEM)
ROOM = 48 << 20


def flip(value, axes, mask, count):
    return lax.ppermute(value, axes, [(i, i ^ mask) for i in range(count)])


def after(value, earlier):
    return lax.optimization_barrier((value, earlier))


def gather_row(value, n_row):
    found = {0: value}
    step = n_row // 2
    while step:
        found.update({k ^ step: flip(held, "row", step, n_row) for k, held in list(found.items())})
        step //= 2
    return [found[k] for k in range(n_row)]


def plane_index():
    return lax.axis_index("col") * lax.axis_size("rep") + lax.axis_index("rep")


def place_kernel(nu_tiles, counts_ref, pairs_any, tiles_any, weight_any, column_any, *refs):
    line_ref, bundle_ref, pairs_ref, tiles_ref, sems = refs
    slots, aux, tile, _ = tiles_ref.shape
    cut = line_ref.shape[0] - 1
    copies = [
        pltpu.make_async_copy(source, target, sems.at[i])
        for i, (source, target) in enumerate(
            [
                (tiles_any, tiles_ref),
                (pairs_any, pairs_ref),
                (weight_any, line_ref.at[cut]),
                (column_any, bundle_ref.at[aux - cut]),
            ]
        )
    ]
    for copy in copies:
        copy.start()
    for copy in copies:
        copy.wait()
    for t in range(slots):
        pair = pairs_ref[t]
        rows = pl.ds(pl.multiple_of(pair // nu_tiles * tile, tile), tile)
        cols = pl.ds(pl.multiple_of(pair % nu_tiles * tile, tile), tile)

        @pl.when(t < counts_ref[0])
        def _():
            line_ref[:cut, rows, cols] = tiles_ref[t, :cut]
            bundle_ref[: aux - cut, rows, cols] = tiles_ref[t, cut:]

        @pl.when(t >= counts_ref[0])
        def _():
            line_ref[:cut, rows, cols] = jnp.zeros((cut, tile, tile), line_ref.dtype)
            bundle_ref[: aux - cut, rows, cols] = jnp.zeros((aux - cut, tile, tile), line_ref.dtype)


def place(tile_pairs, tile_counts, tensor_tiles, weight, column):
    slots, aux, tile, _ = tensor_tiles.shape
    mu, nu = weight.shape
    cut = aux // 2
    stays = [
        pltpu.with_memory_space_constraint(value, pltpu.HBM) for value in (tile_pairs, tensor_tiles, weight, column)
    ]
    return pl.pallas_call(
        functools.partial(place_kernel, nu // tile),
        out_shape=[jax.ShapeDtypeStruct((count + 1, mu, nu), weight.dtype) for count in (cut, aux - cut)],
        in_specs=[SMEM] + [pl.BlockSpec(memory_space=pltpu.HBM)] * 4,
        out_specs=[VMEM, VMEM],
        scratch_shapes=[
            pltpu.SMEM(tile_pairs.shape, tile_pairs.dtype),
            pltpu.VMEM(tensor_tiles.shape, tensor_tiles.dtype),
            pltpu.SemaphoreType.DMA((4,)),
        ],
        compiler_params=pltpu.CompilerParams(vmem_limit_bytes=ROOM),
        cost_estimate=pl.CostEstimate(flops=0, bytes_accessed=6 * tensor_tiles.size, transcendentals=0),
        name="place",
    )(tile_counts, *stays)


def dot(left, right):
    return jnp.dot(left, right, preferred_element_type=jnp.float32)


def mix_kernel(n_row, n_plane, *refs):
    lines, bundles = refs[:n_row], refs[n_row : n_row + n_plane]
    half_ref, mixed_ref, weight_ref, panel_ref = refs[n_row + n_plane :]
    planes, mu, nu = lines[0].shape
    cut, rest = planes - 1, bundles[0].shape[0] - 1
    row, plane = lax.axis_index("row"), plane_index()
    for k in range(n_plane):
        panel_ref[pl.ds(pl.multiple_of((plane ^ k) * mu, mu), mu), :] = bundles[k][rest]
    for k in range(n_row):
        weight_ref[:, pl.ds(pl.multiple_of((row ^ k) * nu, nu), nu)] = lines[k][cut]
    for p in range(cut):
        total = jnp.zeros((mu, nu), jnp.float32)
        for k in range(n_row):
            at = pl.multiple_of((row ^ k) * nu, nu)
            total += dot(lines[k][p], panel_ref[pl.ds(at, nu), :])
        half_ref[:, p * nu : (p + 1) * nu] = total.astype(half_ref.dtype)
    for p in range(rest):
        total = jnp.zeros((mu, nu), jnp.float32)
        for k in range(n_plane):
            at = pl.multiple_of((plane ^ k) * mu, mu)
            total += dot(weight_ref[:, pl.ds(at, mu)], bundles[k][p])
        mixed_ref[:, p * nu : (p + 1) * nu] = total.astype(mixed_ref.dtype)


def mix(lines, bundles):
    planes, mu, nu = lines[0].shape
    cut, rest = planes - 1, bundles[0].shape[0] - 1
    n_row, n_plane = len(lines), len(bundles)
    kind = lines[0].dtype
    return pl.pallas_call(
        functools.partial(mix_kernel, n_row, n_plane),
        out_shape=(
            jax.ShapeDtypeStruct((mu, cut * nu), kind),
            jax.ShapeDtypeStruct((mu, rest * nu), kind),
            jax.ShapeDtypeStruct((mu, n_row * nu), kind),
            jax.ShapeDtypeStruct((n_plane * mu, nu), kind),
        ),
        in_specs=[VMEM] * (n_row + n_plane),
        out_specs=[VMEM] * 4,
        compiler_params=pltpu.CompilerParams(vmem_limit_bytes=ROOM),
        cost_estimate=pl.CostEstimate(
            flops=2 * (cut + rest) * mu * nu * nu * n_row,
            bytes_accessed=4 * n_row * (cut + rest) * mu * nu,
            transcendentals=0,
        ),
        name="mix",
    )(*lines, *bundles)


def dress_kernel(n_row, n_plane, n_all, total_ao, weight_ref, panel_ref, line_ref, bundle_ref, *refs):
    halves, mixed = refs[:n_plane], refs[n_plane : n_plane + n_row]
    out_ref, share_ref = refs[n_plane + n_row :]
    mu, aux, nu = out_ref.shape
    cut = line_ref.shape[0] - 1
    row, plane = lax.axis_index("row"), plane_index()
    lanes = lax.broadcasted_iota(jnp.int32, share_ref.shape[1:], 1)
    share = jnp.zeros(share_ref.shape[1:], jnp.float32)
    for q in range(aux):
        total = jnp.zeros((mu, nu), jnp.float32)
        if q < cut:
            for k in range(n_plane):
                at = pl.multiple_of((plane ^ k) * mu, mu)
                total += dot(weight_ref[:, pl.ds(at, mu)], halves[k][:, q * nu : (q + 1) * nu])
        else:
            for k in range(n_row):
                at = pl.multiple_of((row ^ k) * nu, nu)
                total += dot(mixed[k][:, (q - cut) * nu : (q - cut + 1) * nu], panel_ref[pl.ds(at, nu), :])
        rounded = total.astype(out_ref.dtype)
        out_ref[:, q, :] = rounded
        wide = rounded.astype(jnp.float32) if q < cut else total
        for p in range(aux):
            block = line_ref[p] if p < cut else bundle_ref[p - cut]
            folded = jnp.sum((block.astype(jnp.float32) * wide).reshape(mu // 8, 8, nu), axis=0)
            own = jnp.sum(jnp.sum(folded, axis=0, keepdims=True), axis=1, keepdims=True) / total_ao
            share = jnp.where(lanes == p * aux + q, own, share)
    for i in range(n_all):
        share_ref[i] = share


def dress(weight, panel, line, bundle, halves, mixed, n_all):
    planes, mu, nu = line.shape
    aux = planes - 1 + bundle.shape[0] - 1
    n_row, n_plane = len(mixed), len(halves)
    return pl.pallas_call(
        functools.partial(dress_kernel, n_row, n_plane, n_all, weight.shape[1]),
        out_shape=(
            jax.ShapeDtypeStruct((mu, aux, nu), line.dtype),
            jax.ShapeDtypeStruct((n_all, 1, 128), jnp.float32),
        ),
        in_specs=[VMEM] * (4 + n_plane + n_row),
        out_specs=(VMEM, VMEM),
        compiler_params=pltpu.CompilerParams(vmem_limit_bytes=ROOM),
        cost_estimate=pl.CostEstimate(
            flops=2 * aux * mu * mu * nu * n_plane, bytes_accessed=4 * n_plane * aux * mu * nu, transcendentals=0
        ),
        name="dress",
    )(weight, panel, line, bundle, *halves, *mixed)


def finish_kernel(shares_ref, out_ref):
    aux = out_ref.shape[0]
    polar = jnp.sum(shares_ref[...], axis=0)
    for p in range(aux):
        out_ref[p : p + 1, :] = polar[:, p * aux : (p + 1) * aux]


def finish(shares, aux):
    return pl.pallas_call(
        finish_kernel,
        out_shape=jax.ShapeDtypeStruct((aux, aux), jnp.float32),
        in_specs=[VMEM],
        out_specs=VMEM,
        compiler_params=pltpu.CompilerParams(vmem_limit_bytes=ROOM),
        name="finish",
    )(shares)


def on_device(tensor_tiles, tile_pairs, tile_counts, occupied, virtual):
    aux = tensor_tiles.shape[1]
    n_row, n_plane = lax.axis_size("row"), lax.axis_size("col") * lax.axis_size("rep")
    near = list(range(2, n_plane, 2))
    sibling = lambda value: flip(value, PLANE, 1, n_plane)

    def gather_plane(value):
        values = [value] + [flip(value, PLANE, k, n_plane) for k in near]
        return [held for value in values for held in (value, sibling(value))]

    line, bundle = place(tile_pairs, tile_counts, tensor_tiles, occupied, virtual)
    half, mixed, weight, panel = mix(gather_row(line, n_row), gather_plane(bundle))
    halves, mixed = gather_plane(half), gather_row(mixed, n_row)
    dressed, shares = dress(weight, panel, line, bundle, halves, mixed, n_row * n_plane)
    polar = finish(lax.all_to_all(shares, EVERY, 0, 0), aux)
    return polar, dressed


def solution(mesh):
    return jax.shard_map(
        on_device,
        mesh=mesh,
        in_specs=(P(EVERY, None, None, None), P(EVERY), P(EVERY), P(PLANE, "row"), P(PLANE, "row")),
        out_specs=(P(), P(PLANE, None, "row")),
        check_vma=False,
    )
```

```python
import functools

import jax
import jax.numpy as jnp
from jax import lax
from jax.experimental import pallas as pl
from jax.experimental.pallas import tpu as pltpu
from jax.sharding import PartitionSpec as P

PLANE = ("col", "rep")
EVERY = ("row", "col", "rep")
VMEM = pl.BlockSpec(memory_space=pltpu.VMEM)
SMEM = pl.BlockSpec(memory_space=pltpu.SMEM)
ROOM = 48 << 20


def flip(value, axes, mask, count):
    return lax.ppermute(value, axes, [(i, i ^ mask) for i in range(count)])


def after(value, earlier):
    return lax.optimization_barrier((value, earlier))


def split_kernel(value_ref, block_ref, weight_ref):
    cut = block_ref.shape[0]
    block_ref[...] = value_ref[:cut]
    weight_ref[...] = value_ref[cut:]


def split(value):
    planes, mu, nu = value.shape
    return pl.pallas_call(
        split_kernel,
        out_shape=[jax.ShapeDtypeStruct((count, mu, nu), value.dtype) for count in (planes - 1, 1)],
        in_specs=[VMEM],
        out_specs=[VMEM, VMEM],
        compiler_params=pltpu.CompilerParams(vmem_limit_bytes=ROOM),
        cost_estimate=pl.CostEstimate(flops=0, bytes_accessed=4 * value.size, transcendentals=0),
        name="split",
    )(value)


def gather_row(value, n_row):
    found = {0: value}
    step = n_row // 2
    while step:
        found.update({k ^ step: flip(held, "row", step, n_row) for k, held in list(found.items())})
        step //= 2
    return [found[k] for k in range(n_row)]


def plane_index():
    return lax.axis_index("col") * lax.axis_size("rep") + lax.axis_index("rep")


def place_kernel(nu_tiles, counts_ref, pairs_any, tiles_any, weight_any, column_any, *refs):
    line_ref, bundle_ref, pairs_ref, tiles_ref, sems = refs
    slots, aux, tile, _ = tiles_ref.shape
    cut = line_ref.shape[0] - 1
    copies = [
        pltpu.make_async_copy(source, target, sems.at[i])
        for i, (source, target) in enumerate(
            [
                (tiles_any, tiles_ref),
                (pairs_any, pairs_ref),
                (weight_any, line_ref.at[cut]),
                (column_any, bundle_ref.at[aux - cut]),
            ]
        )
    ]
    for copy in copies:
        copy.start()
    for copy in copies:
        copy.wait()
    for t in range(slots):
        pair = pairs_ref[t]
        rows = pl.ds(pl.multiple_of(pair // nu_tiles * tile, tile), tile)
        cols = pl.ds(pl.multiple_of(pair % nu_tiles * tile, tile), tile)

        @pl.when(t < counts_ref[0])
        def _():
            line_ref[:cut, rows, cols] = tiles_ref[t, :cut]
            bundle_ref[: aux - cut, rows, cols] = tiles_ref[t, cut:]

        @pl.when(t >= counts_ref[0])
        def _():
            line_ref[:cut, rows, cols] = jnp.zeros((cut, tile, tile), line_ref.dtype)
            bundle_ref[: aux - cut, rows, cols] = jnp.zeros((aux - cut, tile, tile), line_ref.dtype)


def place(tile_pairs, tile_counts, tensor_tiles, weight, column):
    slots, aux, tile, _ = tensor_tiles.shape
    mu, nu = weight.shape
    cut = aux // 2
    stays = [
        pltpu.with_memory_space_constraint(value, pltpu.HBM) for value in (tile_pairs, tensor_tiles, weight, column)
    ]
    return pl.pallas_call(
        functools.partial(place_kernel, nu // tile),
        out_shape=[jax.ShapeDtypeStruct((count + 1, mu, nu), weight.dtype) for count in (cut, aux - cut)],
        in_specs=[SMEM] + [pl.BlockSpec(memory_space=pltpu.HBM)] * 4,
        out_specs=[VMEM, VMEM],
        scratch_shapes=[
            pltpu.SMEM(tile_pairs.shape, tile_pairs.dtype),
            pltpu.VMEM(tensor_tiles.shape, tensor_tiles.dtype),
            pltpu.SemaphoreType.DMA((4,)),
        ],
        compiler_params=pltpu.CompilerParams(vmem_limit_bytes=ROOM),
        cost_estimate=pl.CostEstimate(flops=0, bytes_accessed=6 * tensor_tiles.size, transcendentals=0),
        name="place",
    )(tile_counts, *stays)


def dot(left, right):
    return jnp.dot(left, right, preferred_element_type=jnp.float32)


def mix_kernel(n_row, n_plane, *refs):
    weights, bundles = refs[:n_row], refs[n_row : n_row + n_plane]
    mixed_ref, weight_ref = refs[n_row + n_plane :]
    _, mu, nu = weights[0].shape
    row, plane = lax.axis_index("row"), plane_index()
    for k, ref in enumerate(weights):
        weight_ref[:, pl.ds(pl.multiple_of((row ^ k) * nu, nu), nu)] = ref[ref.shape[0] - 1]
    for p in range(bundles[0].shape[0] - 1):
        total = jnp.zeros((mu, nu), jnp.float32)
        for k in range(n_plane):
            at = pl.multiple_of((plane ^ k) * mu, mu)
            total += dot(weight_ref[:, pl.ds(at, mu)], bundles[k][p])
        mixed_ref[:, p * nu : (p + 1) * nu] = total.astype(mixed_ref.dtype)


def mix(weights, bundles):
    planes, mu, nu = bundles[0].shape
    n_row, n_plane = len(weights), len(bundles)
    kind = weights[0].dtype
    return pl.pallas_call(
        functools.partial(mix_kernel, n_row, n_plane),
        out_shape=(
            jax.ShapeDtypeStruct((mu, (planes - 1) * nu), kind),
            jax.ShapeDtypeStruct((mu, n_row * nu), kind),
        ),
        in_specs=[VMEM] * (n_row + n_plane),
        out_specs=[VMEM] * 2,
        compiler_params=pltpu.CompilerParams(vmem_limit_bytes=ROOM),
        cost_estimate=pl.CostEstimate(
            flops=2 * planes * mu * nu * nu * n_row, bytes_accessed=4 * n_row * planes * mu * nu, transcendentals=0
        ),
        name="mix",
    )(*weights, *bundles)


def half_kernel(cut, n_row, n_plane, *refs):
    lines, bundles = refs[:n_row], refs[n_row : n_row + n_plane]
    half_ref, panel_ref = refs[n_row + n_plane :]
    planes, mu, nu = bundles[0].shape
    row, plane = lax.axis_index("row"), plane_index()
    for k in range(n_plane):
        panel_ref[pl.ds(pl.multiple_of((plane ^ k) * mu, mu), mu), :] = bundles[k][planes - 1]
    for p in range(cut):
        total = jnp.zeros((mu, nu), jnp.float32)
        for k in range(n_row):
            at = pl.multiple_of((row ^ k) * nu, nu)
            total += dot(lines[k][p], panel_ref[pl.ds(at, nu), :])
        half_ref[:, p * nu : (p + 1) * nu] = total.astype(half_ref.dtype)


def half_of(lines, bundles):
    planes, mu, nu = lines[0].shape
    cut, n_row, n_plane = planes - 1, len(lines), len(bundles)
    kind = lines[0].dtype
    return pl.pallas_call(
        functools.partial(half_kernel, cut, n_row, n_plane),
        out_shape=(
            jax.ShapeDtypeStruct((mu, cut * nu), kind),
            jax.ShapeDtypeStruct((n_plane * mu, nu), kind),
        ),
        in_specs=[VMEM] * (n_row + n_plane),
        out_specs=[VMEM] * 2,
        compiler_params=pltpu.CompilerParams(vmem_limit_bytes=ROOM),
        cost_estimate=pl.CostEstimate(
            flops=2 * cut * mu * nu * nu * n_row, bytes_accessed=4 * n_row * cut * mu * nu, transcendentals=0
        ),
        name="half_product",
    )(*lines, *bundles)


def dress_kernel(n_row, n_plane, n_all, total_ao, weight_ref, panel_ref, line_ref, bundle_ref, *refs):
    halves, mixed = refs[:n_plane], refs[n_plane : n_plane + n_row]
    out_ref, share_ref = refs[n_plane + n_row :]
    mu, aux, nu = out_ref.shape
    cut = line_ref.shape[0] - 1
    row, plane = lax.axis_index("row"), plane_index()
    lanes = lax.broadcasted_iota(jnp.int32, share_ref.shape[1:], 1)
    share = jnp.zeros(share_ref.shape[1:], jnp.float32)
    for q in range(aux):
        total = jnp.zeros((mu, nu), jnp.float32)
        if q < cut:
            for k in range(n_plane):
                at = pl.multiple_of((plane ^ k) * mu, mu)
                total += dot(weight_ref[:, pl.ds(at, mu)], halves[k][:, q * nu : (q + 1) * nu])
        else:
            for k in range(n_row):
                at = pl.multiple_of((row ^ k) * nu, nu)
                total += dot(mixed[k][:, (q - cut) * nu : (q - cut + 1) * nu], panel_ref[pl.ds(at, nu), :])
        rounded = total.astype(out_ref.dtype)
        out_ref[:, q, :] = rounded
        wide = rounded.astype(jnp.float32) if q < cut else total
        for p in range(aux):
            block = line_ref[p] if p < cut else bundle_ref[p - cut]
            folded = jnp.sum((block.astype(jnp.float32) * wide).reshape(mu // 8, 8, nu), axis=0)
            own = jnp.sum(jnp.sum(folded, axis=0, keepdims=True), axis=1, keepdims=True) / total_ao
            share = jnp.where(lanes == p * aux + q, own, share)
    for i in range(n_all):
        share_ref[i] = share


def dress(weight, panel, line, bundle, halves, mixed, n_all):
    planes, mu, nu = line.shape
    aux = planes - 1 + bundle.shape[0] - 1
    n_row, n_plane = len(mixed), len(halves)
    return pl.pallas_call(
        functools.partial(dress_kernel, n_row, n_plane, n_all, weight.shape[1]),
        out_shape=(
            jax.ShapeDtypeStruct((mu, aux, nu), line.dtype),
            jax.ShapeDtypeStruct((n_all, 1, 128), jnp.float32),
        ),
        in_specs=[VMEM] * (4 + n_plane + n_row),
        out_specs=(VMEM, VMEM),
        compiler_params=pltpu.CompilerParams(vmem_limit_bytes=ROOM),
        cost_estimate=pl.CostEstimate(
            flops=2 * aux * mu * mu * nu * n_plane, bytes_accessed=4 * n_plane * aux * mu * nu, transcendentals=0
        ),
        name="dress",
    )(weight, panel, line, bundle, *halves, *mixed)


def finish_kernel(shares_ref, out_ref):
    aux = out_ref.shape[0]
    polar = jnp.sum(shares_ref[...], axis=0)
    for p in range(aux):
        out_ref[p : p + 1, :] = polar[:, p * aux : (p + 1) * aux]


def finish(shares, aux):
    return pl.pallas_call(
        finish_kernel,
        out_shape=jax.ShapeDtypeStruct((aux, aux), jnp.float32),
        in_specs=[VMEM],
        out_specs=VMEM,
        compiler_params=pltpu.CompilerParams(vmem_limit_bytes=ROOM),
        name="finish",
    )(shares)


def on_device(tensor_tiles, tile_pairs, tile_counts, occupied, virtual):
    aux = tensor_tiles.shape[1]
    n_row, n_plane = lax.axis_size("row"), lax.axis_size("col") * lax.axis_size("rep")
    near = list(range(2, n_plane, 2))
    sibling = lambda value: flip(value, PLANE, 1, n_plane)

    def gather_plane(value):
        return [value] + [flip(value, PLANE, k, n_plane) for k in near]

    def with_siblings(values):
        return [held for value in values for held in (value, sibling(value))]

    line, bundle = place(tile_pairs, tile_counts, tensor_tiles, occupied, virtual)
    far, step = {0: line}, n_row // 2
    while step > 1:
        far.update({k ^ step: flip(held, "row", step, n_row) for k, held in list(far.items())})
        step //= 2
    beside = flip(far.pop(0), "row", 1, n_row)
    pieces = {k: split(held) for k, held in far.items()}
    pieces.update({k ^ 1: [flip(piece, "row", 1, n_row) for piece in pieces[k]] for k in far})
    weights = [pieces[k][1] for k in range(2, n_row)]
    (beside, weights), bundles = after((beside, weights), gather_plane(bundle))
    bundles = with_siblings(bundles)

    mixed, weight = mix([line, beside] + weights, bundles)
    half, panel = half_of([line, beside] + [pieces[k][0] for k in range(2, n_row)], bundles)
    halves, mixed = with_siblings(gather_plane(half)), gather_row(mixed, n_row)
    dressed, shares = dress(weight, panel, line, bundle, halves, mixed, n_row * n_plane)
    polar = finish(lax.all_to_all(shares, EVERY, 0, 0), aux)
    return polar, dressed


def solution(mesh):
    return jax.shard_map(
        on_device,
        mesh=mesh,
        in_specs=(P(EVERY, None, None, None), P(EVERY), P(EVERY), P(PLANE, "row"), P(PLANE, "row")),
        out_specs=(P(), P(PLANE, None, "row")),
        check_vma=False,
    )
```

```python
import functools

import jax
import jax.numpy as jnp
from jax import lax
from jax.experimental import pallas as pl
from jax.experimental.pallas import tpu as pltpu
from jax.sharding import PartitionSpec as P

PLANE = ("col", "rep")
EVERY = ("row", "col", "rep")
VMEM = pl.BlockSpec(memory_space=pltpu.VMEM)
SMEM = pl.BlockSpec(memory_space=pltpu.SMEM)
ROOM = 48 << 20


def flip(value, axes, mask, count):
    return lax.ppermute(value, axes, [(i, i ^ mask) for i in range(count)])


def after(value, earlier):
    return lax.optimization_barrier((value, earlier))


def split_kernel(value_ref, block_ref, weight_ref):
    cut = block_ref.shape[0]
    block_ref[...] = value_ref[:cut]
    weight_ref[...] = value_ref[cut:]


def split(value):
    planes, mu, nu = value.shape
    return pl.pallas_call(
        split_kernel,
        out_shape=[jax.ShapeDtypeStruct((count, mu, nu), value.dtype) for count in (planes - 1, 1)],
        in_specs=[VMEM],
        out_specs=[VMEM, VMEM],
        compiler_params=pltpu.CompilerParams(vmem_limit_bytes=ROOM),
        cost_estimate=pl.CostEstimate(flops=0, bytes_accessed=4 * value.size, transcendentals=0),
        name="split",
    )(value)


def gather_row(value, n_row):
    found = {0: value}
    step = n_row // 2
    while step:
        found.update({k ^ step: flip(held, "row", step, n_row) for k, held in list(found.items())})
        step //= 2
    return [found[k] for k in range(n_row)]


def plane_index():
    return lax.axis_index("col") * lax.axis_size("rep") + lax.axis_index("rep")


def place_kernel(nu_tiles, counts_ref, pairs_any, tiles_any, weight_any, column_any, *refs):
    line_ref, bundle_ref, pairs_ref, tiles_ref, sems = refs
    slots, aux, tile, _ = tiles_ref.shape
    cut = line_ref.shape[0] - 1
    copies = [
        pltpu.make_async_copy(source, target, sems.at[i])
        for i, (source, target) in enumerate(
            [
                (tiles_any, tiles_ref),
                (pairs_any, pairs_ref),
                (weight_any, line_ref.at[cut]),
                (column_any, bundle_ref.at[aux - cut]),
            ]
        )
    ]
    for copy in copies:
        copy.start()
    for copy in copies:
        copy.wait()
    for t in range(slots):
        pair = pairs_ref[t]
        rows = pl.ds(pl.multiple_of(pair // nu_tiles * tile, tile), tile)
        cols = pl.ds(pl.multiple_of(pair % nu_tiles * tile, tile), tile)

        @pl.when(t < counts_ref[0])
        def _():
            line_ref[:cut, rows, cols] = tiles_ref[t, :cut]
            bundle_ref[: aux - cut, rows, cols] = tiles_ref[t, cut:]

        @pl.when(t >= counts_ref[0])
        def _():
            line_ref[:cut, rows, cols] = jnp.zeros((cut, tile, tile), line_ref.dtype)
            bundle_ref[: aux - cut, rows, cols] = jnp.zeros((aux - cut, tile, tile), line_ref.dtype)


def place(tile_pairs, tile_counts, tensor_tiles, weight, column):
    slots, aux, tile, _ = tensor_tiles.shape
    mu, nu = weight.shape
    cut = aux // 2
    stays = [
        pltpu.with_memory_space_constraint(value, pltpu.HBM) for value in (tile_pairs, tensor_tiles, weight, column)
    ]
    return pl.pallas_call(
        functools.partial(place_kernel, nu // tile),
        out_shape=[jax.ShapeDtypeStruct((count + 1, mu, nu), weight.dtype) for count in (cut, aux - cut)],
        in_specs=[SMEM] + [pl.BlockSpec(memory_space=pltpu.HBM)] * 4,
        out_specs=[VMEM, VMEM],
        scratch_shapes=[
            pltpu.SMEM(tile_pairs.shape, tile_pairs.dtype),
            pltpu.VMEM(tensor_tiles.shape, tensor_tiles.dtype),
            pltpu.SemaphoreType.DMA((4,)),
        ],
        compiler_params=pltpu.CompilerParams(vmem_limit_bytes=ROOM),
        cost_estimate=pl.CostEstimate(flops=0, bytes_accessed=6 * tensor_tiles.size, transcendentals=0),
        name="place",
    )(tile_counts, *stays)


def dot(left, right):
    return jnp.dot(left, right, preferred_element_type=jnp.float32)


def mix_kernel(n_row, n_plane, *refs):
    weights, bundles = refs[:n_row], refs[n_row : n_row + n_plane]
    mixed_ref, weight_ref = refs[n_row + n_plane :]
    _, mu, nu = weights[0].shape
    row, plane = lax.axis_index("row"), plane_index()
    for k, ref in enumerate(weights):
        weight_ref[:, pl.ds(pl.multiple_of((row ^ k) * nu, nu), nu)] = ref[ref.shape[0] - 1]
    for p in range(bundles[0].shape[0] - 1):
        total = jnp.zeros((mu, nu), jnp.float32)
        for k in range(n_plane):
            at = pl.multiple_of((plane ^ k) * mu, mu)
            total += dot(weight_ref[:, pl.ds(at, mu)], bundles[k][p])
        mixed_ref[:, p * nu : (p + 1) * nu] = total.astype(mixed_ref.dtype)


def mix(weights, bundles):
    planes, mu, nu = bundles[0].shape
    n_row, n_plane = len(weights), len(bundles)
    kind = weights[0].dtype
    return pl.pallas_call(
        functools.partial(mix_kernel, n_row, n_plane),
        out_shape=(
            jax.ShapeDtypeStruct((mu, (planes - 1) * nu), kind),
            jax.ShapeDtypeStruct((mu, n_row * nu), kind),
        ),
        in_specs=[VMEM] * (n_row + n_plane),
        out_specs=[VMEM] * 2,
        compiler_params=pltpu.CompilerParams(vmem_limit_bytes=ROOM),
        cost_estimate=pl.CostEstimate(
            flops=2 * planes * mu * nu * nu * n_row, bytes_accessed=4 * n_row * planes * mu * nu, transcendentals=0
        ),
        name="mix",
    )(*weights, *bundles)


def half_kernel(cut, n_row, n_plane, *refs):
    lines, bundles = refs[:n_row], refs[n_row : n_row + n_plane]
    half_ref, panel_ref = refs[n_row + n_plane :]
    planes, mu, nu = bundles[0].shape
    row, plane = lax.axis_index("row"), plane_index()
    for k in range(n_plane):
        panel_ref[pl.ds(pl.multiple_of((plane ^ k) * mu, mu), mu), :] = bundles[k][planes - 1]
    for p in range(cut):
        total = jnp.zeros((mu, nu), jnp.float32)
        for k in range(n_row):
            at = pl.multiple_of((row ^ k) * nu, nu)
            total += dot(lines[k][p], panel_ref[pl.ds(at, nu), :])
        half_ref[:, p * nu : (p + 1) * nu] = total.astype(half_ref.dtype)


def half_of(lines, bundles):
    planes, mu, nu = lines[0].shape
    cut, n_row, n_plane = planes - 1, len(lines), len(bundles)
    kind = lines[0].dtype
    return pl.pallas_call(
        functools.partial(half_kernel, cut, n_row, n_plane),
        out_shape=(
            jax.ShapeDtypeStruct((mu, cut * nu), kind),
            jax.ShapeDtypeStruct((n_plane * mu, nu), kind),
        ),
        in_specs=[VMEM] * (n_row + n_plane),
        out_specs=[VMEM] * 2,
        compiler_params=pltpu.CompilerParams(vmem_limit_bytes=ROOM),
        cost_estimate=pl.CostEstimate(
            flops=2 * cut * mu * nu * nu * n_row, bytes_accessed=4 * n_row * cut * mu * nu, transcendentals=0
        ),
        name="half_product",
    )(*lines, *bundles)


def late(n_row):
    return list(range(3, n_row, 2))


def near_kernel(n_row, n_plane, total_ao, weight_ref, panel_ref, line_ref, bundle_ref, *refs):
    halves, mixed = refs[:n_plane], refs[n_plane : -3]
    out_ref, part_ref, share_ref = refs[-3:]
    mu, aux, nu = out_ref.shape
    cut = line_ref.shape[0] - 1
    row, plane = lax.axis_index("row"), plane_index()
    share = jnp.zeros(share_ref.shape, jnp.float32)
    for q in range(cut):
        total = jnp.zeros((mu, nu), jnp.float32)
        for k in range(n_plane):
            at = pl.multiple_of((plane ^ k) * mu, mu)
            total += dot(weight_ref[:, pl.ds(at, mu)], halves[k][:, q * nu : (q + 1) * nu])
        rounded = total.astype(out_ref.dtype)
        out_ref[:, q, :] = rounded
        share = shares_with(share, line_ref, bundle_ref, q, rounded.astype(jnp.float32), total_ao)
    for q in range(cut, aux):
        total = jnp.zeros((mu, nu), jnp.float32)
        for k, ref in zip([k for k in range(n_row) if k not in late(n_row)], mixed):
            at = pl.multiple_of((row ^ k) * nu, nu)
            total += dot(ref[:, (q - cut) * nu : (q - cut + 1) * nu], panel_ref[pl.ds(at, nu), :])
        part_ref[q - cut] = total
        out_ref[:, q, :] = jnp.zeros((mu, nu), out_ref.dtype)
    share_ref[...] = share


def shares_with(share, line_ref, bundle_ref, q, dressed, total_ao):
    cut, rest = line_ref.shape[0] - 1, bundle_ref.shape[0] - 1
    mu, nu = dressed.shape
    lanes = lax.broadcasted_iota(jnp.int32, share.shape, 1)
    for p in range(cut + rest):
        block = line_ref[p] if p < cut else bundle_ref[p - cut]
        folded = jnp.sum((block.astype(jnp.float32) * dressed).reshape(mu // 8, 8, nu), axis=0)
        own = jnp.sum(jnp.sum(folded, axis=0, keepdims=True), axis=1, keepdims=True) / total_ao
        share = jnp.where(lanes == p * (cut + rest) + q, own, share)
    return share


def near(weight, panel, line, bundle, halves, mixed, n_row):
    planes, mu, nu = line.shape
    cut, rest, n_plane = planes - 1, bundle.shape[0] - 1, len(halves)
    return pl.pallas_call(
        functools.partial(near_kernel, n_row, n_plane, weight.shape[1]),
        out_shape=(
            jax.ShapeDtypeStruct((mu, cut + rest, nu), line.dtype),
            jax.ShapeDtypeStruct((rest, mu, nu), jnp.float32),
            jax.ShapeDtypeStruct((1, 128), jnp.float32),
        ),
        in_specs=[VMEM] * (4 + n_plane + len(mixed)),
        out_specs=[VMEM] * 3,
        compiler_params=pltpu.CompilerParams(vmem_limit_bytes=ROOM),
        cost_estimate=pl.CostEstimate(
            flops=2 * (cut + rest) * mu * mu * nu * n_plane,
            bytes_accessed=4 * n_plane * (cut + rest) * mu * nu,
            transcendentals=0,
        ),
        name="near",
    )(weight, panel, line, bundle, *halves, *mixed)


def dress_kernel(n_row, total_ao, panel_ref, line_ref, bundle_ref, known_ref, part_ref, begun_ref, *refs):
    mixed, (out_ref, share_ref) = refs[:-2], refs[-2:]
    aux, cut = out_ref.shape[1], line_ref.shape[0] - 1
    nu = out_ref.shape[2]
    row = lax.axis_index("row")
    out_ref[...] = known_ref[...]
    share = begun_ref[...]
    for q in range(cut, aux):
        total = part_ref[q - cut]
        for k, ref in zip(late(n_row), mixed):
            at = pl.multiple_of((row ^ k) * nu, nu)
            total += dot(ref[:, (q - cut) * nu : (q - cut + 1) * nu], panel_ref[pl.ds(at, nu), :])
        out_ref[:, q, :] = total.astype(out_ref.dtype)
        share = shares_with(share, line_ref, bundle_ref, q, total, total_ao)
    for i in range(share_ref.shape[0]):
        share_ref[i] = share


def dress(panel, line, bundle, known, part, begun, mixed, n_row, n_all):
    mu, aux, nu = known.shape
    return pl.pallas_call(
        functools.partial(dress_kernel, n_row, panel.shape[0]),
        out_shape=(
            jax.ShapeDtypeStruct(known.shape, known.dtype),
            jax.ShapeDtypeStruct((n_all, 1, 128), jnp.float32),
        ),
        in_specs=[VMEM] * (6 + len(mixed)),
        out_specs=(VMEM, VMEM),
        compiler_params=pltpu.CompilerParams(vmem_limit_bytes=ROOM),
        cost_estimate=pl.CostEstimate(flops=2 * mu * nu * nu * aux, bytes_accessed=8 * mu * aux * nu, transcendentals=0),
        name="dress",
    )(panel, line, bundle, known, part, begun, *mixed)


def finish_kernel(shares_ref, out_ref):
    aux = out_ref.shape[0]
    polar = jnp.sum(shares_ref[...], axis=0)
    for p in range(aux):
        out_ref[p : p + 1, :] = polar[:, p * aux : (p + 1) * aux]


def finish(shares, aux):
    return pl.pallas_call(
        finish_kernel,
        out_shape=jax.ShapeDtypeStruct((aux, aux), jnp.float32),
        in_specs=[VMEM],
        out_specs=VMEM,
        compiler_params=pltpu.CompilerParams(vmem_limit_bytes=ROOM),
        name="finish",
    )(shares)


def on_device(tensor_tiles, tile_pairs, tile_counts, occupied, virtual):
    aux = tensor_tiles.shape[1]
    n_row, n_plane = lax.axis_size("row"), lax.axis_size("col") * lax.axis_size("rep")
    chips = list(range(2, n_plane, 2))
    sibling = lambda value: flip(value, PLANE, 1, n_plane)

    def gather_plane(value):
        return [value] + [flip(value, PLANE, k, n_plane) for k in chips]

    def with_siblings(values):
        return [held for value in values for held in (value, sibling(value))]

    line, bundle = place(tile_pairs, tile_counts, tensor_tiles, occupied, virtual)
    far, step = {0: line}, n_row // 2
    while step > 1:
        far.update({k ^ step: flip(held, "row", step, n_row) for k, held in list(far.items())})
        step //= 2
    beside = flip(far.pop(0), "row", 1, n_row)
    pieces = {k: split(held) for k, held in far.items()}
    pieces.update({k ^ 1: [flip(piece, "row", 1, n_row) for piece in pieces[k]] for k in far})
    weights = [pieces[k][1] for k in range(2, n_row)]
    (beside, weights), bundles = after((beside, weights), gather_plane(bundle))
    bundles = with_siblings(bundles)

    mixed, weight = mix([line, beside] + weights, bundles)
    half, panel = half_of([line, beside] + [pieces[k][0] for k in range(2, n_row)], bundles)
    halves, mixed = with_siblings(gather_plane(half)), gather_row(mixed, n_row)
    early = [mixed[k] for k in range(n_row) if k not in late(n_row)]
    known = near(weight, panel, line, bundle, halves, early, n_row)
    last = [mixed[k] for k in late(n_row)]
    dressed, shares = dress(panel, line, bundle, *known, last, n_row, n_row * n_plane)
    polar = finish(lax.all_to_all(shares, EVERY, 0, 0), aux)
    return polar, dressed


def solution(mesh):
    return jax.shard_map(
        on_device,
        mesh=mesh,
        in_specs=(P(EVERY, None, None, None), P(EVERY), P(EVERY), P(PLANE, "row"), P(PLANE, "row")),
        out_specs=(P(), P(PLANE, None, "row")),
        check_vma=False,
    )
```

```python
import functools

import jax
import jax.numpy as jnp
from jax import lax
from jax.experimental import pallas as pl
from jax.experimental.pallas import tpu as pltpu
from jax.sharding import PartitionSpec as P

PLANE = ("col", "rep")
EVERY = ("row", "col", "rep")
VMEM = pl.BlockSpec(memory_space=pltpu.VMEM)
SMEM = pl.BlockSpec(memory_space=pltpu.SMEM)
ROOM = 48 << 20


def flip(value, axes, mask, count):
    return lax.ppermute(value, axes, [(i, i ^ mask) for i in range(count)])


def after(value, earlier):
    return lax.optimization_barrier((value, earlier))


def gather_row(value, n_row):
    found = {0: value}
    step = n_row // 2
    while step:
        found.update({k ^ step: flip(held, "row", step, n_row) for k, held in list(found.items())})
        step //= 2
    return [found[k] for k in range(n_row)]


def plane_index():
    return lax.axis_index("col") * lax.axis_size("rep") + lax.axis_index("rep")


def place_kernel(nu_tiles, counts_ref, pairs_any, tiles_any, weight_any, column_any, *refs):
    line_ref, bundle_ref, pairs_ref, tiles_ref, sems = refs
    slots, aux, tile, _ = tiles_ref.shape
    copies = [
        pltpu.make_async_copy(source, target, sems.at[i])
        for i, (source, target) in enumerate(
            [
                (tiles_any, tiles_ref),
                (pairs_any, pairs_ref),
                (weight_any, line_ref.at[aux]),
                (column_any, bundle_ref.at[aux]),
            ]
        )
    ]
    for copy in copies:
        copy.start()
    for copy in copies:
        copy.wait()
    for t in range(slots):
        pair = pairs_ref[t]
        rows = pl.ds(pl.multiple_of(pair // nu_tiles * tile, tile), tile)
        cols = pl.ds(pl.multiple_of(pair % nu_tiles * tile, tile), tile)

        @pl.when(t < counts_ref[0])
        def _():
            for out_ref in (line_ref, bundle_ref):
                out_ref[:aux, rows, cols] = tiles_ref[t]

        @pl.when(t >= counts_ref[0])
        def _():
            for out_ref in (line_ref, bundle_ref):
                out_ref[:aux, rows, cols] = jnp.zeros((aux, tile, tile), out_ref.dtype)


def place(tile_pairs, tile_counts, tensor_tiles, weight, column):
    slots, aux, tile, _ = tensor_tiles.shape
    mu, nu = weight.shape
    shape = jax.ShapeDtypeStruct((aux + 1, mu, nu), weight.dtype)
    stays = [pltpu.with_memory_space_constraint(value, pltpu.HBM) for value in (tile_pairs, tensor_tiles, weight, column)]
    return pl.pallas_call(
        functools.partial(place_kernel, nu // tile),
        out_shape=(shape, shape),
        in_specs=[SMEM] + [pl.BlockSpec(memory_space=pltpu.HBM)] * 4,
        out_specs=(VMEM, VMEM),
        scratch_shapes=[
            pltpu.SMEM(tile_pairs.shape, tile_pairs.dtype),
            pltpu.VMEM(tensor_tiles.shape, tensor_tiles.dtype),
            pltpu.SemaphoreType.DMA((4,)),
        ],
        compiler_params=pltpu.CompilerParams(vmem_limit_bytes=ROOM),
        cost_estimate=pl.CostEstimate(flops=0, bytes_accessed=6 * tensor_tiles.size, transcendentals=0),
        name="place",
    )(tile_counts, *stays)


def half_kernel(n_row, n_plane, *refs):
    lines, bundles = refs[:n_row], refs[n_row : n_row + n_plane]
    out_ref, panel = refs[n_row + n_plane :]
    planes, mu, nu = lines[0].shape
    aux = planes - 1
    row, plane = lax.axis_index("row"), plane_index()
    for k in range(n_plane):
        panel[pl.ds(pl.multiple_of((plane ^ k) * mu, mu), mu), :] = bundles[k][aux]
    for p in range(aux):
        total = jnp.zeros((mu, nu), jnp.float32)
        for k in range(n_row):
            at = pl.multiple_of((row ^ k) * nu, nu)
            total += jnp.dot(lines[k][p], panel[pl.ds(at, nu), :], preferred_element_type=jnp.float32)
        out_ref[:, p * nu : (p + 1) * nu] = total.astype(out_ref.dtype)


def half(lines, bundles):
    planes, mu, nu = lines[0].shape
    aux = planes - 1
    n_row, n_plane = len(lines), len(bundles)
    kind = lines[0].dtype
    return pl.pallas_call(
        functools.partial(half_kernel, n_row, n_plane),
        out_shape=jax.ShapeDtypeStruct((mu, aux * nu), kind),
        in_specs=[VMEM] * (n_row + n_plane),
        out_specs=VMEM,
        scratch_shapes=[pltpu.VMEM((n_plane * mu, nu), kind)],
        compiler_params=pltpu.CompilerParams(vmem_limit_bytes=ROOM),
        cost_estimate=pl.CostEstimate(
            flops=2 * aux * mu * nu * nu * n_row, bytes_accessed=4 * n_row * aux * mu * nu, transcendentals=0
        ),
        name="half_product",
    )(*lines, *bundles)


def share_kernel(n_row, n_plane, half_ref, *refs):
    weights, bundles = refs[:n_row], refs[n_row : n_row + n_plane]
    weight_ref, share_ref = refs[n_row + n_plane :]
    planes, mu, nu = weights[0].shape
    aux = planes - 1
    row, plane = lax.axis_index("row"), plane_index()
    lanes = lax.broadcasted_iota(jnp.int32, share_ref.shape[1:], 1)
    share = jnp.zeros(share_ref.shape[1:], jnp.float32)
    for k in range(n_row):
        weight_ref[:, pl.ds(pl.multiple_of((row ^ k) * nu, nu), nu)] = weights[k][weights[k].shape[0] - 1]
    for p in range(aux):
        mixed = jnp.zeros((mu, nu), jnp.float32)
        for k in range(n_plane):
            at = pl.multiple_of((plane ^ k) * mu, mu)
            mixed += jnp.dot(weight_ref[:, pl.ds(at, mu)], bundles[k][p], preferred_element_type=jnp.float32)
        for q in range(aux):
            product = mixed * half_ref[:, q * nu : (q + 1) * nu].astype(jnp.float32)
            folded = jnp.sum(product.reshape(mu // 8, 8, nu), axis=0)
            own = jnp.sum(jnp.sum(folded, axis=0, keepdims=True), axis=1, keepdims=True)
            share = jnp.where(lanes == p * aux + q, own, share)
    for i in range(n_row * n_plane):
        share_ref[i] = share


def share_of(half_block, weights, bundles):
    planes, mu, nu = weights[0].shape
    aux, n_row, n_plane = planes - 1, len(weights), len(bundles)
    return pl.pallas_call(
        functools.partial(share_kernel, n_row, n_plane),
        out_shape=(
            jax.ShapeDtypeStruct((mu, n_row * nu), weights[0].dtype),
            jax.ShapeDtypeStruct((n_row * n_plane, 1, 128), jnp.float32),
        ),
        in_specs=[VMEM] * (1 + n_row + n_plane),
        out_specs=(VMEM, VMEM),
        compiler_params=pltpu.CompilerParams(vmem_limit_bytes=ROOM),
        cost_estimate=pl.CostEstimate(
            flops=2 * aux * mu * mu * nu * n_plane, bytes_accessed=4 * n_plane * aux * mu * nu, transcendentals=0
        ),
        name="polar_share",
    )(half_block, *weights, *bundles)


def near_kernel(places, total_ao, weight_ref, shares_ref, *refs):
    halves, (part_ref, polar_ref) = refs[:-2], refs[-2:]
    aux, mu, nu = part_ref.shape
    plane = plane_index()
    for q in range(aux):
        total = jnp.zeros((mu, nu), jnp.float32)
        for k, ref in zip(places, halves):
            total += jnp.dot(
                weight_ref[:, pl.ds(pl.multiple_of((plane ^ k) * mu, mu), mu)],
                ref[:, q * nu : (q + 1) * nu],
                preferred_element_type=jnp.float32,
            )
        part_ref[q] = total
    polar = jnp.sum(shares_ref[...], axis=0) / total_ao
    for p in range(aux):
        polar_ref[p : p + 1, :] = polar[:, p * aux : (p + 1) * aux]


def near(weight, halves, shares, aux, total_ao):
    mu, width = halves[0].shape
    return pl.pallas_call(
        functools.partial(near_kernel, list(halves), total_ao),
        out_shape=(
            jax.ShapeDtypeStruct((aux, mu, width // aux), jnp.float32),
            jax.ShapeDtypeStruct((aux, aux), jnp.float32),
        ),
        in_specs=[VMEM] * (2 + len(halves)),
        out_specs=(VMEM, VMEM),
        compiler_params=pltpu.CompilerParams(vmem_limit_bytes=ROOM),
        cost_estimate=pl.CostEstimate(
            flops=2 * mu * mu * width * len(halves), bytes_accessed=4 * len(halves) * mu * width, transcendentals=0
        ),
        name="near",
    )(weight, shares, *halves.values())


def dress_kernel(places, weight_ref, part_ref, *refs):
    halves, out_ref = refs[:-1], refs[-1]
    mu, aux, nu = out_ref.shape
    plane = plane_index()
    for q in range(aux):
        total = part_ref[q]
        for k, ref in zip(places, halves):
            total += jnp.dot(
                weight_ref[:, pl.ds(pl.multiple_of((plane ^ k) * mu, mu), mu)],
                ref[:, q * nu : (q + 1) * nu],
                preferred_element_type=jnp.float32,
            )
        out_ref[:, q, :] = total.astype(out_ref.dtype)


def dress(weight, part, halves):
    aux, mu, nu = part.shape
    return pl.pallas_call(
        functools.partial(dress_kernel, list(halves)),
        out_shape=jax.ShapeDtypeStruct((mu, aux, nu), weight.dtype),
        in_specs=[VMEM] * (2 + len(halves)),
        out_specs=VMEM,
        compiler_params=pltpu.CompilerParams(vmem_limit_bytes=ROOM),
        cost_estimate=pl.CostEstimate(
            flops=2 * aux * mu * mu * nu * len(halves),
            bytes_accessed=4 * len(halves) * aux * mu * nu,
            transcendentals=0,
        ),
        name="dress",
    )(weight, part, *halves.values())


def on_device(tensor_tiles, tile_pairs, tile_counts, occupied, virtual):
    aux = tensor_tiles.shape[1]
    nu = virtual.shape[1]
    n_row, n_plane = lax.axis_size("row"), lax.axis_size("col") * lax.axis_size("rep")
    near_chips = list(range(2, n_plane, 2))
    sibling = lambda value: flip(value, PLANE, 1, n_plane)

    line, bundle = place(tile_pairs, tile_counts, tensor_tiles, occupied, virtual)
    lines = gather_row(line, n_row)
    bundles = []
    for value in [bundle] + [flip(bundle, PLANE, k, n_plane) for k in near_chips]:
        bundles += [value, sibling(value)]
    own = half(lines, bundles)

    arrivals = [flip(own, PLANE, k, n_plane) for k in near_chips]
    other = sibling(own)
    weight, share = share_of(own, lines, bundles)
    shares, (other, arrivals) = after(lax.all_to_all(share, EVERY, 0, 0), (other, arrivals))
    here = {0: own, 1: other, **dict(zip(near_chips, arrivals))}
    part, polar = near(weight, here, shares, aux, n_row * nu)
    dressed = dress(weight, part, {k ^ 1: sibling(here[k]) for k in near_chips})
    return polar, dressed


def solution(mesh):
    return jax.shard_map(
        on_device,
        mesh=mesh,
        in_specs=(P(EVERY, None, None, None), P(EVERY), P(EVERY), P(PLANE, "row"), P(PLANE, "row")),
        out_specs=(P(), P(PLANE, None, "row")),
        check_vma=False,
    )
```

```python
import functools

import jax
import jax.numpy as jnp
from jax import lax
from jax.experimental import pallas as pl
from jax.experimental.pallas import tpu as pltpu
from jax.sharding import PartitionSpec as P

PLANE = ("col", "rep")
EVERY = ("row", "col", "rep")
VMEM = pl.BlockSpec(memory_space=pltpu.VMEM)
SMEM = pl.BlockSpec(memory_space=pltpu.SMEM)
ROOM = 48 << 20


def flip(value, axes, mask, count):
    return lax.ppermute(value, axes, [(i, i ^ mask) for i in range(count)])


def after(value, earlier):
    return lax.optimization_barrier((value, earlier))


def gather_row(value, n_row):
    found = {0: value}
    step = n_row // 2
    while step:
        found.update({k ^ step: flip(held, "row", step, n_row) for k, held in list(found.items())})
        step //= 2
    return [found[k] for k in range(n_row)]


def late(n_row):
    return list(range(3, n_row, 2))


def plane_index():
    return lax.axis_index("col") * lax.axis_size("rep") + lax.axis_index("rep")


def place_kernel(nu_tiles, counts_ref, pairs_any, tiles_any, weight_any, column_any, *refs):
    line_ref, bundle_ref, pairs_ref, tiles_ref, sems = refs
    slots, aux, tile, _ = tiles_ref.shape
    cut = line_ref.shape[0] - 1
    copies = [
        pltpu.make_async_copy(source, target, sems.at[i])
        for i, (source, target) in enumerate(
            [
                (tiles_any, tiles_ref),
                (pairs_any, pairs_ref),
                (weight_any, line_ref.at[cut]),
                (column_any, bundle_ref.at[aux - cut]),
            ]
        )
    ]
    for copy in copies:
        copy.start()
    for copy in copies:
        copy.wait()
    for t in range(slots):
        pair = pairs_ref[t]
        rows = pl.ds(pl.multiple_of(pair // nu_tiles * tile, tile), tile)
        cols = pl.ds(pl.multiple_of(pair % nu_tiles * tile, tile), tile)

        @pl.when(t < counts_ref[0])
        def _():
            line_ref[:cut, rows, cols] = tiles_ref[t, :cut]
            bundle_ref[: aux - cut, rows, cols] = tiles_ref[t, cut:]

        @pl.when(t >= counts_ref[0])
        def _():
            line_ref[:cut, rows, cols] = jnp.zeros((cut, tile, tile), line_ref.dtype)
            bundle_ref[: aux - cut, rows, cols] = jnp.zeros((aux - cut, tile, tile), line_ref.dtype)


def place(tile_pairs, tile_counts, tensor_tiles, weight, column):
    slots, aux, tile, _ = tensor_tiles.shape
    mu, nu = weight.shape
    cut = aux // 2
    stays = [
        pltpu.with_memory_space_constraint(value, pltpu.HBM) for value in (tile_pairs, tensor_tiles, weight, column)
    ]
    return pl.pallas_call(
        functools.partial(place_kernel, nu // tile),
        out_shape=[jax.ShapeDtypeStruct((count + 1, mu, nu), weight.dtype) for count in (cut, aux - cut)],
        in_specs=[SMEM] + [pl.BlockSpec(memory_space=pltpu.HBM)] * 4,
        out_specs=[VMEM, VMEM],
        scratch_shapes=[
            pltpu.SMEM(tile_pairs.shape, tile_pairs.dtype),
            pltpu.VMEM(tensor_tiles.shape, tensor_tiles.dtype),
            pltpu.SemaphoreType.DMA((4,)),
        ],
        compiler_params=pltpu.CompilerParams(vmem_limit_bytes=ROOM),
        cost_estimate=pl.CostEstimate(flops=0, bytes_accessed=6 * tensor_tiles.size, transcendentals=0),
        name="place",
    )(tile_counts, *stays)


def dot(left, right):
    return jnp.dot(left, right, preferred_element_type=jnp.float32)


def mix_kernel(n_row, n_plane, *refs):
    lines, bundles = refs[:n_row], refs[n_row : n_row + n_plane]
    half_ref, mixed_ref, both_ref, weight_ref, panel_ref = refs[n_row + n_plane :]
    planes, mu, nu = lines[0].shape
    cut, rest = planes - 1, bundles[0].shape[0] - 1
    row, plane = lax.axis_index("row"), plane_index()
    for k in range(n_plane):
        panel_ref[pl.ds(pl.multiple_of((plane ^ k) * mu, mu), mu), :] = bundles[k][rest]
    for k in range(n_row):
        weight_ref[:, pl.ds(pl.multiple_of((row ^ k) * nu, nu), nu)] = lines[k][cut]
    for p in range(cut):
        total = jnp.zeros((mu, nu), jnp.float32)
        for k in range(n_row):
            at = pl.multiple_of((row ^ k) * nu, nu)
            total += dot(lines[k][p], panel_ref[pl.ds(at, nu), :])
        half_ref[:, p * nu : (p + 1) * nu] = total.astype(half_ref.dtype)
    for p in range(rest):
        total = jnp.zeros((mu, nu), jnp.float32)
        for k in range(n_plane):
            at = pl.multiple_of((plane ^ k) * mu, mu)
            total += dot(weight_ref[:, pl.ds(at, mu)], bundles[k][p])
        mixed_ref[:, p * nu : (p + 1) * nu] = total.astype(mixed_ref.dtype)
        both_ref[:, p * nu : (p + 1) * nu] = total.astype(both_ref.dtype)
        for i, k in enumerate(late(n_row)):
            at = pl.multiple_of((row ^ k) * nu, nu)
            turned = lax.dot_general(
                bundles[0][p], panel_ref[pl.ds(at, nu), :], (((1,), (1,)), ((), ())), preferred_element_type=jnp.float32
            )
            place_at = ((i + 1) * rest + p) * nu
            both_ref[:, place_at : place_at + nu] = turned.astype(both_ref.dtype)


def mix(lines, bundles):
    planes, mu, nu = lines[0].shape
    cut, rest = planes - 1, bundles[0].shape[0] - 1
    n_row, n_plane = len(lines), len(bundles)
    kind = lines[0].dtype
    return pl.pallas_call(
        functools.partial(mix_kernel, n_row, n_plane),
        out_shape=(
            jax.ShapeDtypeStruct((mu, cut * nu), kind),
            jax.ShapeDtypeStruct((mu, rest * nu), kind),
            jax.ShapeDtypeStruct((mu, (1 + len(late(n_row))) * rest * nu), kind),
            jax.ShapeDtypeStruct((mu, n_row * nu), kind),
            jax.ShapeDtypeStruct((n_plane * mu, nu), kind),
        ),
        in_specs=[VMEM] * (n_row + n_plane),
        out_specs=[VMEM] * 5,
        compiler_params=pltpu.CompilerParams(vmem_limit_bytes=ROOM),
        cost_estimate=pl.CostEstimate(
            flops=2 * (cut + rest) * mu * nu * nu * n_row,
            bytes_accessed=4 * n_row * (cut + rest) * mu * nu,
            transcendentals=0,
        ),
        name="mix",
    )(*lines, *bundles)


def share_kernel(n_row, n_plane, weight_ref, panel_ref, line_ref, bundle_ref, near_ref, *refs):
    halves, far = refs[:n_plane], refs[n_plane : n_plane + n_row // 2]
    first_ref, part_ref, share_ref = refs[n_plane + n_row // 2 :]
    cut, mu, nu = first_ref.shape
    rest = part_ref.shape[0]
    aux = cut + rest
    row, plane = lax.axis_index("row"), plane_index()
    known = {2 * i: ref for i, ref in enumerate(far)}
    known[1] = near_ref

    def product(left, right):
        folded = jnp.sum((left.astype(jnp.float32) * right).reshape(mu // 8, 8, nu), axis=0)
        return sum([folded[:, i : i + 128] for i in range(128, nu, 128)], folded[:, :128])

    lanes = lax.broadcasted_iota(jnp.int32, share_ref.shape[1:], 1)
    shares = [jnp.zeros(share_ref.shape[1:], jnp.float32)]

    def store(p, q, value):
        total = jnp.sum(jnp.sum(value, axis=0, keepdims=True), axis=1, keepdims=True)
        shares[0] = jnp.where(lanes == p * aux + q, total, shares[0])

    for q in range(cut):
        total = jnp.zeros((mu, nu), jnp.float32)
        for k in range(n_plane):
            at = pl.multiple_of((plane ^ k) * mu, mu)
            total += dot(weight_ref[:, pl.ds(at, mu)], halves[k][:, q * nu : (q + 1) * nu])
        rounded = total.astype(first_ref.dtype)
        first_ref[q] = rounded
        for p in range(aux):
            value = product(line_ref[p] if p < cut else bundle_ref[p - cut], rounded.astype(jnp.float32))
            store(p, q, value)
            if p >= cut:
                store(q, p, value)
    for q in range(rest):
        total = jnp.zeros((mu, nu), jnp.float32)
        for k, ref in known.items():
            at = pl.multiple_of((row ^ k) * nu, nu)
            total += dot(ref[:, q * nu : (q + 1) * nu], panel_ref[pl.ds(at, nu), :])
        part_ref[q] = total
        for p in range(rest):
            value = product(bundle_ref[p], total)
            for i, k in enumerate(late(n_row)):
                at = ((i + 1) * rest + p) * nu
                other = known[k ^ 1][:, q * nu : (q + 1) * nu]
                value += product(near_ref[:, at : at + nu], other.astype(jnp.float32))
            store(cut + p, cut + q, value)
    for i in range(share_ref.shape[0]):
        share_ref[i] = shares[0]


def share_of(weight, panel, line, bundle, near, halves, far):
    planes, mu, nu = line.shape
    cut, rest = planes - 1, bundle.shape[0] - 1
    n_row, n_plane = 2 * len(far), len(halves)
    return pl.pallas_call(
        functools.partial(share_kernel, n_row, n_plane),
        out_shape=(
            jax.ShapeDtypeStruct((cut, mu, nu), line.dtype),
            jax.ShapeDtypeStruct((rest, mu, nu), jnp.float32),
            jax.ShapeDtypeStruct((n_row * n_plane, 1, 128), jnp.float32),
        ),
        in_specs=[VMEM] * (5 + n_plane + len(far)),
        out_specs=[VMEM] * 3,
        compiler_params=pltpu.CompilerParams(vmem_limit_bytes=ROOM),
        cost_estimate=pl.CostEstimate(
            flops=2 * (cut + rest) * mu * mu * nu * n_plane,
            bytes_accessed=4 * n_plane * (cut + rest) * mu * nu,
            transcendentals=0,
        ),
        name="polar_share",
    )(weight, panel, line, bundle, near, *halves, *far)


def dress_kernel(n_row, panel_ref, first_ref, part_ref, shares_ref, *refs):
    blocks, (out_ref, polar_ref) = refs[:-2], refs[-2:]
    cut, _, nu = first_ref.shape
    row = lax.axis_index("row")
    for q in range(cut):
        out_ref[:, q, :] = first_ref[q]
    for q in range(part_ref.shape[0]):
        total = part_ref[q]
        for k, ref in zip(late(n_row), blocks):
            at = pl.multiple_of((row ^ k) * nu, nu)
            total += dot(ref[:, q * nu : (q + 1) * nu], panel_ref[pl.ds(at, nu), :])
        out_ref[:, cut + q, :] = total.astype(out_ref.dtype)
    aux = polar_ref.shape[0]
    polar = jnp.sum(shares_ref[...], axis=0) / panel_ref.shape[0]
    for p in range(aux):
        polar_ref[p : p + 1, :] = polar[:, p * aux : (p + 1) * aux]


def dress(panel, first, part, shares, blocks, n_row):
    cut, mu, nu = first.shape
    aux = cut + part.shape[0]
    return pl.pallas_call(
        functools.partial(dress_kernel, n_row),
        out_shape=(
            jax.ShapeDtypeStruct((mu, aux, nu), first.dtype),
            jax.ShapeDtypeStruct((aux, aux), jnp.float32),
        ),
        in_specs=[VMEM] * (4 + len(blocks)),
        out_specs=(VMEM, VMEM),
        compiler_params=pltpu.CompilerParams(vmem_limit_bytes=ROOM),
        cost_estimate=pl.CostEstimate(flops=2 * mu * nu * nu * aux, bytes_accessed=8 * mu * aux * nu, transcendentals=0),
        name="dress",
    )(panel, first, part, shares, *blocks)


def on_device(tensor_tiles, tile_pairs, tile_counts, occupied, virtual):
    aux = tensor_tiles.shape[1]
    n_row, n_plane = lax.axis_size("row"), lax.axis_size("col") * lax.axis_size("rep")
    near = list(range(2, n_plane, 2))
    sibling = lambda value: flip(value, PLANE, 1, n_plane)

    def gather_plane(value):
        values = [value] + [flip(value, PLANE, k, n_plane) for k in near]
        return [held for value in values for held in (value, sibling(value))]

    line, bundle = place(tile_pairs, tile_counts, tensor_tiles, occupied, virtual)
    half, mixed, both, weight, panel = mix(gather_row(line, n_row), gather_plane(bundle))
    far = {0: mixed}
    step = n_row // 2
    while step > 1:
        far.update({k ^ step: flip(held, "row", step, n_row) for k, held in list(far.items())})
        step //= 2
    beside = flip(both, "row", 1, n_row)
    sources, beside = after([far[k ^ 1] for k in late(n_row)], beside)
    blocks = [flip(held, "row", 1, n_row) for held in sources]
    first, part, share = share_of(
        weight, panel, line, bundle, beside, gather_plane(half), [far[k] for k in range(0, n_row, 2)]
    )
    dressed, polar = dress(panel, first, part, lax.all_to_all(share, EVERY, 0, 0), blocks, n_row)
    return polar, dressed


def solution(mesh):
    return jax.shard_map(
        on_device,
        mesh=mesh,
        in_specs=(P(EVERY, None, None, None), P(EVERY), P(EVERY), P(PLANE, "row"), P(PLANE, "row")),
        out_specs=(P(), P(PLANE, None, "row")),
        check_vma=False,
    )
```

```python
import functools

import jax
import jax.numpy as jnp
from jax import lax
from jax.experimental import pallas as pl
from jax.experimental.pallas import tpu as pltpu
from jax.sharding import PartitionSpec as P

PLANE = ("col", "rep")
EVERY = ("row", "col", "rep")
VMEM = pl.BlockSpec(memory_space=pltpu.VMEM)
SMEM = pl.BlockSpec(memory_space=pltpu.SMEM)
ROOM = 48 << 20


def flip(value, axes, mask, count):
    return lax.ppermute(value, axes, [(i, i ^ mask) for i in range(count)])


def after(value, earlier):
    return lax.optimization_barrier((value, earlier))


def gather_row(value, n_row):
    found = {0: value}
    step = n_row // 2
    while step:
        found.update({k ^ step: flip(held, "row", step, n_row) for k, held in list(found.items())})
        step //= 2
    return [found[k] for k in range(n_row)]


def late(n_row):
    return list(range(3, n_row, 2))


def plane_index():
    return lax.axis_index("col") * lax.axis_size("rep") + lax.axis_index("rep")


def place_kernel(nu_tiles, counts_ref, pairs_any, tiles_any, weight_any, column_any, *refs):
    line_ref, bundle_ref, pairs_ref, tiles_ref, sems = refs
    slots, aux, tile, _ = tiles_ref.shape
    cut = line_ref.shape[0] - 1
    copies = [
        pltpu.make_async_copy(source, target, sems.at[i])
        for i, (source, target) in enumerate(
            [
                (tiles_any, tiles_ref),
                (pairs_any, pairs_ref),
                (weight_any, line_ref.at[cut]),
                (column_any, bundle_ref.at[aux - cut]),
            ]
        )
    ]
    for copy in copies:
        copy.start()
    for copy in copies:
        copy.wait()
    for t in range(slots):
        pair = pairs_ref[t]
        rows = pl.ds(pl.multiple_of(pair // nu_tiles * tile, tile), tile)
        cols = pl.ds(pl.multiple_of(pair % nu_tiles * tile, tile), tile)

        @pl.when(t < counts_ref[0])
        def _():
            line_ref[:cut, rows, cols] = tiles_ref[t, :cut]
            bundle_ref[: aux - cut, rows, cols] = tiles_ref[t, cut:]

        @pl.when(t >= counts_ref[0])
        def _():
            line_ref[:cut, rows, cols] = jnp.zeros((cut, tile, tile), line_ref.dtype)
            bundle_ref[: aux - cut, rows, cols] = jnp.zeros((aux - cut, tile, tile), line_ref.dtype)


def place(tile_pairs, tile_counts, tensor_tiles, weight, column):
    slots, aux, tile, _ = tensor_tiles.shape
    mu, nu = weight.shape
    cut = aux // 2
    stays = [
        pltpu.with_memory_space_constraint(value, pltpu.HBM) for value in (tile_pairs, tensor_tiles, weight, column)
    ]
    return pl.pallas_call(
        functools.partial(place_kernel, nu // tile),
        out_shape=[jax.ShapeDtypeStruct((count + 1, mu, nu), weight.dtype) for count in (cut, aux - cut)],
        in_specs=[SMEM] + [pl.BlockSpec(memory_space=pltpu.HBM)] * 4,
        out_specs=[VMEM, VMEM],
        scratch_shapes=[
            pltpu.SMEM(tile_pairs.shape, tile_pairs.dtype),
            pltpu.VMEM(tensor_tiles.shape, tensor_tiles.dtype),
            pltpu.SemaphoreType.DMA((4,)),
        ],
        compiler_params=pltpu.CompilerParams(vmem_limit_bytes=ROOM),
        cost_estimate=pl.CostEstimate(flops=0, bytes_accessed=6 * tensor_tiles.size, transcendentals=0),
        name="place",
    )(tile_counts, *stays)


def dot(left, right):
    return jnp.dot(left, right, preferred_element_type=jnp.float32)


def mix_kernel(n_row, n_plane, *refs):
    lines, bundles = refs[:n_row], refs[n_row : n_row + n_plane]
    half_ref, mixed_ref, both_ref, weight_ref, panel_ref, begun_ref = refs[n_row + n_plane :]
    planes, mu, nu = lines[0].shape
    cut, rest = planes - 1, bundles[0].shape[0] - 1
    row, plane = lax.axis_index("row"), plane_index()
    for k in range(n_plane):
        panel_ref[pl.ds(pl.multiple_of((plane ^ k) * mu, mu), mu), :] = bundles[k][rest]
    for k in range(n_row):
        weight_ref[:, pl.ds(pl.multiple_of((row ^ k) * nu, nu), nu)] = lines[k][cut]
    halves = []
    for p in range(cut):
        total = jnp.zeros((mu, nu), jnp.float32)
        for k in range(n_row):
            at = pl.multiple_of((row ^ k) * nu, nu)
            total += dot(lines[k][p], panel_ref[pl.ds(at, nu), :])
        half_ref[:, p * nu : (p + 1) * nu] = total.astype(half_ref.dtype)
        halves.append(total)
    lanes = lax.broadcasted_iota(jnp.int32, begun_ref.shape, 1)
    begun = jnp.zeros(begun_ref.shape, jnp.float32)
    for p in range(rest):
        total = jnp.zeros((mu, nu), jnp.float32)
        for k in range(n_plane):
            at = pl.multiple_of((plane ^ k) * mu, mu)
            total += dot(weight_ref[:, pl.ds(at, mu)], bundles[k][p])
        for q, value in enumerate(halves):
            folded = jnp.sum((total * value).reshape(mu // 8, 8, nu), axis=0)
            own = jnp.sum(jnp.sum(folded, axis=0, keepdims=True), axis=1, keepdims=True)
            begun = jnp.where(lanes == q * (cut + rest) + cut + p, own, begun)
        mixed_ref[:, p * nu : (p + 1) * nu] = total.astype(mixed_ref.dtype)
        both_ref[:, p * nu : (p + 1) * nu] = total.astype(both_ref.dtype)
        for i, k in enumerate(late(n_row)):
            at = pl.multiple_of((row ^ k) * nu, nu)
            turned = lax.dot_general(
                bundles[0][p], panel_ref[pl.ds(at, nu), :], (((1,), (1,)), ((), ())), preferred_element_type=jnp.float32
            )
            place_at = ((i + 1) * rest + p) * nu
            both_ref[:, place_at : place_at + nu] = turned.astype(both_ref.dtype)
    begun_ref[...] = begun


def mix(lines, bundles):
    planes, mu, nu = lines[0].shape
    cut, rest = planes - 1, bundles[0].shape[0] - 1
    n_row, n_plane = len(lines), len(bundles)
    kind = lines[0].dtype
    return pl.pallas_call(
        functools.partial(mix_kernel, n_row, n_plane),
        out_shape=(
            jax.ShapeDtypeStruct((mu, cut * nu), kind),
            jax.ShapeDtypeStruct((mu, rest * nu), kind),
            jax.ShapeDtypeStruct((mu, (1 + len(late(n_row))) * rest * nu), kind),
            jax.ShapeDtypeStruct((mu, n_row * nu), kind),
            jax.ShapeDtypeStruct((n_plane * mu, nu), kind),
            jax.ShapeDtypeStruct((1, 128), jnp.float32),
        ),
        in_specs=[VMEM] * (n_row + n_plane),
        out_specs=[VMEM] * 6,
        compiler_params=pltpu.CompilerParams(vmem_limit_bytes=ROOM),
        cost_estimate=pl.CostEstimate(
            flops=2 * (cut + rest) * mu * nu * nu * n_row,
            bytes_accessed=4 * n_row * (cut + rest) * mu * nu,
            transcendentals=0,
        ),
        name="mix",
    )(*lines, *bundles)


def share_kernel(n_row, n_plane, begun_ref, weight_ref, panel_ref, line_ref, bundle_ref, near_ref, *refs):
    halves, far = refs[:n_plane], refs[n_plane : n_plane + n_row // 2]
    first_ref, part_ref, share_ref = refs[n_plane + n_row // 2 :]
    cut, mu, nu = first_ref.shape
    rest = part_ref.shape[0]
    aux = cut + rest
    row, plane = lax.axis_index("row"), plane_index()
    known = {2 * i: ref for i, ref in enumerate(far)}
    known[1] = near_ref

    def product(left, right):
        folded = jnp.sum((left.astype(jnp.float32) * right).reshape(mu // 8, 8, nu), axis=0)
        return sum([folded[:, i : i + 128] for i in range(128, nu, 128)], folded[:, :128])

    lanes = lax.broadcasted_iota(jnp.int32, share_ref.shape[1:], 1)
    shares = [begun_ref[...]]

    def store(p, q, value):
        total = jnp.sum(jnp.sum(value, axis=0, keepdims=True), axis=1, keepdims=True)
        shares[0] = jnp.where(lanes == p * aux + q, total, shares[0])

    for q in range(cut):
        total = jnp.zeros((mu, nu), jnp.float32)
        for k in range(n_plane):
            at = pl.multiple_of((plane ^ k) * mu, mu)
            total += dot(weight_ref[:, pl.ds(at, mu)], halves[k][:, q * nu : (q + 1) * nu])
        rounded = total.astype(first_ref.dtype)
        first_ref[q] = rounded
        for p in range(aux):
            value = product(line_ref[p] if p < cut else bundle_ref[p - cut], rounded.astype(jnp.float32))
            store(p, q, value)
    for q in range(rest):
        total = jnp.zeros((mu, nu), jnp.float32)
        for k, ref in known.items():
            at = pl.multiple_of((row ^ k) * nu, nu)
            total += dot(ref[:, q * nu : (q + 1) * nu], panel_ref[pl.ds(at, nu), :])
        part_ref[q] = total
        for p in range(rest):
            value = product(bundle_ref[p], total)
            for i, k in enumerate(late(n_row)):
                at = ((i + 1) * rest + p) * nu
                other = known[k ^ 1][:, q * nu : (q + 1) * nu]
                value += product(near_ref[:, at : at + nu], other.astype(jnp.float32))
            store(cut + p, cut + q, value)
    for i in range(share_ref.shape[0]):
        share_ref[i] = shares[0]


def share_of(begun, weight, panel, line, bundle, near, halves, far):
    planes, mu, nu = line.shape
    cut, rest = planes - 1, bundle.shape[0] - 1
    n_row, n_plane = 2 * len(far), len(halves)
    return pl.pallas_call(
        functools.partial(share_kernel, n_row, n_plane),
        out_shape=(
            jax.ShapeDtypeStruct((cut, mu, nu), line.dtype),
            jax.ShapeDtypeStruct((rest, mu, nu), jnp.float32),
            jax.ShapeDtypeStruct((n_row * n_plane, 1, 128), jnp.float32),
        ),
        in_specs=[VMEM] * (6 + n_plane + len(far)),
        out_specs=[VMEM] * 3,
        compiler_params=pltpu.CompilerParams(vmem_limit_bytes=ROOM),
        cost_estimate=pl.CostEstimate(
            flops=2 * (cut + rest) * mu * mu * nu * n_plane,
            bytes_accessed=4 * n_plane * (cut + rest) * mu * nu,
            transcendentals=0,
        ),
        name="polar_share",
    )(begun, weight, panel, line, bundle, near, *halves, *far)


def dress_kernel(n_row, panel_ref, first_ref, part_ref, shares_ref, *refs):
    blocks, (out_ref, polar_ref) = refs[:-2], refs[-2:]
    cut, _, nu = first_ref.shape
    row = lax.axis_index("row")
    for q in range(cut):
        out_ref[:, q, :] = first_ref[q]
    for q in range(part_ref.shape[0]):
        total = part_ref[q]
        for k, ref in zip(late(n_row), blocks):
            at = pl.multiple_of((row ^ k) * nu, nu)
            total += dot(ref[:, q * nu : (q + 1) * nu], panel_ref[pl.ds(at, nu), :])
        out_ref[:, cut + q, :] = total.astype(out_ref.dtype)
    aux = polar_ref.shape[0]
    polar = jnp.sum(shares_ref[...], axis=0) / panel_ref.shape[0]
    for p in range(aux):
        polar_ref[p : p + 1, :] = polar[:, p * aux : (p + 1) * aux]


def dress(panel, first, part, shares, blocks, n_row):
    cut, mu, nu = first.shape
    aux = cut + part.shape[0]
    return pl.pallas_call(
        functools.partial(dress_kernel, n_row),
        out_shape=(
            jax.ShapeDtypeStruct((mu, aux, nu), first.dtype),
            jax.ShapeDtypeStruct((aux, aux), jnp.float32),
        ),
        in_specs=[VMEM] * (4 + len(blocks)),
        out_specs=(VMEM, VMEM),
        compiler_params=pltpu.CompilerParams(vmem_limit_bytes=ROOM),
        cost_estimate=pl.CostEstimate(flops=2 * mu * nu * nu * aux, bytes_accessed=8 * mu * aux * nu, transcendentals=0),
        name="dress",
    )(panel, first, part, shares, *blocks)


def on_device(tensor_tiles, tile_pairs, tile_counts, occupied, virtual):
    aux = tensor_tiles.shape[1]
    n_row, n_plane = lax.axis_size("row"), lax.axis_size("col") * lax.axis_size("rep")
    near = list(range(2, n_plane, 2))
    sibling = lambda value: flip(value, PLANE, 1, n_plane)

    def gather_plane(value):
        values = [value] + [flip(value, PLANE, k, n_plane) for k in near]
        return [held for value in values for held in (value, sibling(value))]

    line, bundle = place(tile_pairs, tile_counts, tensor_tiles, occupied, virtual)
    half, mixed, both, weight, panel, begun = mix(gather_row(line, n_row), gather_plane(bundle))
    far = {0: mixed}
    step = n_row // 2
    while step > 1:
        far.update({k ^ step: flip(held, "row", step, n_row) for k, held in list(far.items())})
        step //= 2
    beside = flip(both, "row", 1, n_row)
    sources, beside = after([far[k ^ 1] for k in late(n_row)], beside)
    blocks = [flip(held, "row", 1, n_row) for held in sources]
    first, part, share = share_of(
        begun, weight, panel, line, bundle, beside, gather_plane(half), [far[k] for k in range(0, n_row, 2)]
    )
    dressed, polar = dress(panel, first, part, lax.all_to_all(share, EVERY, 0, 0), blocks, n_row)
    return polar, dressed


def solution(mesh):
    return jax.shard_map(
        on_device,
        mesh=mesh,
        in_specs=(P(EVERY, None, None, None), P(EVERY), P(EVERY), P(PLANE, "row"), P(PLANE, "row")),
        out_specs=(P(), P(PLANE, None, "row")),
        check_vma=False,
    )
```

```python
import functools

import jax
import jax.numpy as jnp
from jax import lax
from jax.experimental import pallas as pl
from jax.experimental.pallas import tpu as pltpu
from jax.sharding import PartitionSpec as P

PLANE = ("col", "rep")
EVERY = ("row", "col", "rep")
VMEM = pl.BlockSpec(memory_space=pltpu.VMEM)
SMEM = pl.BlockSpec(memory_space=pltpu.SMEM)
ROOM = 48 << 20


def flip(value, axes, mask, count):
    return lax.ppermute(value, axes, [(i, i ^ mask) for i in range(count)])


def after(value, earlier):
    return lax.optimization_barrier((value, earlier))


def gather_row(value, n_row):
    found = {0: value}
    step = n_row // 2
    while step:
        found.update({k ^ step: flip(held, "row", step, n_row) for k, held in list(found.items())})
        step //= 2
    return [found[k] for k in range(n_row)]


def late(n_row):
    return list(range(3, n_row, 2))


def plane_index():
    return lax.axis_index("col") * lax.axis_size("rep") + lax.axis_index("rep")


def place_kernel(nu_tiles, counts_ref, pairs_any, tiles_any, weight_any, column_any, *refs):
    line_ref, bundle_ref, pairs_ref, tiles_ref, sems = refs
    slots, aux, tile, _ = tiles_ref.shape
    cut = line_ref.shape[0] - 1
    copies = [
        pltpu.make_async_copy(source, target, sems.at[i])
        for i, (source, target) in enumerate(
            [
                (tiles_any, tiles_ref),
                (pairs_any, pairs_ref),
                (weight_any, line_ref.at[cut]),
                (column_any, bundle_ref.at[aux - cut]),
            ]
        )
    ]
    for copy in copies:
        copy.start()
    for copy in copies:
        copy.wait()
    for t in range(slots):
        pair = pairs_ref[t]
        rows = pl.ds(pl.multiple_of(pair // nu_tiles * tile, tile), tile)
        cols = pl.ds(pl.multiple_of(pair % nu_tiles * tile, tile), tile)

        @pl.when(t < counts_ref[0])
        def _():
            line_ref[:cut, rows, cols] = tiles_ref[t, :cut]
            bundle_ref[: aux - cut, rows, cols] = tiles_ref[t, cut:]

        @pl.when(t >= counts_ref[0])
        def _():
            line_ref[:cut, rows, cols] = jnp.zeros((cut, tile, tile), line_ref.dtype)
            bundle_ref[: aux - cut, rows, cols] = jnp.zeros((aux - cut, tile, tile), line_ref.dtype)


def place(tile_pairs, tile_counts, tensor_tiles, weight, column):
    slots, aux, tile, _ = tensor_tiles.shape
    mu, nu = weight.shape
    cut = aux // 2
    stays = [
        pltpu.with_memory_space_constraint(value, pltpu.HBM) for value in (tile_pairs, tensor_tiles, weight, column)
    ]
    return pl.pallas_call(
        functools.partial(place_kernel, nu // tile),
        out_shape=[jax.ShapeDtypeStruct((count + 1, mu, nu), weight.dtype) for count in (cut, aux - cut)],
        in_specs=[SMEM] + [pl.BlockSpec(memory_space=pltpu.HBM)] * 4,
        out_specs=[VMEM, VMEM],
        scratch_shapes=[
            pltpu.SMEM(tile_pairs.shape, tile_pairs.dtype),
            pltpu.VMEM(tensor_tiles.shape, tensor_tiles.dtype),
            pltpu.SemaphoreType.DMA((4,)),
        ],
        compiler_params=pltpu.CompilerParams(vmem_limit_bytes=ROOM),
        cost_estimate=pl.CostEstimate(flops=0, bytes_accessed=6 * tensor_tiles.size, transcendentals=0),
        name="place",
    )(tile_counts, *stays)


def dot(left, right):
    return jnp.dot(left, right, preferred_element_type=jnp.float32)


def mix_kernel(n_row, n_plane, *refs):
    lines, bundles = refs[:n_row], refs[n_row : n_row + n_plane]
    half_ref, mixed_ref, both_ref, weight_ref, panel_ref, begun_ref = refs[n_row + n_plane :]
    planes, mu, nu = lines[0].shape
    cut, rest = planes - 1, bundles[0].shape[0] - 1
    row, plane = lax.axis_index("row"), plane_index()
    for k in range(n_plane):
        panel_ref[pl.ds(pl.multiple_of((plane ^ k) * mu, mu), mu), :] = bundles[k][rest]
    for k in range(n_row):
        weight_ref[:, pl.ds(pl.multiple_of((row ^ k) * nu, nu), nu)] = lines[k][cut]
    halves = []
    for p in range(cut):
        total = jnp.zeros((mu, nu), jnp.float32)
        for k in range(n_row):
            at = pl.multiple_of((row ^ k) * nu, nu)
            total += dot(lines[k][p], panel_ref[pl.ds(at, nu), :])
        half_ref[:, p * nu : (p + 1) * nu] = total.astype(half_ref.dtype)
        halves.append(total)
    lanes = lax.broadcasted_iota(jnp.int32, begun_ref.shape, 1)
    begun = jnp.zeros(begun_ref.shape, jnp.float32)
    for p in range(rest):
        total = jnp.zeros((mu, nu), jnp.float32)
        for k in range(n_plane):
            at = pl.multiple_of((plane ^ k) * mu, mu)
            total += dot(weight_ref[:, pl.ds(at, mu)], bundles[k][p])
        for q, value in enumerate(halves):
            folded = jnp.sum((total * value).reshape(mu // 8, 8, nu), axis=0)
            own = jnp.sum(jnp.sum(folded, axis=0, keepdims=True), axis=1, keepdims=True)
            begun = jnp.where(lanes == q * (cut + rest) + cut + p, own, begun)
        mixed_ref[:, p * nu : (p + 1) * nu] = total.astype(mixed_ref.dtype)
        both_ref[:, p * nu : (p + 1) * nu] = total.astype(both_ref.dtype)
        for i, k in enumerate(late(n_row)):
            at = pl.multiple_of((row ^ k) * nu, nu)
            turned = lax.dot_general(
                bundles[0][p], panel_ref[pl.ds(at, nu), :], (((1,), (1,)), ((), ())), preferred_element_type=jnp.float32
            )
            place_at = ((i + 1) * rest + p) * nu
            both_ref[:, place_at : place_at + nu] = turned.astype(both_ref.dtype)
    begun_ref[...] = begun


def mix(lines, bundles):
    planes, mu, nu = lines[0].shape
    cut, rest = planes - 1, bundles[0].shape[0] - 1
    n_row, n_plane = len(lines), len(bundles)
    kind = lines[0].dtype
    return pl.pallas_call(
        functools.partial(mix_kernel, n_row, n_plane),
        out_shape=(
            jax.ShapeDtypeStruct((mu, cut * nu), kind),
            jax.ShapeDtypeStruct((mu, rest * nu), kind),
            jax.ShapeDtypeStruct((mu, (1 + len(late(n_row))) * rest * nu), kind),
            jax.ShapeDtypeStruct((mu, n_row * nu), kind),
            jax.ShapeDtypeStruct((n_plane * mu, nu), kind),
            jax.ShapeDtypeStruct((1, 128), jnp.float32),
        ),
        in_specs=[VMEM] * (n_row + n_plane),
        out_specs=[VMEM] * 6,
        compiler_params=pltpu.CompilerParams(vmem_limit_bytes=ROOM),
        cost_estimate=pl.CostEstimate(
            flops=2 * (cut + rest) * mu * nu * nu * n_row,
            bytes_accessed=4 * n_row * (cut + rest) * mu * nu,
            transcendentals=0,
        ),
        name="mix",
    )(*lines, *bundles)


def share_kernel(n_row, n_plane, begun_ref, weight_ref, panel_ref, line_ref, bundle_ref, near_ref, *refs):
    halves, far = refs[:n_plane], refs[n_plane : n_plane + n_row // 2]
    first_ref, part_ref, share_ref = refs[n_plane + n_row // 2 :]
    cut, mu, nu = first_ref.shape
    rest = part_ref.shape[0]
    aux = cut + rest
    row, plane = lax.axis_index("row"), plane_index()
    known = {2 * i: ref for i, ref in enumerate(far)}
    known[1] = near_ref

    def product(left, right):
        folded = jnp.sum((left.astype(jnp.float32) * right).reshape(mu // 8, 8, nu), axis=0)
        return sum([folded[:, i : i + 128] for i in range(128, nu, 128)], folded[:, :128])

    lanes = lax.broadcasted_iota(jnp.int32, share_ref.shape[1:], 1)
    shares = [begun_ref[...]]

    def store(p, q, value):
        total = jnp.sum(jnp.sum(value, axis=0, keepdims=True), axis=1, keepdims=True)
        shares[0] = jnp.where(lanes == p * aux + q, total, shares[0])

    for q in range(cut):
        total = jnp.zeros((mu, nu), jnp.float32)
        for k in range(n_plane):
            at = pl.multiple_of((plane ^ k) * mu, mu)
            total += dot(weight_ref[:, pl.ds(at, mu)], halves[k][:, q * nu : (q + 1) * nu])
        rounded = total.astype(first_ref.dtype)
        first_ref[q] = rounded
        for p in range(aux):
            value = product(line_ref[p] if p < cut else bundle_ref[p - cut], rounded.astype(jnp.float32))
            store(p, q, value)
    for q in range(rest):
        total = jnp.zeros((mu, nu), jnp.float32)
        for k, ref in known.items():
            at = pl.multiple_of((row ^ k) * nu, nu)
            total += dot(ref[:, q * nu : (q + 1) * nu], panel_ref[pl.ds(at, nu), :])
        part_ref[q] = total
        for p in range(rest):
            value = product(bundle_ref[p], total)
            for i, k in enumerate(late(n_row)):
                at = ((i + 1) * rest + p) * nu
                other = known[k ^ 1][:, q * nu : (q + 1) * nu]
                value += product(near_ref[:, at : at + nu], other.astype(jnp.float32))
            store(cut + p, cut + q, value)
    for i in range(share_ref.shape[0]):
        share_ref[i] = shares[0]


def share_of(begun, weight, panel, line, bundle, near, halves, far):
    planes, mu, nu = line.shape
    cut, rest = planes - 1, bundle.shape[0] - 1
    n_row, n_plane = 2 * len(far), len(halves)
    return pl.pallas_call(
        functools.partial(share_kernel, n_row, n_plane),
        out_shape=(
            jax.ShapeDtypeStruct((cut, mu, nu), line.dtype),
            jax.ShapeDtypeStruct((rest, mu, nu), jnp.float32),
            jax.ShapeDtypeStruct((n_row * n_plane, 1, 128), jnp.float32),
        ),
        in_specs=[VMEM] * (6 + n_plane + len(far)),
        out_specs=[VMEM] * 3,
        compiler_params=pltpu.CompilerParams(vmem_limit_bytes=ROOM),
        cost_estimate=pl.CostEstimate(
            flops=2 * (cut + rest) * mu * mu * nu * n_plane,
            bytes_accessed=4 * n_plane * (cut + rest) * mu * nu,
            transcendentals=0,
        ),
        name="polar_share",
    )(begun, weight, panel, line, bundle, near, *halves, *far)


def dress_kernel(n_row, panel_ref, first_ref, part_ref, shares_ref, *refs):
    blocks, (out_ref, polar_ref) = refs[:-2], refs[-2:]
    cut, _, nu = first_ref.shape
    row = lax.axis_index("row")
    values = [first_ref[q] for q in range(cut)]
    for q in range(part_ref.shape[0]):
        total = part_ref[q]
        for k, ref in zip(late(n_row), blocks):
            at = pl.multiple_of((row ^ k) * nu, nu)
            total += dot(ref[:, q * nu : (q + 1) * nu], panel_ref[pl.ds(at, nu), :])
        values.append(total.astype(out_ref.dtype))
    for q in range(0, len(values), 2):
        out_ref[:, q : q + 2, :] = jnp.stack(values[q : q + 2], axis=1)
    aux = polar_ref.shape[0]
    polar = jnp.sum(shares_ref[...], axis=0) / panel_ref.shape[0]
    for p in range(aux):
        polar_ref[p : p + 1, :] = polar[:, p * aux : (p + 1) * aux]


def dress(panel, first, part, shares, blocks, n_row):
    cut, mu, nu = first.shape
    aux = cut + part.shape[0]
    return pl.pallas_call(
        functools.partial(dress_kernel, n_row),
        out_shape=(
            jax.ShapeDtypeStruct((mu, aux, nu), first.dtype),
            jax.ShapeDtypeStruct((aux, aux), jnp.float32),
        ),
        in_specs=[VMEM] * (4 + len(blocks)),
        out_specs=(VMEM, VMEM),
        compiler_params=pltpu.CompilerParams(vmem_limit_bytes=ROOM),
        cost_estimate=pl.CostEstimate(flops=2 * mu * nu * nu * aux, bytes_accessed=8 * mu * aux * nu, transcendentals=0),
        name="dress",
    )(panel, first, part, shares, *blocks)


def on_device(tensor_tiles, tile_pairs, tile_counts, occupied, virtual):
    aux = tensor_tiles.shape[1]
    n_row, n_plane = lax.axis_size("row"), lax.axis_size("col") * lax.axis_size("rep")
    near = list(range(2, n_plane, 2))
    sibling = lambda value: flip(value, PLANE, 1, n_plane)

    def gather_plane(value):
        values = [value] + [flip(value, PLANE, k, n_plane) for k in near]
        return [held for value in values for held in (value, sibling(value))]

    line, bundle = place(tile_pairs, tile_counts, tensor_tiles, occupied, virtual)
    half, mixed, both, weight, panel, begun = mix(gather_row(line, n_row), gather_plane(bundle))
    far = {0: mixed}
    step = n_row // 2
    while step > 1:
        far.update({k ^ step: flip(held, "row", step, n_row) for k, held in list(far.items())})
        step //= 2
    beside = flip(both, "row", 1, n_row)
    sources, beside = after([far[k ^ 1] for k in late(n_row)], beside)
    blocks = [flip(held, "row", 1, n_row) for held in sources]
    first, part, share = share_of(
        begun, weight, panel, line, bundle, beside, gather_plane(half), [far[k] for k in range(0, n_row, 2)]
    )
    dressed, polar = dress(panel, first, part, lax.all_to_all(share, EVERY, 0, 0), blocks, n_row)
    return polar, dressed


def solution(mesh):
    return jax.shard_map(
        on_device,
        mesh=mesh,
        in_specs=(P(EVERY, None, None, None), P(EVERY), P(EVERY), P(PLANE, "row"), P(PLANE, "row")),
        out_specs=(P(), P(PLANE, None, "row")),
        check_vma=False,
    )
```

```python
import functools

import jax
import jax.numpy as jnp
from jax import lax
from jax.experimental import pallas as pl
from jax.experimental.pallas import tpu as pltpu
from jax.sharding import PartitionSpec as P

PLANE = ("col", "rep")
EVERY = ("row", "col", "rep")
VMEM = pl.BlockSpec(memory_space=pltpu.VMEM)
SMEM = pl.BlockSpec(memory_space=pltpu.SMEM)
ROOM = 48 << 20


def flip(value, axes, mask, count):
    return lax.ppermute(value, axes, [(i, i ^ mask) for i in range(count)])


def after(value, earlier):
    return lax.optimization_barrier((value, earlier))


def gather_row(value, n_row):
    found = {0: value}
    step = n_row // 2
    while step:
        found.update({k ^ step: flip(held, "row", step, n_row) for k, held in list(found.items())})
        step //= 2
    return [found[k] for k in range(n_row)]


def late(n_row):
    return list(range(3, n_row, 2))


def chip_order(n_plane):
    return [2 * (i ^ (i >> 1)) for i in range(1, n_plane // 2)]


def by_distance(refs):
    places = [k for chip in [0] + chip_order(len(refs)) for k in (chip, chip ^ 1)]
    return [refs[places.index(k)] for k in range(len(refs))]


def plane_index():
    return lax.axis_index("col") * lax.axis_size("rep") + lax.axis_index("rep")


def place_kernel(nu_tiles, counts_ref, pairs_any, tiles_any, weight_any, column_any, *refs):
    line_ref, bundle_ref, pairs_ref, tiles_ref, sems = refs
    slots, aux, tile, _ = tiles_ref.shape
    cut = line_ref.shape[0] - 1
    copies = [
        pltpu.make_async_copy(source, target, sems.at[i])
        for i, (source, target) in enumerate(
            [
                (tiles_any, tiles_ref),
                (pairs_any, pairs_ref),
                (weight_any, line_ref.at[cut]),
                (column_any, bundle_ref.at[aux - cut]),
            ]
        )
    ]
    for copy in copies:
        copy.start()
    for copy in copies:
        copy.wait()
    for t in range(slots):
        pair = pairs_ref[t]
        rows = pl.ds(pl.multiple_of(pair // nu_tiles * tile, tile), tile)
        cols = pl.ds(pl.multiple_of(pair % nu_tiles * tile, tile), tile)

        @pl.when(t < counts_ref[0])
        def _():
            line_ref[:cut, rows, cols] = tiles_ref[t, :cut]
            bundle_ref[: aux - cut, rows, cols] = tiles_ref[t, cut:]

        @pl.when(t >= counts_ref[0])
        def _():
            line_ref[:cut, rows, cols] = jnp.zeros((cut, tile, tile), line_ref.dtype)
            bundle_ref[: aux - cut, rows, cols] = jnp.zeros((aux - cut, tile, tile), line_ref.dtype)


def place(tile_pairs, tile_counts, tensor_tiles, weight, column):
    slots, aux, tile, _ = tensor_tiles.shape
    mu, nu = weight.shape
    cut = aux // 2
    stays = [
        pltpu.with_memory_space_constraint(value, pltpu.HBM) for value in (tile_pairs, tensor_tiles, weight, column)
    ]
    return pl.pallas_call(
        functools.partial(place_kernel, nu // tile),
        out_shape=[jax.ShapeDtypeStruct((count + 1, mu, nu), weight.dtype) for count in (cut, aux - cut)],
        in_specs=[SMEM] + [pl.BlockSpec(memory_space=pltpu.HBM)] * 4,
        out_specs=[VMEM, VMEM],
        scratch_shapes=[
            pltpu.SMEM(tile_pairs.shape, tile_pairs.dtype),
            pltpu.VMEM(tensor_tiles.shape, tensor_tiles.dtype),
            pltpu.SemaphoreType.DMA((4,)),
        ],
        compiler_params=pltpu.CompilerParams(vmem_limit_bytes=ROOM),
        cost_estimate=pl.CostEstimate(flops=0, bytes_accessed=6 * tensor_tiles.size, transcendentals=0),
        name="place",
    )(tile_counts, *stays)


def dot(left, right):
    return jnp.dot(left, right, preferred_element_type=jnp.float32)


def mix_kernel(n_row, n_plane, *refs):
    lines, bundles = refs[:n_row], by_distance(refs[n_row : n_row + n_plane])
    half_ref, mixed_ref, both_ref, weight_ref, panel_ref, begun_ref = refs[n_row + n_plane :]
    planes, mu, nu = lines[0].shape
    cut, rest = planes - 1, bundles[0].shape[0] - 1
    row, plane = lax.axis_index("row"), plane_index()
    for k in range(n_plane):
        panel_ref[pl.ds(pl.multiple_of((plane ^ k) * mu, mu), mu), :] = bundles[k][rest]
    for k in range(n_row):
        weight_ref[:, pl.ds(pl.multiple_of((row ^ k) * nu, nu), nu)] = lines[k][cut]
    halves = []
    for p in range(cut):
        total = jnp.zeros((mu, nu), jnp.float32)
        for k in range(n_row):
            at = pl.multiple_of((row ^ k) * nu, nu)
            total += dot(lines[k][p], panel_ref[pl.ds(at, nu), :])
        half_ref[:, p * nu : (p + 1) * nu] = total.astype(half_ref.dtype)
        halves.append(total)
    lanes = lax.broadcasted_iota(jnp.int32, begun_ref.shape, 1)
    begun = jnp.zeros(begun_ref.shape, jnp.float32)
    for p in range(rest):
        total = jnp.zeros((mu, nu), jnp.float32)
        for k in range(n_plane):
            at = pl.multiple_of((plane ^ k) * mu, mu)
            total += dot(weight_ref[:, pl.ds(at, mu)], bundles[k][p])
        for q, value in enumerate(halves):
            folded = jnp.sum((total * value).reshape(mu // 8, 8, nu), axis=0)
            own = jnp.sum(jnp.sum(folded, axis=0, keepdims=True), axis=1, keepdims=True)
            begun = jnp.where(lanes == q * (cut + rest) + cut + p, own, begun)
        mixed_ref[:, p * nu : (p + 1) * nu] = total.astype(mixed_ref.dtype)
        both_ref[:, p * nu : (p + 1) * nu] = total.astype(both_ref.dtype)
        for i, k in enumerate(late(n_row)):
            at = pl.multiple_of((row ^ k) * nu, nu)
            turned = lax.dot_general(
                bundles[0][p], panel_ref[pl.ds(at, nu), :], (((1,), (1,)), ((), ())), preferred_element_type=jnp.float32
            )
            place_at = ((i + 1) * rest + p) * nu
            both_ref[:, place_at : place_at + nu] = turned.astype(both_ref.dtype)
    begun_ref[...] = begun


def mix(lines, bundles):
    planes, mu, nu = lines[0].shape
    cut, rest = planes - 1, bundles[0].shape[0] - 1
    n_row, n_plane = len(lines), len(bundles)
    kind = lines[0].dtype
    return pl.pallas_call(
        functools.partial(mix_kernel, n_row, n_plane),
        out_shape=(
            jax.ShapeDtypeStruct((mu, cut * nu), kind),
            jax.ShapeDtypeStruct((mu, rest * nu), kind),
            jax.ShapeDtypeStruct((mu, (1 + len(late(n_row))) * rest * nu), kind),
            jax.ShapeDtypeStruct((mu, n_row * nu), kind),
            jax.ShapeDtypeStruct((n_plane * mu, nu), kind),
            jax.ShapeDtypeStruct((1, 128), jnp.float32),
        ),
        in_specs=[VMEM] * (n_row + n_plane),
        out_specs=[VMEM] * 6,
        compiler_params=pltpu.CompilerParams(vmem_limit_bytes=ROOM),
        cost_estimate=pl.CostEstimate(
            flops=2 * (cut + rest) * mu * nu * nu * n_row,
            bytes_accessed=4 * n_row * (cut + rest) * mu * nu,
            transcendentals=0,
        ),
        name="mix",
    )(*lines, *bundles)


def share_kernel(n_row, n_plane, begun_ref, weight_ref, panel_ref, line_ref, bundle_ref, near_ref, *refs):
    halves, far = by_distance(refs[:n_plane]), refs[n_plane : n_plane + n_row // 2]
    first_ref, part_ref, share_ref = refs[n_plane + n_row // 2 :]
    cut, mu, nu = first_ref.shape
    rest = part_ref.shape[0]
    aux = cut + rest
    row, plane = lax.axis_index("row"), plane_index()
    known = {2 * i: ref for i, ref in enumerate(far)}
    known[1] = near_ref

    def product(left, right):
        folded = jnp.sum((left.astype(jnp.float32) * right).reshape(mu // 8, 8, nu), axis=0)
        return sum([folded[:, i : i + 128] for i in range(128, nu, 128)], folded[:, :128])

    lanes = lax.broadcasted_iota(jnp.int32, share_ref.shape[1:], 1)
    shares = [begun_ref[...]]

    def store(p, q, value):
        total = jnp.sum(jnp.sum(value, axis=0, keepdims=True), axis=1, keepdims=True)
        shares[0] = jnp.where(lanes == p * aux + q, total, shares[0])

    for q in range(cut):
        total = jnp.zeros((mu, nu), jnp.float32)
        for k in range(n_plane):
            at = pl.multiple_of((plane ^ k) * mu, mu)
            total += dot(weight_ref[:, pl.ds(at, mu)], halves[k][:, q * nu : (q + 1) * nu])
        rounded = total.astype(first_ref.dtype)
        first_ref[q] = rounded
        for p in range(aux):
            value = product(line_ref[p] if p < cut else bundle_ref[p - cut], rounded.astype(jnp.float32))
            store(p, q, value)
    for q in range(rest):
        total = jnp.zeros((mu, nu), jnp.float32)
        for k, ref in known.items():
            at = pl.multiple_of((row ^ k) * nu, nu)
            total += dot(ref[:, q * nu : (q + 1) * nu], panel_ref[pl.ds(at, nu), :])
        part_ref[q] = total
        for p in range(rest):
            value = product(bundle_ref[p], total)
            for i, k in enumerate(late(n_row)):
                at = ((i + 1) * rest + p) * nu
                other = known[k ^ 1][:, q * nu : (q + 1) * nu]
                value += product(near_ref[:, at : at + nu], other.astype(jnp.float32))
            store(cut + p, cut + q, value)
    for i in range(share_ref.shape[0]):
        share_ref[i] = shares[0]


def share_of(begun, weight, panel, line, bundle, near, halves, far):
    planes, mu, nu = line.shape
    cut, rest = planes - 1, bundle.shape[0] - 1
    n_row, n_plane = 2 * len(far), len(halves)
    return pl.pallas_call(
        functools.partial(share_kernel, n_row, n_plane),
        out_shape=(
            jax.ShapeDtypeStruct((cut, mu, nu), line.dtype),
            jax.ShapeDtypeStruct((rest, mu, nu), jnp.float32),
            jax.ShapeDtypeStruct((n_row * n_plane, 1, 128), jnp.float32),
        ),
        in_specs=[VMEM] * (6 + n_plane + len(far)),
        out_specs=[VMEM] * 3,
        compiler_params=pltpu.CompilerParams(vmem_limit_bytes=ROOM),
        cost_estimate=pl.CostEstimate(
            flops=2 * (cut + rest) * mu * mu * nu * n_plane,
            bytes_accessed=4 * n_plane * (cut + rest) * mu * nu,
            transcendentals=0,
        ),
        name="polar_share",
    )(begun, weight, panel, line, bundle, near, *halves, *far)


def dress_kernel(n_row, panel_ref, first_ref, part_ref, shares_ref, *refs):
    blocks, (out_ref, polar_ref) = refs[:-2], refs[-2:]
    cut, _, nu = first_ref.shape
    row = lax.axis_index("row")
    for q in range(cut):
        out_ref[:, q, :] = first_ref[q]
    for q in range(part_ref.shape[0]):
        total = part_ref[q]
        for k, ref in zip(late(n_row), blocks):
            at = pl.multiple_of((row ^ k) * nu, nu)
            total += dot(ref[:, q * nu : (q + 1) * nu], panel_ref[pl.ds(at, nu), :])
        out_ref[:, cut + q, :] = total.astype(out_ref.dtype)
    aux = polar_ref.shape[0]
    polar = jnp.sum(shares_ref[...], axis=0) / panel_ref.shape[0]
    for p in range(aux):
        polar_ref[p : p + 1, :] = polar[:, p * aux : (p + 1) * aux]


def dress(panel, first, part, shares, blocks, n_row):
    cut, mu, nu = first.shape
    aux = cut + part.shape[0]
    return pl.pallas_call(
        functools.partial(dress_kernel, n_row),
        out_shape=(
            jax.ShapeDtypeStruct((mu, aux, nu), first.dtype),
            jax.ShapeDtypeStruct((aux, aux), jnp.float32),
        ),
        in_specs=[VMEM] * (4 + len(blocks)),
        out_specs=(VMEM, VMEM),
        compiler_params=pltpu.CompilerParams(vmem_limit_bytes=ROOM),
        cost_estimate=pl.CostEstimate(flops=2 * mu * nu * nu * aux, bytes_accessed=8 * mu * aux * nu, transcendentals=0),
        name="dress",
    )(panel, first, part, shares, *blocks)


def on_device(tensor_tiles, tile_pairs, tile_counts, occupied, virtual):
    aux = tensor_tiles.shape[1]
    n_row, n_plane = lax.axis_size("row"), lax.axis_size("col") * lax.axis_size("rep")
    sibling = lambda value: flip(value, PLANE, 1, n_plane)

    def gather_plane(value):
        values = [value] + [flip(value, PLANE, k, n_plane) for k in chip_order(n_plane)]
        return [held for value in values for held in (value, sibling(value))]

    line, bundle = place(tile_pairs, tile_counts, tensor_tiles, occupied, virtual)
    half, mixed, both, weight, panel, begun = mix(gather_row(line, n_row), gather_plane(bundle))
    far = {0: mixed}
    step = n_row // 2
    while step > 1:
        far.update({k ^ step: flip(held, "row", step, n_row) for k, held in list(far.items())})
        step //= 2
    beside = flip(both, "row", 1, n_row)
    sources, beside = after([far[k ^ 1] for k in late(n_row)], beside)
    blocks = [flip(held, "row", 1, n_row) for held in sources]
    first, part, share = share_of(
        begun, weight, panel, line, bundle, beside, gather_plane(half), [far[k] for k in range(0, n_row, 2)]
    )
    dressed, polar = dress(panel, first, part, lax.all_to_all(share, EVERY, 0, 0), blocks, n_row)
    return polar, dressed


def solution(mesh):
    return jax.shard_map(
        on_device,
        mesh=mesh,
        in_specs=(P(EVERY, None, None, None), P(EVERY), P(EVERY), P(PLANE, "row"), P(PLANE, "row")),
        out_specs=(P(), P(PLANE, None, "row")),
        check_vma=False,
    )
```

```python
import functools

import jax
import jax.numpy as jnp
from jax import lax
from jax.experimental import pallas as pl
from jax.experimental.pallas import tpu as pltpu
from jax.sharding import PartitionSpec as P

PLANE = ("col", "rep")
EVERY = ("row", "col", "rep")
VMEM = pl.BlockSpec(memory_space=pltpu.VMEM)
SMEM = pl.BlockSpec(memory_space=pltpu.SMEM)
ROOM = 48 << 20


def flip(value, axes, mask, count):
    return lax.ppermute(value, axes, [(i, i ^ mask) for i in range(count)])


def after(value, earlier):
    return lax.optimization_barrier((value, earlier))


def gather_row(value, n_row):
    found = {0: value}
    step = n_row // 2
    while step:
        found.update({k ^ step: flip(held, "row", step, n_row) for k, held in list(found.items())})
        step //= 2
    return [found[k] for k in range(n_row)]


def late(n_row):
    return list(range(3, n_row, 2))


def chip_order(n_plane):
    return [2 * (i ^ (i >> 1)) for i in range(1, n_plane // 2)]


def by_distance(refs):
    places = [k for chip in [0] + chip_order(len(refs)) for k in (chip, chip ^ 1)]
    return [refs[places.index(k)] for k in range(len(refs))]


def plane_index():
    return lax.axis_index("col") * lax.axis_size("rep") + lax.axis_index("rep")


def place_kernel(nu_tiles, counts_ref, pairs_any, tiles_any, weight_any, column_any, *refs):
    line_ref, bundle_ref, pairs_ref, tiles_ref, sems = refs
    slots, aux, tile, _ = tiles_ref.shape
    cut = line_ref.shape[0] - 1
    copies = [
        pltpu.make_async_copy(source, target, sems.at[i])
        for i, (source, target) in enumerate(
            [
                (tiles_any, tiles_ref),
                (pairs_any, pairs_ref),
                (weight_any, line_ref.at[cut]),
                (column_any, bundle_ref.at[aux - cut]),
            ]
        )
    ]
    for copy in copies:
        copy.start()
    for copy in copies:
        copy.wait()
    for t in range(slots):
        pair = pairs_ref[t]
        rows = pl.ds(pl.multiple_of(pair // nu_tiles * tile, tile), tile)
        cols = pl.ds(pl.multiple_of(pair % nu_tiles * tile, tile), tile)

        @pl.when(t < counts_ref[0])
        def _():
            line_ref[:cut, rows, cols] = tiles_ref[t, :cut]
            bundle_ref[: aux - cut, rows, cols] = tiles_ref[t, cut:]

        @pl.when(t >= counts_ref[0])
        def _():
            line_ref[:cut, rows, cols] = jnp.zeros((cut, tile, tile), line_ref.dtype)
            bundle_ref[: aux - cut, rows, cols] = jnp.zeros((aux - cut, tile, tile), line_ref.dtype)


def place(tile_pairs, tile_counts, tensor_tiles, weight, column):
    slots, aux, tile, _ = tensor_tiles.shape
    mu, nu = weight.shape
    cut = aux // 2
    stays = [
        pltpu.with_memory_space_constraint(value, pltpu.HBM) for value in (tile_pairs, tensor_tiles, weight, column)
    ]
    return pl.pallas_call(
        functools.partial(place_kernel, nu // tile),
        out_shape=[jax.ShapeDtypeStruct((count + 1, mu, nu), weight.dtype) for count in (cut, aux - cut)],
        in_specs=[SMEM] + [pl.BlockSpec(memory_space=pltpu.HBM)] * 4,
        out_specs=[VMEM, VMEM],
        scratch_shapes=[
            pltpu.SMEM(tile_pairs.shape, tile_pairs.dtype),
            pltpu.VMEM(tensor_tiles.shape, tensor_tiles.dtype),
            pltpu.SemaphoreType.DMA((4,)),
        ],
        compiler_params=pltpu.CompilerParams(vmem_limit_bytes=ROOM),
        cost_estimate=pl.CostEstimate(flops=0, bytes_accessed=6 * tensor_tiles.size, transcendentals=0),
        name="place",
    )(tile_counts, *stays)


def dot(left, right):
    return jnp.dot(left, right, preferred_element_type=jnp.float32)


def pair(weight_ref, plane, k, mu):
    spots = [pl.ds(pl.multiple_of((plane ^ i) * mu, mu), mu) for i in (k, k + 1)]
    return jnp.concatenate([weight_ref[:, spot] for spot in spots], axis=1)


def mix_kernel(n_row, n_plane, *refs):
    lines, bundles = refs[:n_row], by_distance(refs[n_row : n_row + n_plane])
    half_ref, mixed_ref, both_ref, weight_ref, panel_ref, begun_ref = refs[n_row + n_plane :]
    planes, mu, nu = lines[0].shape
    cut, rest = planes - 1, bundles[0].shape[0] - 1
    row, plane = lax.axis_index("row"), plane_index()
    for k in range(n_plane):
        panel_ref[pl.ds(pl.multiple_of((plane ^ k) * mu, mu), mu), :] = bundles[k][rest]
    for k in range(n_row):
        weight_ref[:, pl.ds(pl.multiple_of((row ^ k) * nu, nu), nu)] = lines[k][cut]
    halves = []
    for p in range(cut):
        total = jnp.zeros((mu, nu), jnp.float32)
        for k in range(n_row):
            at = pl.multiple_of((row ^ k) * nu, nu)
            total += dot(lines[k][p], panel_ref[pl.ds(at, nu), :])
        half_ref[:, p * nu : (p + 1) * nu] = total.astype(half_ref.dtype)
        halves.append(total)
    lanes = lax.broadcasted_iota(jnp.int32, begun_ref.shape, 1)
    begun = jnp.zeros(begun_ref.shape, jnp.float32)
    for p in range(rest):
        total = jnp.zeros((mu, nu), jnp.float32)
        for k in range(0, n_plane, 2):
            total += dot(pair(weight_ref, plane, k, mu), jnp.concatenate([bundles[k][p], bundles[k + 1][p]], axis=0))
        for q, value in enumerate(halves):
            folded = jnp.sum((total * value).reshape(mu // 8, 8, nu), axis=0)
            own = jnp.sum(jnp.sum(folded, axis=0, keepdims=True), axis=1, keepdims=True)
            begun = jnp.where(lanes == q * (cut + rest) + cut + p, own, begun)
        mixed_ref[:, p * nu : (p + 1) * nu] = total.astype(mixed_ref.dtype)
        both_ref[:, p * nu : (p + 1) * nu] = total.astype(both_ref.dtype)
        for i, k in enumerate(late(n_row)):
            at = pl.multiple_of((row ^ k) * nu, nu)
            turned = lax.dot_general(
                bundles[0][p], panel_ref[pl.ds(at, nu), :], (((1,), (1,)), ((), ())), preferred_element_type=jnp.float32
            )
            place_at = ((i + 1) * rest + p) * nu
            both_ref[:, place_at : place_at + nu] = turned.astype(both_ref.dtype)
    begun_ref[...] = begun


def mix(lines, bundles):
    planes, mu, nu = lines[0].shape
    cut, rest = planes - 1, bundles[0].shape[0] - 1
    n_row, n_plane = len(lines), len(bundles)
    kind = lines[0].dtype
    return pl.pallas_call(
        functools.partial(mix_kernel, n_row, n_plane),
        out_shape=(
            jax.ShapeDtypeStruct((mu, cut * nu), kind),
            jax.ShapeDtypeStruct((mu, rest * nu), kind),
            jax.ShapeDtypeStruct((mu, (1 + len(late(n_row))) * rest * nu), kind),
            jax.ShapeDtypeStruct((mu, n_row * nu), kind),
            jax.ShapeDtypeStruct((n_plane * mu, nu), kind),
            jax.ShapeDtypeStruct((1, 128), jnp.float32),
        ),
        in_specs=[VMEM] * (n_row + n_plane),
        out_specs=[VMEM] * 6,
        compiler_params=pltpu.CompilerParams(vmem_limit_bytes=ROOM),
        cost_estimate=pl.CostEstimate(
            flops=2 * (cut + rest) * mu * nu * nu * n_row,
            bytes_accessed=4 * n_row * (cut + rest) * mu * nu,
            transcendentals=0,
        ),
        name="mix",
    )(*lines, *bundles)


def share_kernel(n_row, n_plane, begun_ref, weight_ref, panel_ref, line_ref, bundle_ref, near_ref, *refs):
    halves, far = by_distance(refs[:n_plane]), refs[n_plane : n_plane + n_row // 2]
    first_ref, part_ref, share_ref = refs[n_plane + n_row // 2 :]
    cut, mu, nu = first_ref.shape
    rest = part_ref.shape[0]
    aux = cut + rest
    row, plane = lax.axis_index("row"), plane_index()
    known = {2 * i: ref for i, ref in enumerate(far)}
    known[1] = near_ref

    def product(left, right):
        folded = jnp.sum((left.astype(jnp.float32) * right).reshape(mu // 8, 8, nu), axis=0)
        return sum([folded[:, i : i + 128] for i in range(128, nu, 128)], folded[:, :128])

    lanes = lax.broadcasted_iota(jnp.int32, share_ref.shape[1:], 1)
    shares = [begun_ref[...]]

    def store(p, q, value):
        total = jnp.sum(jnp.sum(value, axis=0, keepdims=True), axis=1, keepdims=True)
        shares[0] = jnp.where(lanes == p * aux + q, total, shares[0])

    for q in range(cut):
        total = jnp.zeros((mu, nu), jnp.float32)
        columns = slice(q * nu, (q + 1) * nu)
        for k in range(0, n_plane, 2):
            both = jnp.concatenate([halves[k][:, columns], halves[k + 1][:, columns]], axis=0)
            total += dot(pair(weight_ref, plane, k, mu), both)
        rounded = total.astype(first_ref.dtype)
        first_ref[q] = rounded
        for p in range(aux):
            value = product(line_ref[p] if p < cut else bundle_ref[p - cut], rounded.astype(jnp.float32))
            store(p, q, value)
    for q in range(rest):
        total = jnp.zeros((mu, nu), jnp.float32)
        for k, ref in known.items():
            at = pl.multiple_of((row ^ k) * nu, nu)
            total += dot(ref[:, q * nu : (q + 1) * nu], panel_ref[pl.ds(at, nu), :])
        part_ref[q] = total
        for p in range(rest):
            value = product(bundle_ref[p], total)
            for i, k in enumerate(late(n_row)):
                at = ((i + 1) * rest + p) * nu
                other = known[k ^ 1][:, q * nu : (q + 1) * nu]
                value += product(near_ref[:, at : at + nu], other.astype(jnp.float32))
            store(cut + p, cut + q, value)
    for i in range(share_ref.shape[0]):
        share_ref[i] = shares[0]


def share_of(begun, weight, panel, line, bundle, near, halves, far):
    planes, mu, nu = line.shape
    cut, rest = planes - 1, bundle.shape[0] - 1
    n_row, n_plane = 2 * len(far), len(halves)
    return pl.pallas_call(
        functools.partial(share_kernel, n_row, n_plane),
        out_shape=(
            jax.ShapeDtypeStruct((cut, mu, nu), line.dtype),
            jax.ShapeDtypeStruct((rest, mu, nu), jnp.float32),
            jax.ShapeDtypeStruct((n_row * n_plane, 1, 128), jnp.float32),
        ),
        in_specs=[VMEM] * (6 + n_plane + len(far)),
        out_specs=[VMEM] * 3,
        compiler_params=pltpu.CompilerParams(vmem_limit_bytes=ROOM),
        cost_estimate=pl.CostEstimate(
            flops=2 * (cut + rest) * mu * mu * nu * n_plane,
            bytes_accessed=4 * n_plane * (cut + rest) * mu * nu,
            transcendentals=0,
        ),
        name="polar_share",
    )(begun, weight, panel, line, bundle, near, *halves, *far)


def dress_kernel(n_row, panel_ref, first_ref, part_ref, shares_ref, *refs):
    blocks, (out_ref, polar_ref) = refs[:-2], refs[-2:]
    cut, _, nu = first_ref.shape
    row = lax.axis_index("row")
    for q in range(cut):
        out_ref[:, q, :] = first_ref[q]
    for q in range(part_ref.shape[0]):
        total = part_ref[q]
        for k, ref in zip(late(n_row), blocks):
            at = pl.multiple_of((row ^ k) * nu, nu)
            total += dot(ref[:, q * nu : (q + 1) * nu], panel_ref[pl.ds(at, nu), :])
        out_ref[:, cut + q, :] = total.astype(out_ref.dtype)
    aux = polar_ref.shape[0]
    polar = jnp.sum(shares_ref[...], axis=0) / panel_ref.shape[0]
    for p in range(aux):
        polar_ref[p : p + 1, :] = polar[:, p * aux : (p + 1) * aux]


def dress(panel, first, part, shares, blocks, n_row):
    cut, mu, nu = first.shape
    aux = cut + part.shape[0]
    return pl.pallas_call(
        functools.partial(dress_kernel, n_row),
        out_shape=(
            jax.ShapeDtypeStruct((mu, aux, nu), first.dtype),
            jax.ShapeDtypeStruct((aux, aux), jnp.float32),
        ),
        in_specs=[VMEM] * (4 + len(blocks)),
        out_specs=(VMEM, VMEM),
        compiler_params=pltpu.CompilerParams(vmem_limit_bytes=ROOM),
        cost_estimate=pl.CostEstimate(flops=2 * mu * nu * nu * aux, bytes_accessed=8 * mu * aux * nu, transcendentals=0),
        name="dress",
    )(panel, first, part, shares, *blocks)


def on_device(tensor_tiles, tile_pairs, tile_counts, occupied, virtual):
    aux = tensor_tiles.shape[1]
    n_row, n_plane = lax.axis_size("row"), lax.axis_size("col") * lax.axis_size("rep")
    sibling = lambda value: flip(value, PLANE, 1, n_plane)

    def gather_plane(value):
        values = [value] + [flip(value, PLANE, k, n_plane) for k in chip_order(n_plane)]
        return [held for value in values for held in (value, sibling(value))]

    line, bundle = place(tile_pairs, tile_counts, tensor_tiles, occupied, virtual)
    half, mixed, both, weight, panel, begun = mix(gather_row(line, n_row), gather_plane(bundle))
    far = {0: mixed}
    step = n_row // 2
    while step > 1:
        far.update({k ^ step: flip(held, "row", step, n_row) for k, held in list(far.items())})
        step //= 2
    beside = flip(both, "row", 1, n_row)
    sources, beside = after([far[k ^ 1] for k in late(n_row)], beside)
    blocks = [flip(held, "row", 1, n_row) for held in sources]
    first, part, share = share_of(
        begun, weight, panel, line, bundle, beside, gather_plane(half), [far[k] for k in range(0, n_row, 2)]
    )
    dressed, polar = dress(panel, first, part, lax.all_to_all(share, EVERY, 0, 0), blocks, n_row)
    return polar, dressed


def solution(mesh):
    return jax.shard_map(
        on_device,
        mesh=mesh,
        in_specs=(P(EVERY, None, None, None), P(EVERY), P(EVERY), P(PLANE, "row"), P(PLANE, "row")),
        out_specs=(P(), P(PLANE, None, "row")),
        check_vma=False,
    )
```

```python
import functools

import jax
import jax.numpy as jnp
from jax import lax
from jax.experimental import pallas as pl
from jax.experimental.pallas import tpu as pltpu
from jax.sharding import PartitionSpec as P

PLANE = ("col", "rep")
EVERY = ("row", "col", "rep")
VMEM = pl.BlockSpec(memory_space=pltpu.VMEM)
SMEM = pl.BlockSpec(memory_space=pltpu.SMEM)
ROOM = 48 << 20


def flip(value, axes, mask, count):
    return lax.ppermute(value, axes, [(i, i ^ mask) for i in range(count)])


def after(value, earlier):
    return lax.optimization_barrier((value, earlier))


def gather_row(value, n_row):
    found = {0: value}
    step = n_row // 2
    while step:
        found.update({k ^ step: flip(held, "row", step, n_row) for k, held in list(found.items())})
        step //= 2
    return [found[k] for k in range(n_row)]


def late(n_row):
    return list(range(3, n_row, 2))


def chip_order(n_plane):
    return [2 * (i ^ (i >> 1)) for i in range(1, n_plane // 2)]


def by_distance(refs):
    places = [k for chip in [0] + chip_order(len(refs)) for k in (chip, chip ^ 1)]
    return [refs[places.index(k)] for k in range(len(refs))]


def plane_index():
    return lax.axis_index("col") * lax.axis_size("rep") + lax.axis_index("rep")


def place_kernel(nu_tiles, counts_ref, pairs_any, tiles_any, weight_any, column_any, *refs):
    line_ref, bundle_ref, pairs_ref, tiles_ref, sems = refs
    slots, aux, tile, _ = tiles_ref.shape
    cut = line_ref.shape[0] - 1
    copies = [
        pltpu.make_async_copy(source, target, sems.at[i])
        for i, (source, target) in enumerate(
            [
                (tiles_any, tiles_ref),
                (pairs_any, pairs_ref),
                (weight_any, line_ref.at[cut]),
                (column_any, bundle_ref.at[aux - cut]),
            ]
        )
    ]
    for copy in copies:
        copy.start()
    for copy in copies:
        copy.wait()
    for t in range(slots):
        pair = pairs_ref[t]
        rows = pl.ds(pl.multiple_of(pair // nu_tiles * tile, tile), tile)
        cols = pl.ds(pl.multiple_of(pair % nu_tiles * tile, tile), tile)

        @pl.when(t < counts_ref[0])
        def _():
            line_ref[:cut, rows, cols] = tiles_ref[t, :cut]
            bundle_ref[: aux - cut, rows, cols] = tiles_ref[t, cut:]

        @pl.when(t >= counts_ref[0])
        def _():
            line_ref[:cut, rows, cols] = jnp.zeros((cut, tile, tile), line_ref.dtype)
            bundle_ref[: aux - cut, rows, cols] = jnp.zeros((aux - cut, tile, tile), line_ref.dtype)


def place(tile_pairs, tile_counts, tensor_tiles, weight, column):
    slots, aux, tile, _ = tensor_tiles.shape
    mu, nu = weight.shape
    cut = aux // 2
    stays = [
        pltpu.with_memory_space_constraint(value, pltpu.HBM) for value in (tile_pairs, tensor_tiles, weight, column)
    ]
    return pl.pallas_call(
        functools.partial(place_kernel, nu // tile),
        out_shape=[jax.ShapeDtypeStruct((count + 1, mu, nu), weight.dtype) for count in (cut, aux - cut)],
        in_specs=[SMEM] + [pl.BlockSpec(memory_space=pltpu.HBM)] * 4,
        out_specs=[VMEM, VMEM],
        scratch_shapes=[
            pltpu.SMEM(tile_pairs.shape, tile_pairs.dtype),
            pltpu.VMEM(tensor_tiles.shape, tensor_tiles.dtype),
            pltpu.SemaphoreType.DMA((4,)),
        ],
        compiler_params=pltpu.CompilerParams(vmem_limit_bytes=ROOM),
        cost_estimate=pl.CostEstimate(flops=0, bytes_accessed=6 * tensor_tiles.size, transcendentals=0),
        name="place",
    )(tile_counts, *stays)


def dot(left, right):
    return jnp.dot(left, right, preferred_element_type=jnp.float32)


def in_plane(weight_ref, plane, mu):
    spots = [pl.ds(pl.multiple_of((plane ^ k) * mu, mu), mu) for k in range(weight_ref.shape[1] // mu)]
    return jnp.concatenate([weight_ref[:, spot] for spot in spots], axis=1)


def mix_kernel(n_row, n_plane, *refs):
    lines, bundles = refs[:n_row], by_distance(refs[n_row : n_row + n_plane])
    half_ref, mixed_ref, both_ref, weight_ref, panel_ref, begun_ref = refs[n_row + n_plane :]
    planes, mu, nu = lines[0].shape
    cut, rest = planes - 1, bundles[0].shape[0] - 1
    row, plane = lax.axis_index("row"), plane_index()
    for k in range(n_plane):
        panel_ref[pl.ds(pl.multiple_of((plane ^ k) * mu, mu), mu), :] = bundles[k][rest]
    for k in range(n_row):
        weight_ref[:, pl.ds(pl.multiple_of((row ^ k) * nu, nu), nu)] = lines[k][cut]
    halves = []
    for p in range(cut):
        total = jnp.zeros((mu, nu), jnp.float32)
        for k in range(n_row):
            at = pl.multiple_of((row ^ k) * nu, nu)
            total += dot(lines[k][p], panel_ref[pl.ds(at, nu), :])
        half_ref[:, p * nu : (p + 1) * nu] = total.astype(half_ref.dtype)
        halves.append(total)
    lanes = lax.broadcasted_iota(jnp.int32, begun_ref.shape, 1)
    begun = jnp.zeros(begun_ref.shape, jnp.float32)
    for p in range(rest):
        total = jnp.zeros((mu, nu), jnp.float32)
        total += dot(in_plane(weight_ref, plane, mu), jnp.concatenate([ref[p] for ref in bundles], axis=0))
        for q, value in enumerate(halves):
            folded = jnp.sum((total * value).reshape(mu // 8, 8, nu), axis=0)
            own = jnp.sum(jnp.sum(folded, axis=0, keepdims=True), axis=1, keepdims=True)
            begun = jnp.where(lanes == q * (cut + rest) + cut + p, own, begun)
        mixed_ref[:, p * nu : (p + 1) * nu] = total.astype(mixed_ref.dtype)
        both_ref[:, p * nu : (p + 1) * nu] = total.astype(both_ref.dtype)
        for i, k in enumerate(late(n_row)):
            at = pl.multiple_of((row ^ k) * nu, nu)
            turned = lax.dot_general(
                bundles[0][p], panel_ref[pl.ds(at, nu), :], (((1,), (1,)), ((), ())), preferred_element_type=jnp.float32
            )
            place_at = ((i + 1) * rest + p) * nu
            both_ref[:, place_at : place_at + nu] = turned.astype(both_ref.dtype)
    begun_ref[...] = begun


def mix(lines, bundles):
    planes, mu, nu = lines[0].shape
    cut, rest = planes - 1, bundles[0].shape[0] - 1
    n_row, n_plane = len(lines), len(bundles)
    kind = lines[0].dtype
    return pl.pallas_call(
        functools.partial(mix_kernel, n_row, n_plane),
        out_shape=(
            jax.ShapeDtypeStruct((mu, cut * nu), kind),
            jax.ShapeDtypeStruct((mu, rest * nu), kind),
            jax.ShapeDtypeStruct((mu, (1 + len(late(n_row))) * rest * nu), kind),
            jax.ShapeDtypeStruct((mu, n_row * nu), kind),
            jax.ShapeDtypeStruct((n_plane * mu, nu), kind),
            jax.ShapeDtypeStruct((1, 128), jnp.float32),
        ),
        in_specs=[VMEM] * (n_row + n_plane),
        out_specs=[VMEM] * 6,
        compiler_params=pltpu.CompilerParams(vmem_limit_bytes=ROOM),
        cost_estimate=pl.CostEstimate(
            flops=2 * (cut + rest) * mu * nu * nu * n_row,
            bytes_accessed=4 * n_row * (cut + rest) * mu * nu,
            transcendentals=0,
        ),
        name="mix",
    )(*lines, *bundles)


def share_kernel(n_row, n_plane, begun_ref, weight_ref, panel_ref, line_ref, bundle_ref, near_ref, *refs):
    halves, far = by_distance(refs[:n_plane]), refs[n_plane : n_plane + n_row // 2]
    first_ref, part_ref, share_ref = refs[n_plane + n_row // 2 :]
    cut, mu, nu = first_ref.shape
    rest = part_ref.shape[0]
    aux = cut + rest
    row, plane = lax.axis_index("row"), plane_index()
    known = {2 * i: ref for i, ref in enumerate(far)}
    known[1] = near_ref

    def product(left, right):
        folded = jnp.sum((left.astype(jnp.float32) * right).reshape(mu // 8, 8, nu), axis=0)
        return sum([folded[:, i : i + 128] for i in range(128, nu, 128)], folded[:, :128])

    lanes = lax.broadcasted_iota(jnp.int32, share_ref.shape[1:], 1)
    shares = [begun_ref[...]]

    def store(p, q, value):
        total = jnp.sum(jnp.sum(value, axis=0, keepdims=True), axis=1, keepdims=True)
        shares[0] = jnp.where(lanes == p * aux + q, total, shares[0])

    for q in range(cut):
        total = jnp.zeros((mu, nu), jnp.float32)
        columns = slice(q * nu, (q + 1) * nu)
        total += dot(in_plane(weight_ref, plane, mu), jnp.concatenate([ref[:, columns] for ref in halves], axis=0))
        rounded = total.astype(first_ref.dtype)
        first_ref[q] = rounded
        for p in range(aux):
            value = product(line_ref[p] if p < cut else bundle_ref[p - cut], rounded.astype(jnp.float32))
            store(p, q, value)
    for q in range(rest):
        total = jnp.zeros((mu, nu), jnp.float32)
        for k, ref in known.items():
            at = pl.multiple_of((row ^ k) * nu, nu)
            total += dot(ref[:, q * nu : (q + 1) * nu], panel_ref[pl.ds(at, nu), :])
        part_ref[q] = total
        for p in range(rest):
            value = product(bundle_ref[p], total)
            for i, k in enumerate(late(n_row)):
                at = ((i + 1) * rest + p) * nu
                other = known[k ^ 1][:, q * nu : (q + 1) * nu]
                value += product(near_ref[:, at : at + nu], other.astype(jnp.float32))
            store(cut + p, cut + q, value)
    for i in range(share_ref.shape[0]):
        share_ref[i] = shares[0]


def share_of(begun, weight, panel, line, bundle, near, halves, far):
    planes, mu, nu = line.shape
    cut, rest = planes - 1, bundle.shape[0] - 1
    n_row, n_plane = 2 * len(far), len(halves)
    return pl.pallas_call(
        functools.partial(share_kernel, n_row, n_plane),
        out_shape=(
            jax.ShapeDtypeStruct((cut, mu, nu), line.dtype),
            jax.ShapeDtypeStruct((rest, mu, nu), jnp.float32),
            jax.ShapeDtypeStruct((n_row * n_plane, 1, 128), jnp.float32),
        ),
        in_specs=[VMEM] * (6 + n_plane + len(far)),
        out_specs=[VMEM] * 3,
        compiler_params=pltpu.CompilerParams(vmem_limit_bytes=ROOM),
        cost_estimate=pl.CostEstimate(
            flops=2 * (cut + rest) * mu * mu * nu * n_plane,
            bytes_accessed=4 * n_plane * (cut + rest) * mu * nu,
            transcendentals=0,
        ),
        name="polar_share",
    )(begun, weight, panel, line, bundle, near, *halves, *far)


def dress_kernel(n_row, panel_ref, first_ref, part_ref, shares_ref, *refs):
    blocks, (out_ref, polar_ref) = refs[:-2], refs[-2:]
    cut, _, nu = first_ref.shape
    row = lax.axis_index("row")
    for q in range(cut):
        out_ref[:, q, :] = first_ref[q]
    for q in range(part_ref.shape[0]):
        total = part_ref[q]
        for k, ref in zip(late(n_row), blocks):
            at = pl.multiple_of((row ^ k) * nu, nu)
            total += dot(ref[:, q * nu : (q + 1) * nu], panel_ref[pl.ds(at, nu), :])
        out_ref[:, cut + q, :] = total.astype(out_ref.dtype)
    aux = polar_ref.shape[0]
    polar = jnp.sum(shares_ref[...], axis=0) / panel_ref.shape[0]
    for p in range(aux):
        polar_ref[p : p + 1, :] = polar[:, p * aux : (p + 1) * aux]


def dress(panel, first, part, shares, blocks, n_row):
    cut, mu, nu = first.shape
    aux = cut + part.shape[0]
    return pl.pallas_call(
        functools.partial(dress_kernel, n_row),
        out_shape=(
            jax.ShapeDtypeStruct((mu, aux, nu), first.dtype),
            jax.ShapeDtypeStruct((aux, aux), jnp.float32),
        ),
        in_specs=[VMEM] * (4 + len(blocks)),
        out_specs=(VMEM, VMEM),
        compiler_params=pltpu.CompilerParams(vmem_limit_bytes=ROOM),
        cost_estimate=pl.CostEstimate(flops=2 * mu * nu * nu * aux, bytes_accessed=8 * mu * aux * nu, transcendentals=0),
        name="dress",
    )(panel, first, part, shares, *blocks)


def on_device(tensor_tiles, tile_pairs, tile_counts, occupied, virtual):
    aux = tensor_tiles.shape[1]
    n_row, n_plane = lax.axis_size("row"), lax.axis_size("col") * lax.axis_size("rep")
    sibling = lambda value: flip(value, PLANE, 1, n_plane)

    def gather_plane(value):
        values = [value] + [flip(value, PLANE, k, n_plane) for k in chip_order(n_plane)]
        return [held for value in values for held in (value, sibling(value))]

    line, bundle = place(tile_pairs, tile_counts, tensor_tiles, occupied, virtual)
    half, mixed, both, weight, panel, begun = mix(gather_row(line, n_row), gather_plane(bundle))
    far = {0: mixed}
    step = n_row // 2
    while step > 1:
        far.update({k ^ step: flip(held, "row", step, n_row) for k, held in list(far.items())})
        step //= 2
    beside = flip(both, "row", 1, n_row)
    sources, beside = after([far[k ^ 1] for k in late(n_row)], beside)
    blocks = [flip(held, "row", 1, n_row) for held in sources]
    first, part, share = share_of(
        begun, weight, panel, line, bundle, beside, gather_plane(half), [far[k] for k in range(0, n_row, 2)]
    )
    dressed, polar = dress(panel, first, part, lax.all_to_all(share, EVERY, 0, 0), blocks, n_row)
    return polar, dressed


def solution(mesh):
    return jax.shard_map(
        on_device,
        mesh=mesh,
        in_specs=(P(EVERY, None, None, None), P(EVERY), P(EVERY), P(PLANE, "row"), P(PLANE, "row")),
        out_specs=(P(), P(PLANE, None, "row")),
        check_vma=False,
    )
```
